128 devices in a mesh: shot: 16 (over x_hi, y, core), sub: 8 (over x_lo, z).
Axes of the slice: x: 4 (x_hi: 2, x_lo: 2; x = x_hi * 2 + x_lo), y: 4, z: 4, core: 2. Of those that a mesh axis runs over, the one named last changes fastest.
Arguments:
- courant_squared: float32 [2, 16, 8, 256, 128], P(None, 'shot', None, 'sub'), may hold values from 0.04 to 0.18
- wave_now: float32 [16, 64, 256, 128], P('shot', 'sub'), may hold values from -1.75 to 1.75
- wave_prev: float32 [16, 64, 256, 128], P('shot', 'sub'), may hold values from -1.75 to 1.75
- adj_late: float32 [16, 64, 256, 128], P('shot', 'sub'), may hold values from -1.75 to 1.75
- adj_later: float32 [16, 64, 256, 128], P('shot', 'sub'), may hold values from -1.75 to 1.75
- wavelet: float32 [16, 4], P('shot'), may hold values from -6 to 6
- sources: int32 [16], P('shot'), may hold values from 0 to 2097151
- receivers: int32 [16, 256], P('shot'), may hold values from 0 to 2097151
- observed: float32 [16, 4, 256], P('shot'), may hold values from -6 to 6
- apertures: int32 [16, 8], replicated, may hold values from 0 to 31, as said below
Outputs:
- gradient: float32 [2, 16, 8, 256, 128], P(None, 'shot', None, 'sub')
The draws below stay inside these ranges and needn't reach their ends.
Inputs may be any that keep to these rules, and one draw needn't show every extreme that they name: `apertures`: row s holds 8 consecutive block numbers in ascending order.
All inputs are finite; a program needn't handle non-finite values.
Results may differ from the reference program's by a relative error of at most 0.0003.
Values sent between devices are 32-bit elements; how exact they have to be, the bound alone decides.
No kernel may reach another device: no remote copies, remote signals or barrier semaphores. Data moves between devices by JAX's collectives and lax.ppermute only.
A program may use at most 64 MiB of HBM per device.

```python
import math
import jax
import jax.numpy as jnp
from jax import lax

BX = 8
NY = 256
NZ = 128
BPO = 2
STEPS = 4
NREC = 256
NBLK = 32
NXA = 64
N_SHOT = 16
N_SUB = 8


def draw_apertures(key, part):
    key = jax.random.fold_in(key, 11)
    key_start, key_order = jax.random.split(key)
    starts = jax.random.randint(key_start, (N_SHOT,), 0, NBLK - N_SUB + 1)
    order = jax.random.permutation(key_order, N_SHOT)
    starts = starts.at[order[0]].set(0).at[order[1]].set(NBLK - N_SUB)
    return (starts[:, None] + jnp.arange(N_SUB)[None, :]).astype(jnp.int32)


def touch_ends(result, rng, least, largest):
    longest = result.shape.index(max(result.shape))
    spots = []
    for shift in (0, 1):
        where = [jax.random.randint(jax.random.fold_in(rng, axis), (), 0, length) for axis, length in enumerate(result.shape)]
        where[longest] = (where[longest] + shift) % result.shape[longest]
        spots.append(tuple(where))
    return result.at[spots[0]].set(least).at[spots[1]].set(largest)


def levels(key, dims, pieces, smallest, top_value):
    loudness = 1.0
    for axis_at, parts in pieces:
        steps = jax.random.uniform(jax.random.fold_in(jax.random.fold_in(key, 6), axis_at), (parts,), jnp.float32, smallest / len(pieces), top_value / len(pieces))
        loudness = loudness * jnp.repeat(jnp.exp(steps), dims[axis_at] // parts).reshape((-1,) + (1,) * (len(dims) - 1 - axis_at))
    return loudness


def noise(key, dims, width, bound, pieces=(), kind=jnp.bfloat16):
    values = width * jax.random.normal(key, dims, jnp.float32)
    if pieces:
        values = values * levels(key, dims, pieces, -0.22, 0.18)
    return jnp.clip(values, -bound, bound).astype(kind)


def setup_inputs(seed: int = 0) -> dict:
    keys = jax.random.split(jax.random.key(seed), 11)
    courant_squared = jnp.clip(jnp.exp(math.log(0.18) - 1.50407746 * jax.random.uniform(keys[0], (BPO, N_SHOT, BX, NY, NZ), jnp.float32) ** levels(keys[0], (BPO, N_SHOT, BX, NY, NZ), ((1, 16), (3, 8)), -0.2, 0.2)), 0.04, 0.18)
    wave_now = noise(keys[1], (N_SHOT, NXA, NY, NZ), 0.3, 1.75, ((0, 16), (1, 8)), jnp.float32)
    wave_prev = noise(keys[2], (N_SHOT, NXA, NY, NZ), 0.3, 1.75, ((0, 16), (1, 8)), jnp.float32)
    adj_late = noise(keys[3], (N_SHOT, NXA, NY, NZ), 0.3, 1.75, ((0, 16), (1, 8)), jnp.float32)
    adj_later = noise(keys[4], (N_SHOT, NXA, NY, NZ), 0.3, 1.75, ((0, 16), (1, 8)), jnp.float32)
    wavelet = noise(keys[5], (N_SHOT, STEPS), 1.0, 6.0, ((0, 16),), jnp.float32)
    sources = touch_ends(jax.random.randint(keys[6], (N_SHOT,), 0, NXA * NY * NZ), jax.random.fold_in(keys[6], 1), 0, (NXA * NY * NZ) - 1).astype(jnp.int32)
    receivers = touch_ends(jax.random.randint(keys[7], (N_SHOT, NREC), 0, NXA * NY * NZ), jax.random.fold_in(keys[7], 1), 0, (NXA * NY * NZ) - 1).astype(jnp.int32)
    observed = noise(keys[8], (N_SHOT, STEPS, NREC), 1.0, 6.0, ((0, 16),), jnp.float32)
    apertures = draw_apertures(jax.random.fold_in(keys[10], 71), 0)
    return {"courant_squared": courant_squared, "wave_now": wave_now, "wave_prev": wave_prev, "adj_late": adj_late, "adj_later": adj_later, "wavelet": wavelet, "sources": sources, "receivers": receivers, "observed": observed, "apertures": apertures}


STENCIL = (-205.0 / 72.0, 8.0 / 5.0, -1.0 / 5.0, 8.0 / 315.0, -1.0 / 560.0)


def laplace(wavefield):
    padded = jnp.pad(wavefield, 4)
    size_x, size_y, size_z = wavefield.shape
    summed = (3.0 * STENCIL[0]) * wavefield
    for shift_by in range(1, 5):
        beside = padded[4 + shift_by:4 + shift_by + size_x, 4:4 + size_y, 4:4 + size_z] + padded[4 - shift_by:4 - shift_by + size_x, 4:4 + size_y, 4:4 + size_z]
        beside = beside + padded[4:4 + size_x, 4 + shift_by:4 + shift_by + size_y, 4:4 + size_z] + padded[4:4 + size_x, 4 - shift_by:4 - shift_by + size_y, 4:4 + size_z]
        beside = beside + padded[4:4 + size_x, 4:4 + size_y, 4 + shift_by:4 + shift_by + size_z] + padded[4:4 + size_x, 4:4 + size_y, 4 - shift_by:4 - shift_by + size_z]
        summed = summed + STENCIL[shift_by] * beside
    return summed


def one_shot(shot_id, grid, wave_now, wave_prev, adj_late, adj_later, wavelet, sources, receivers, observed, apertures):
    zero_index = jnp.zeros((), jnp.int32)
    offset = (apertures[shot_id, 0] * BX).astype(jnp.int32)
    courant = lax.dynamic_slice(grid, (offset, zero_index, zero_index), (NXA, NY, NZ))
    current = wave_now[shot_id]
    earlier = wave_prev[shot_id]
    source_cell = sources[shot_id]
    recv_cells = receivers[shot_id]
    lap_terms = []
    samples = []
    for step in range(STEPS):
        lap_now = laplace(current)
        lap_terms.append(lap_now)
        next_wave = 2.0 * current - earlier + courant * lap_now
        next_wave = next_wave.reshape(-1).at[source_cell].add(wavelet[shot_id, step]).reshape(current.shape)
        samples.append(next_wave.reshape(-1)[recv_cells])
        earlier, current = current, next_wave
    adj_older = adj_later[shot_id]
    adj_newer = adj_late[shot_id]
    gradient_sum = jnp.zeros_like(current)
    for step in range(STEPS, 0, -1):
        adjoint = 2.0 * adj_newer + laplace(courant * adj_newer) - adj_older
        misfit = samples[step - 1] - observed[shot_id, step - 1]
        adjoint = adjoint.reshape(-1).at[recv_cells].add(misfit).reshape(current.shape)
        gradient_sum = gradient_sum + adjoint * lap_terms[step - 1]
        adj_older, adj_newer = adj_newer, adjoint
    return gradient_sum


def reference(courant_squared, wave_now, wave_prev, adj_late, adj_later, wavelet, sources, receivers, observed, apertures):
    grid = courant_squared.reshape(NBLK * BX, NY, NZ)
    zero_index = jnp.zeros((), jnp.int32)

    def accumulate(carry, shot_id):
        shot_grad = one_shot(shot_id, grid, wave_now, wave_prev, adj_late, adj_later, wavelet, sources, receivers, observed, apertures)
        offset = (apertures[shot_id, 0] * BX).astype(jnp.int32)
        before = lax.dynamic_slice(carry, (offset, zero_index, zero_index), (NXA, NY, NZ))
        carry = lax.dynamic_update_slice(carry, before + shot_grad, (offset, zero_index, zero_index))
        return carry, None

    summed, _ = lax.scan(accumulate, jnp.zeros((NBLK * BX, NY, NZ), jnp.float32), jnp.arange(N_SHOT, dtype=jnp.int32))
    return summed.reshape(BPO, N_SHOT, BX, NY, NZ)
```

```python
import functools

import jax
import jax.numpy as jnp
import ml_dtypes
import numpy as np
from jax import lax
from jax.experimental import pallas as pl
from jax.experimental.pallas import tpu as pltpu
from jax.sharding import PartitionSpec as P

STEPS = 4
STENCIL = (-205.0 / 72.0, 8.0 / 5.0, -1.0 / 5.0, 8.0 / 315.0, -1.0 / 560.0)
F32 = jnp.float32
BF16 = jnp.bfloat16
SMEM = pl.BlockSpec(memory_space=pltpu.SMEM)
VMEM = pl.BlockSpec(memory_space=pltpu.VMEM)
NX, NYL, NZ = 64, 32, 128
GROUP = 8
PAD = 4
ROW0 = 8
ROWS = 48


def depth_operator():
    band = np.zeros((NZ, NZ), np.float32)
    for i in range(NZ):
        band[i, i] = np.float32(3.0 * STENCIL[0])
        for k in range(1, 5):
            for j in (i - k, i + k):
                if 0 <= j < NZ:
                    band[j, i] = np.float32(STENCIL[k])
    high = band.astype(ml_dtypes.bfloat16)
    low = (band - high.astype(np.float32)).astype(ml_dtypes.bfloat16)
    zero = np.zeros_like(high)
    return np.block([[high, low], [high, zero]])


def fill_edges(ext, halo_lo, halo_hi):
    zeros = jnp.zeros((PAD, ROWS, NZ), F32)
    ext[0:PAD] = zeros
    ext[PAD + NX : 2 * PAD + NX] = zeros

    def body(t, carry):
        lo = halo_lo[t]
        hi = halo_hi[t]
        for half in range(2):
            x = PAD + 2 * t + half
            ext[x, ROW0 - 4 : ROW0, :] = lo[4 * half : 4 * half + 4]
            ext[x, ROW0 + NYL : ROW0 + NYL + 4, :] = hi[4 * half : 4 * half + 4]
        return carry

    lax.fori_loop(0, NX // 2, body, 0, unroll=4)


def laplace_group(ext, oper, g, emit):
    base = PAD + g * GROUP
    own = ext[pl.ds(base, GROUP), ROW0 : ROW0 + NYL, :].reshape(GROUP * NYL, NZ)
    high = own.astype(BF16)
    low = (own - high.astype(F32)).astype(BF16)
    prod = jnp.dot(jnp.concatenate([high, low], axis=1), oper[...], preferred_element_type=F32)
    depth = prod[:, :NZ] + prod[:, NZ:]
    depth = depth.reshape(GROUP, NYL, NZ)
    for j in range(NYL // 8):
        r0 = ROW0 + 8 * j
        col = [ext[base - PAD + i, r0 : r0 + 8, :] for i in range(GROUP + 2 * PAD)]
        for xi in range(GROUP):
            acc = depth[xi, 8 * j : 8 * j + 8, :]
            for k in range(1, 5):
                beside = (
                    col[xi + PAD + k]
                    + col[xi + PAD - k]
                    + (
                        ext[base + xi, r0 + k : r0 + k + 8, :]
                        + ext[base + xi, r0 - k : r0 - k + 8, :]
                    )
                )
                acc = acc + STENCIL[k] * beside
            emit(xi, j, acc)


def send_rows(send_lo, send_hi, read):
    def body(t, carry):
        for half in range(2):
            send_lo[t, 4 * half : 4 * half + 4, :] = read(2 * t + half, 0)
            send_hi[t, 4 * half : 4 * half + 4, :] = read(2 * t + half, NYL - 4)
        return carry

    lax.fori_loop(0, NX // 2, body, 0, unroll=4)


def forward_kernel(packed, spots, amount, now, prev, r2, halo_lo, halo_hi, oper, lap, new, send_lo, send_hi, ext):
    first = spots[0]

    def plane(ref, which, g, xi):
        return ref[g, which, xi] if packed else ref[g * GROUP + xi]

    def copy(g, carry):
        for xi in range(GROUP):
            ext[PAD + g * GROUP + xi, ROW0 : ROW0 + NYL, :] = plane(now, 0, g, xi)
        return carry

    lax.fori_loop(0, NX // GROUP, copy, 0)
    fill_edges(ext, halo_lo, halo_hi)

    def body(g, carry):
        slot = lax.rem(first + g, GROUP)

        def emit(xi, j, value):
            rows = slice(8 * j, 8 * j + 8)
            x = g * GROUP + xi
            lap[x, rows, :] = value
            here = ext[PAD + x, ROW0 + 8 * j : ROW0 + 8 * j + 8, :]
            old = prev[g, 1, xi, rows, :] if packed else prev[x, rows, :]
            new[x, rows, :] = 2.0 * here - old + r2[slot, xi, rows, :] * value

        laplace_group(ext, oper, g, emit)
        return carry

    lax.fori_loop(0, NX // GROUP, body, 0)

    @pl.when(spots[1] == 1)
    def _():
        x, y, z = spots[2], spots[3], spots[4]
        lanes = lax.broadcasted_iota(jnp.int32, (1, NZ), 1)
        row = new[x, pl.ds(y, 1), :]
        new[x, pl.ds(y, 1), :] = row + jnp.where(lanes == z, amount[0], 0.0)

    send_rows(send_lo, send_hi, lambda x, r: new[x, r : r + 4, :])


def edge_kernel(packed, weighted, spots, now, r2, send_lo, send_hi):
    first = spots[0]

    def read(x, r):
        g, xi = x // GROUP, lax.rem(x, GROUP)
        value = now[g, 0, xi, r : r + 4, :]
        if weighted:
            value = value * r2[lax.rem(first + g, GROUP), xi, r : r + 4, :]
        return value

    send_rows(send_lo, send_hi, read)


def adjoint_kernel(
    packed, begin, last, spots, late, later, r2, halo_lo, halo_hi, oper, count, data, wave, lap, *rest
):
    rest = list(rest)
    total_in = None if begin else rest.pop(0)
    if last:
        total, ext = rest
        new = send_lo = send_hi = None
    else:
        total, new, send_lo, send_hi, ext = rest
    first = spots[0]

    def load(ref, which, g, xi, rows):
        return ref[g, which, xi, rows, :] if packed == 2 or (packed == 1 and which == 1) else ref[g * GROUP + xi, rows, :]

    every = slice(0, NYL)

    def copy(g, carry):
        slot = lax.rem(first + g, GROUP)
        for xi in range(GROUP):
            ext[PAD + g * GROUP + xi, ROW0 : ROW0 + NYL, :] = load(late, 0, g, xi, every) * r2[slot, xi]
        return carry

    lax.fori_loop(0, NX // GROUP, copy, 0)
    fill_edges(ext, halo_lo, halo_hi)

    def body(g, carry):
        slot = lax.rem(first + g, GROUP)

        def emit(xi, j, value):
            rows = slice(8 * j, 8 * j + 8)
            x = g * GROUP + xi
            mu = 2.0 * load(late, 0, g, xi, rows) + value - load(later, 1, g, xi, rows)
            mu = mu + (count[x, rows, :] * wave[x, rows, :] - data[x, rows, :])
            part = mu * lap[x, rows, :]
            if total_in is not None:
                part = part + total_in[x, rows, :]
            if last:
                total[slot, xi, rows, :] = part
            else:
                total[x, rows, :] = part
                new[x, rows, :] = mu

        laplace_group(ext, oper, g, emit)
        return carry

    lax.fori_loop(0, NX // GROUP, body, 0)
    if not last:

        def read(x, r):
            g, xi = x // GROUP, lax.rem(x, GROUP)
            return new[x, r : r + 4, :] * r2[lax.rem(first + g, GROUP), xi, r : r + 4, :]

        send_rows(send_lo, send_hi, read)


def receivers_kernel(cells, mine, observed, count, *datas):
    zeros = jnp.zeros((NYL, NZ), F32)

    def clear(x, carry):
        count[x] = zeros
        for d in datas:
            d[x] = zeros
        return carry

    lax.fori_loop(0, NX, clear, 0)
    lanes = lax.broadcasted_iota(jnp.int32, (1, NZ), 1)

    def body(r, carry):
        @pl.when(mine[r] == 1)
        def _():
            cell = cells[r]
            x = cell // (256 * NZ)
            y = lax.rem(cell // NZ, NYL)
            hit = lanes == lax.rem(cell, NZ)
            count[x, pl.ds(y, 1), :] = count[x, pl.ds(y, 1), :] + jnp.where(hit, 1.0, 0.0)
            for n, d in enumerate(datas):
                d[x, pl.ds(y, 1), :] = d[x, pl.ds(y, 1), :] + jnp.where(hit, observed[n, r], 0.0)

        return carry

    lax.fori_loop(0, cells.shape[0], body, 0)


def bins_kernel(slots, half, recv, keep, give):
    zeros = jnp.zeros((GROUP, NYL, NZ), F32)
    for i in range(2):
        keep[i] = zeros
        give[i] = zeros
    mine = half[0]
    for t in range(GROUP):
        m = slots[t]
        i = m // 2

        @pl.when(lax.rem(m, 2) == mine)
        def _():
            keep[i] = keep[i] + recv[t]

        @pl.when(lax.rem(m, 2) != mine)
        def _():
            give[i] = give[i] + recv[t]


FIELD = jax.ShapeDtypeStruct((NX, NYL, NZ), F32)
EDGE = jax.ShapeDtypeStruct((NX // 2, 8, NZ), F32)
EXT = pltpu.VMEM((NX + 2 * PAD, ROWS, NZ), F32)
PARAMS = pltpu.CompilerParams(vmem_limit_bytes=48 * 1024 * 1024)


def call(kernel, specs, outs, scratch=(), flops=0, moved=0):
    return pl.pallas_call(
        kernel,
        in_specs=specs,
        out_specs=[VMEM] * len(outs),
        out_shape=outs,
        scratch_shapes=list(scratch),
        compiler_params=PARAMS,
        cost_estimate=pl.CostEstimate(flops=flops, bytes_accessed=moved, transcendentals=0),
    )


def per_device(
    courant_squared,
    wave_now,
    wave_prev,
    adj_late,
    adj_later,
    wavelet,
    sources,
    receivers,
    observed,
    apertures,
):
    me = lax.axis_index("shot")
    part = lax.axis_index("sub")
    half, clas = me // 8, me % 8
    starts = apertures[:, 0]
    first = starts[me]
    oper = jnp.asarray(depth_operator())
    up = [(i, i + 1) for i in range(7)]
    down = [(i + 1, i) for i in range(7)]
    across = [(i, (i + 8) % 16) for i in range(16)]
    halves = [list(range(8)), list(range(8, 16))]

    def edges(lo, hi):
        return lax.ppermute(hi, "sub", up), lax.ppermute(lo, "sub", down)

    def turn(a, b):
        both = jnp.stack([f[0].reshape(GROUP, 8, NYL, NZ).transpose(1, 0, 2, 3) for f in (a, b)], axis=1)
        return lax.all_to_all(both, "sub", 0, 0, tiled=True)

    piece = courant_squared[:, 0]
    other = lax.ppermute(piece, "shot", across)
    mine_first = half == 0
    cand = jnp.stack(
        [
            jnp.where(mine_first, piece[0], other[0]),
            jnp.where(mine_first, other[0], piece[0]),
            jnp.where(mine_first, piece[1], other[1]),
            jnp.where(mine_first, other[1], piece[1]),
        ]
    )
    group_starts = lax.dynamic_slice(starts, (half * 8,), (8,))
    slots = (group_starts + (clas - group_starts) % 8) // 8
    r2 = lax.all_to_all(jnp.take(cand, slots, axis=0), "shot", 0, 0, axis_index_groups=halves, tiled=True)

    waves = turn(wave_now, wave_prev)
    adjs = turn(adj_late, adj_later)

    cell = sources[0]
    row = (cell // NZ) % 256
    spots = jnp.stack([first % 8, (row // NYL == part).astype(jnp.int32), cell // (256 * NZ), row % NYL, cell % NZ])
    cells = receivers[0]
    mine = ((cells // NZ) % 256 // NYL == part).astype(jnp.int32)
    count, *datas = call(receivers_kernel, [SMEM] * 3, [FIELD] * 5, moved=6 << 20)(cells, mine, observed[0])

    send = call(functools.partial(edge_kernel, True, False), [SMEM, VMEM, VMEM], [EDGE] * 2, moved=1 << 20)(spots, waves, r2)
    laps, fields = [], []
    now, prev = waves, waves
    for step in range(STEPS):
        halo = edges(*send)
        if step == 1:
            prev = waves[:, 0].reshape(NX, NYL, NZ)
        lap, new, *send = call(
            functools.partial(forward_kernel, step == 0),
            [SMEM, SMEM] + [VMEM] * 6,
            [FIELD, FIELD, EDGE, EDGE],
            [EXT],
            flops=10 << 20,
            moved=6 << 20,
        )(spots, wavelet[0, step : step + 1], now, prev, r2, *halo, oper)
        laps.append(lap)
        fields.append(new)
        now, prev = new, now

    send = call(functools.partial(edge_kernel, True, True), [SMEM, VMEM, VMEM], [EDGE] * 2, moved=1 << 20)(spots, adjs, r2)
    late, later = adjs, adjs
    total = None
    for step in range(STEPS, 0, -1):
        halo = edges(*send)
        begin, last = step == STEPS, step == 1
        if step == STEPS - 1:
            later = adjs[:, 0].reshape(NX, NYL, NZ)
        outs = [jax.ShapeDtypeStruct((8, GROUP, NYL, NZ), F32)] if last else [FIELD, FIELD, EDGE, EDGE]
        args = [spots, late, later, r2, *halo, oper, count, datas[step - 1], fields[step - 1], laps[step - 1]]
        if not begin:
            args.append(total)
        total, *more = call(
            functools.partial(adjoint_kernel, 2 if begin else 0, begin, last),
            [SMEM] + [VMEM] * (len(args) - 1),
            outs,
            [EXT],
            flops=10 << 20,
            moved=8 << 20,
        )(*args)
        if not last:
            late, later = more[0], late
            send = more[1:]

    recv = lax.all_to_all(total, "shot", 0, 0, axis_index_groups=halves, tiled=True)
    owned = jax.ShapeDtypeStruct((2, GROUP, NYL, NZ), F32)
    keep, give = call(bins_kernel, [SMEM, SMEM, VMEM], [owned, owned], moved=2 << 20)(slots, half[None], recv)
    result = keep + lax.ppermute(give, "shot", across)
    return result[:, None]


def solution(mesh):
    in_specs = (
        P(None, "shot", None, "sub", None),
        P("shot", "sub", None, None),
        P("shot", "sub", None, None),
        P("shot", "sub", None, None),
        P("shot", "sub", None, None),
        P("shot", None),
        P("shot"),
        P("shot", None),
        P("shot", None, None),
        P(),
    )
    out_specs = P(None, "shot", None, "sub", None)
    return jax.shard_map(
        per_device, mesh=mesh, in_specs=in_specs, out_specs=out_specs, check_vma=False
    )
```

```python
import functools

import jax
import jax.numpy as jnp
import ml_dtypes
import numpy as np
from jax import lax
from jax.experimental import pallas as pl
from jax.experimental.pallas import tpu as pltpu
from jax.sharding import PartitionSpec as P

STEPS = 4
STENCIL = (-205.0 / 72.0, 8.0 / 5.0, -1.0 / 5.0, 8.0 / 315.0, -1.0 / 560.0)
F32 = jnp.float32
BF16 = jnp.bfloat16
SMEM = pl.BlockSpec(memory_space=pltpu.SMEM)
VMEM = pl.BlockSpec(memory_space=pltpu.VMEM)
NX, NYL, NZ = 64, 32, 128
GROUP = 8
PAD = 4
ROW0 = 8
ROWS = 48


def depth_operator():
    band = np.zeros((NZ, NZ), np.float32)
    for i in range(NZ):
        band[i, i] = np.float32(3.0 * STENCIL[0])
        for k in range(1, 5):
            for j in (i - k, i + k):
                if 0 <= j < NZ:
                    band[j, i] = np.float32(STENCIL[k])
    high = band.astype(ml_dtypes.bfloat16)
    low = (band - high.astype(np.float32)).astype(ml_dtypes.bfloat16)
    zero = np.zeros_like(high)
    return np.block([[high, low], [high, zero]])


def read_field(ref, off, g, xi, rows):
    if off is None:
        return ref[g * GROUP + xi, rows, :]
    return ref[g, xi, off + rows.start : off + rows.stop, :]


def clear_ends(ext):
    zeros = jnp.zeros((PAD, ROWS, NZ), F32)
    ext[0:PAD] = zeros
    ext[PAD + NX : 2 * PAD + NX] = zeros


def fill_edges(ext, spots, halo_lo, halo_hi):
    has_lo, has_hi = spots[5] == 1, spots[6] == 1

    def body(t, carry):
        lo = jnp.where(has_lo, halo_lo[t], 0.0)
        hi = jnp.where(has_hi, halo_hi[t], 0.0)
        for half in range(2):
            x = PAD + 2 * t + half
            ext[x, ROW0 - 4 : ROW0, :] = lo[4 * half : 4 * half + 4]
            ext[x, ROW0 + NYL : ROW0 + NYL + 4, :] = hi[4 * half : 4 * half + 4]
        return carry

    lax.fori_loop(0, NX // 2, body, 0, unroll=4)


def apply_depth(ext, oper, depth):
    own = ext[PAD : PAD + NX, ROW0 : ROW0 + NYL, :].reshape(NX * NYL, NZ)
    high = own.astype(BF16)
    low = (own - high.astype(F32)).astype(BF16)
    prod = jnp.dot(jnp.concatenate([high, low], axis=1), oper[...], preferred_element_type=F32)
    depth[...] = (prod[:, :NZ] + prod[:, NZ:]).reshape(NX, NYL, NZ)


def laplace_group(ext, depth, g, emit):
    base = PAD + g * GROUP
    for j in range(NYL // 8):
        r0 = ROW0 + 8 * j
        col = [ext[base - PAD + i, r0 : r0 + 8, :] for i in range(GROUP + 2 * PAD)]
        for xi in range(GROUP):
            acc = depth[g * GROUP + xi, 8 * j : 8 * j + 8, :]
            for k in range(1, 5):
                beside = (
                    col[xi + PAD + k]
                    + col[xi + PAD - k]
                    + (
                        ext[base + xi, r0 + k : r0 + k + 8, :]
                        + ext[base + xi, r0 - k : r0 - k + 8, :]
                    )
                )
                acc = acc + STENCIL[k] * beside
            emit(xi, j, acc)


def send_rows(send_lo, send_hi, read):
    def body(t, carry):
        for half in range(2):
            send_lo[t, 4 * half : 4 * half + 4, :] = read(2 * t + half, slice(0, 4))
            send_hi[t, 4 * half : 4 * half + 4, :] = read(2 * t + half, slice(NYL - 4, NYL))
        return carry

    lax.fori_loop(0, NX // 2, body, 0, unroll=4)


EVERY = slice(0, NYL)


def forward_kernel(off_now, off_prev, last, spots, amount, now, prev, r2, oper, *rest):
    rest = list(rest)
    halos = None if off_now is not None else (rest.pop(0), rest.pop(0))
    if last:
        lap, new, ext, depth = rest
    else:
        lap, new, send_lo, send_hi, ext, depth = rest

    clear_ends(ext)

    def copy(g, carry):
        for xi in range(GROUP):
            ext[PAD + g * GROUP + xi, ROW0 : ROW0 + NYL, :] = read_field(now, off_now, g, xi, EVERY)
            if halos is None:
                edge = now[g, xi, EDGES : EDGES + 8, :]
                ext[PAD + g * GROUP + xi, ROW0 - 4 : ROW0, :] = edge[0:4]
                ext[PAD + g * GROUP + xi, ROW0 + NYL : ROW0 + NYL + 4, :] = edge[4:8]
        return carry

    lax.fori_loop(0, NX // GROUP, copy, 0)
    if halos is not None:
        fill_edges(ext, spots, *halos)
    apply_depth(ext, oper, depth)

    def body(g, carry):
        def emit(xi, j, value):
            rows = slice(8 * j, 8 * j + 8)
            x = g * GROUP + xi
            lap[x, rows, :] = value
            here = ext[PAD + x, ROW0 + 8 * j : ROW0 + 8 * j + 8, :]
            new[x, rows, :] = 2.0 * here - read_field(prev, off_prev, g, xi, rows) + r2[g, xi, rows, :] * value

        laplace_group(ext, depth, g, emit)
        return carry

    lax.fori_loop(0, NX // GROUP, body, 0)

    @pl.when(spots[1] == 1)
    def _():
        x, y, z = spots[2], spots[3], spots[4]
        lanes = lax.broadcasted_iota(jnp.int32, (1, NZ), 1)
        row = new[x, pl.ds(y, 1), :]
        new[x, pl.ds(y, 1), :] = row + jnp.where(lanes == z, amount[0], 0.0)

    if not last:
        send_rows(send_lo, send_hi, lambda x, rows: new[x, rows, :])


def edge_kernel(turned, r2, send_lo, send_hi):
    def read(x, rows):
        g, xi = x // GROUP, lax.rem(x, GROUP)
        return read_field(turned, LATE, g, xi, rows) * r2[g, xi, rows, :]

    send_rows(send_lo, send_hi, read)


def adjoint_kernel(
    off_late, off_later, begin, last, spots, late, later, r2, halo_lo, halo_hi, oper, count, data, wave, lap, *rest
):
    rest = list(rest)
    total_in = None if begin else rest.pop(0)
    if last:
        total, ext, depth = rest
    else:
        total, new, send_lo, send_hi, ext, depth = rest
    first = spots[0]

    clear_ends(ext)

    def copy(g, carry):
        for xi in range(GROUP):
            ext[PAD + g * GROUP + xi, ROW0 : ROW0 + NYL, :] = (
                read_field(late, off_late, g, xi, EVERY) * r2[g, xi]
            )
        return carry

    lax.fori_loop(0, NX // GROUP, copy, 0)
    fill_edges(ext, spots, halo_lo, halo_hi)
    apply_depth(ext, oper, depth)

    def body(g, carry):
        slot = lax.rem(first + g, GROUP)

        def emit(xi, j, value):
            rows = slice(8 * j, 8 * j + 8)
            x = g * GROUP + xi
            mu = 2.0 * read_field(late, off_late, g, xi, rows) + value - read_field(later, off_later, g, xi, rows)
            mu = mu + (count[x, rows, :] * wave[x, rows, :] - data[x, rows, :])
            part = mu * lap[x, rows, :]
            if total_in is not None:
                part = part + total_in[x, rows, :]
            if last:
                total[slot, xi, rows, :] = part
            else:
                total[x, rows, :] = part
                new[x, rows, :] = mu

        laplace_group(ext, depth, g, emit)
        return carry

    lax.fori_loop(0, NX // GROUP, body, 0)
    if not last:

        def read(x, rows):
            return new[x, rows, :] * r2[x // GROUP, lax.rem(x, GROUP), rows, :]

        send_rows(send_lo, send_hi, read)


NOW, PREV, LATE, LATER, EDGES, TURNED = 0, 32, 64, 96, 128, 136


def pack_kernel(now, prev, late, later, out):
    none = jnp.zeros((4, NZ), F32)

    def body(xi, carry):
        for p in range(8):
            lo = NYL * p
            for off, field in ((NOW, now), (PREV, prev), (LATE, late), (LATER, later)):
                out[p, xi, off : off + NYL, :] = field[xi, lo : lo + NYL, :]
            out[p, xi, EDGES : EDGES + 4, :] = now[xi, lo - 4 : lo, :] if p > 0 else none
            out[p, xi, EDGES + 4 : EDGES + 8, :] = now[xi, lo + NYL : lo + NYL + 4, :] if p < 7 else none
        return carry

    lax.fori_loop(0, GROUP, body, 0)


def copy_block(dst, src):
    def body(x, carry):
        dst[x] = src[x]
        return carry

    lax.fori_loop(0, GROUP, body, 0, unroll=4)


def select_kernel(slots, here, piece, other, piece_c, other_c, *outs):
    half, core = here[0], here[1]
    for k in range(4):
        for j in range(2):
            m = slots[2 * k + j]
            row = m // 2
            own_half = lax.rem(m, 2) == half
            own_core = core == j
            for src, same_half, same_core in (
                (piece, True, True),
                (other, False, True),
                (piece_c, True, False),
                (other_c, False, False),
            ):

                @pl.when(jnp.logical_and(own_half == same_half, own_core == same_core))
                def _():
                    copy_block(outs[k].at[j], src.at[row])


def assemble_kernel(places, r0, r1, r2, r3, out):
    for k, src in enumerate((r0, r1, r2, r3)):
        for j in range(2):
            copy_block(out.at[places[2 * k + j]], src.at[j])


def receivers_kernel(cells, mine, observed, count, *datas):
    zeros = jnp.zeros((NYL, NZ), F32)

    def clear(x, carry):
        count[x] = zeros
        for d in datas:
            d[x] = zeros
        return carry

    lax.fori_loop(0, NX, clear, 0)
    lanes = lax.broadcasted_iota(jnp.int32, (1, NZ), 1)

    def body(r, carry):
        @pl.when(mine[r] == 1)
        def _():
            cell = cells[r]
            x = cell // (256 * NZ)
            y = lax.rem(cell // NZ, NYL)
            hit = lanes == lax.rem(cell, NZ)
            count[x, pl.ds(y, 1), :] = count[x, pl.ds(y, 1), :] + jnp.where(hit, 1.0, 0.0)
            for n, d in enumerate(datas):
                d[x, pl.ds(y, 1), :] = d[x, pl.ds(y, 1), :] + jnp.where(hit, observed[n, r], 0.0)

        return carry

    lax.fori_loop(0, cells.shape[0], body, 0)


def bins_kernel(slots, half, recv, keep, give):
    zeros = jnp.zeros((GROUP, NYL, NZ), F32)
    for i in range(2):
        keep[i] = zeros
        give[i] = zeros
    mine = half[0]
    for t in range(GROUP):
        m = slots[t]
        i = m // 2

        @pl.when(lax.rem(m, 2) == mine)
        def _():
            keep[i] = keep[i] + recv[t]

        @pl.when(lax.rem(m, 2) != mine)
        def _():
            give[i] = give[i] + recv[t]


FIELD = jax.ShapeDtypeStruct((NX, NYL, NZ), F32)
EDGE = jax.ShapeDtypeStruct((NX // 2, 8, NZ), F32)
BLOCKS = jax.ShapeDtypeStruct((8, GROUP, NYL, NZ), F32)
PAIR = jax.ShapeDtypeStruct((2, GROUP, NYL, NZ), F32)
SCRATCH = [pltpu.VMEM((NX + 2 * PAD, ROWS, NZ), F32), pltpu.VMEM((NX, NYL, NZ), F32)]
PARAMS = pltpu.CompilerParams(vmem_limit_bytes=14 * 1024 * 1024)


def call(kernel, specs, outs, scratch=(), flops=0, moved=0):
    return pl.pallas_call(
        kernel,
        in_specs=specs,
        out_specs=[VMEM] * len(outs),
        out_shape=outs,
        scratch_shapes=list(scratch),
        compiler_params=PARAMS,
        cost_estimate=pl.CostEstimate(flops=flops, bytes_accessed=moved, transcendentals=0),
    )


def per_device(
    courant_squared,
    wave_now,
    wave_prev,
    adj_late,
    adj_later,
    wavelet,
    sources,
    receivers,
    observed,
    apertures,
):
    me = lax.axis_index("shot")
    part = lax.axis_index("sub")
    half, clas = me // 8, me % 8
    row, core = clas // 2, clas % 2
    starts = apertures[:, 0]
    first = starts[me]
    oper = jnp.asarray(depth_operator())
    up = [(i, (i + 1) % 8) for i in range(8)]
    down = [((i + 1) % 8, i) for i in range(8)]
    across = [(i, (i + 8) % 16) for i in range(16)]
    chip = [(i, i ^ 1) for i in range(16)]
    halves = [list(range(8)), list(range(8, 16))]

    def along(k):
        return [(8 * h + 2 * y + c, 8 * h + 2 * ((y + k) % 4) + c) for h in range(2) for y in range(4) for c in range(2)]

    def edges(lo, hi):
        return lax.ppermute(hi, "sub", up), lax.ppermute(lo, "sub", down)

    piece = courant_squared[:, 0]
    other = lax.ppermute(piece, "shot", across)
    piece_c = lax.ppermute(piece, "shot", chip)
    other_c = lax.ppermute(other, "shot", chip)
    ahead = jnp.arange(4)
    two = jnp.arange(2)
    want = starts[half * 8 + (row + ahead) % 4 * 2 + core][:, None]
    have = (2 * row + two)[None, :]
    chosen = ((want + (have - want) % 8) // 8).reshape(8).astype(jnp.int32)
    here = jnp.stack([half, core]).astype(jnp.int32)
    blocks = call(select_kernel, [SMEM] * 2 + [VMEM] * 4, [PAIR] * 4, moved=2 << 20)(chosen, here, piece, other, piece_c, other_c)
    come = [blocks[0]] + [lax.ppermute(blocks[k], "shot", along(k)) for k in (1, 2, 3)]
    from_class = ((row - ahead) % 4 * 2)[:, None] + two[None, :]
    places = ((from_class - first) % 8).reshape(8).astype(jnp.int32)

    (packed,) = call(pack_kernel, [VMEM] * 4, [jax.ShapeDtypeStruct((8, GROUP, TURNED, NZ), F32)], moved=8 << 20)(
        wave_now[0], wave_prev[0], adj_late[0], adj_later[0]
    )
    packed, come[1] = lax.optimization_barrier((packed, come[1]))
    turned = lax.all_to_all(packed, "sub", 0, 0, tiled=True)
    (r2,) = call(assemble_kernel, [SMEM] + [VMEM] * 4, [BLOCKS], moved=2 << 20)(places, *come)

    cell = sources[0]
    line = (cell // NZ) % 256
    spots = jnp.stack(
        [
            first % 8,
            (line // NYL == part).astype(jnp.int32),
            cell // (256 * NZ),
            line % NYL,
            cell % NZ,
            (part > 0).astype(jnp.int32),
            (part < 7).astype(jnp.int32),
        ]
    )
    cells = receivers[0]
    mine = ((cells // NZ) % 256 // NYL == part).astype(jnp.int32)
    count, *datas = call(receivers_kernel, [SMEM] * 3, [FIELD] * 5, moved=6 << 20)(cells, mine, observed[0])

    laps, fields = [], []
    now, prev = turned, turned
    offs = (NOW, PREV)
    halo = ()
    for step in range(STEPS):
        last = step == STEPS - 1
        args = [spots, wavelet[0, step : step + 1], now, prev, r2, oper, *halo]
        lap, new, *send = call(
            functools.partial(forward_kernel, *offs, last),
            [SMEM, SMEM] + [VMEM] * (len(args) - 2),
            [FIELD, FIELD] + ([] if last else [EDGE, EDGE]),
            SCRATCH,
            flops=10 << 20,
            moved=6 << 20,
        )(*args)
        laps.append(lap)
        fields.append(new)
        now, prev = new, now
        offs = (None, offs[0])
        if not last:
            halo = edges(*send)

    send = call(edge_kernel, [VMEM, VMEM], [EDGE] * 2, moved=1 << 20)(turned, r2)
    late, later = turned, turned
    offs = (LATE, LATER)
    total = None
    for step in range(STEPS, 0, -1):
        halo = edges(*send)
        begin, last = step == STEPS, step == 1
        outs = [BLOCKS] if last else [FIELD, FIELD, EDGE, EDGE]
        args = [spots, late, later, r2, *halo, oper, count, datas[step - 1], fields[step - 1], laps[step - 1]]
        if not begin:
            args.append(total)
        total, *more = call(
            functools.partial(adjoint_kernel, *offs, begin, last),
            [SMEM] + [VMEM] * (len(args) - 1),
            outs,
            SCRATCH,
            flops=10 << 20,
            moved=8 << 20,
        )(*args)
        if not last:
            late, later = more[0], late
            offs = (None, offs[0])
            send = more[1:]

    recv = lax.all_to_all(total, "shot", 0, 0, axis_index_groups=halves, tiled=True)
    group = starts[half * 8 + jnp.arange(8)]
    slots = ((group + (clas - group) % 8) // 8).astype(jnp.int32)
    keep, give = call(bins_kernel, [SMEM, SMEM, VMEM], [PAIR, PAIR], moved=2 << 20)(slots, half[None], recv)
    result = keep + lax.ppermute(give, "shot", across)
    return result[:, None]


def solution(mesh):
    in_specs = (
        P(None, "shot", None, "sub", None),
        P("shot", "sub", None, None),
        P("shot", "sub", None, None),
        P("shot", "sub", None, None),
        P("shot", "sub", None, None),
        P("shot", None),
        P("shot"),
        P("shot", None),
        P("shot", None, None),
        P(),
    )
    out_specs = P(None, "shot", None, "sub", None)
    return jax.shard_map(
        per_device, mesh=mesh, in_specs=in_specs, out_specs=out_specs, check_vma=False
    )
```

```python
import functools

import jax
import jax.numpy as jnp
import ml_dtypes
import numpy as np
from jax import lax
from jax.experimental import pallas as pl
from jax.experimental.pallas import tpu as pltpu
from jax.sharding import PartitionSpec as P

STEPS = 4
STENCIL = (-205.0 / 72.0, 8.0 / 5.0, -1.0 / 5.0, 8.0 / 315.0, -1.0 / 560.0)
F32 = jnp.float32
BF16 = jnp.bfloat16
SMEM = pl.BlockSpec(memory_space=pltpu.SMEM)
VMEM = pl.BlockSpec(memory_space=pltpu.VMEM)
ANY = pl.BlockSpec(memory_space=pltpu.HBM)
NX, NYL, NZ = 64, 32, 128
GROUP = 8
PAD = 4
ROW0 = 8
ROWS = 48


def depth_operator():
    band = np.zeros((NZ, NZ), np.float32)
    for i in range(NZ):
        band[i, i] = np.float32(3.0 * STENCIL[0])
        for k in range(1, 5):
            for j in (i - k, i + k):
                if 0 <= j < NZ:
                    band[j, i] = np.float32(STENCIL[k])
    high = band.astype(ml_dtypes.bfloat16)
    low = (band - high.astype(np.float32)).astype(ml_dtypes.bfloat16)
    zero = np.zeros_like(high)
    return np.block([[high, low], [high, zero]])


def clear_ends(ext):
    zeros = jnp.zeros((PAD, ROWS, NZ), F32)
    ext[0:PAD] = zeros
    ext[PAD + NX : 2 * PAD + NX] = zeros


def fill_edges(ext, spots, halo_lo, halo_hi):
    has_lo, has_hi = spots[5] == 1, spots[6] == 1

    def body(t, carry):
        lo = jnp.where(has_lo, halo_lo[t], 0.0)
        hi = jnp.where(has_hi, halo_hi[t], 0.0)
        for half in range(2):
            x = PAD + 2 * t + half
            ext[x, ROW0 - 4 : ROW0, :] = lo[4 * half : 4 * half + 4]
            ext[x, ROW0 + NYL : ROW0 + NYL + 4, :] = hi[4 * half : 4 * half + 4]
        return carry

    lax.fori_loop(0, NX // 2, body, 0, unroll=4)


def apply_depth(ext, oper, depth):
    own = ext[PAD : PAD + NX, ROW0 : ROW0 + NYL, :].reshape(NX * NYL, NZ)
    high = own.astype(BF16)
    low = (own - high.astype(F32)).astype(BF16)
    prod = jnp.dot(jnp.concatenate([high, low], axis=1), oper[...], preferred_element_type=F32)
    depth[...] = (prod[:, :NZ] + prod[:, NZ:]).reshape(NX, NYL, NZ)


def laplace_group(ext, depth, g, emit):
    base = PAD + g * GROUP
    for j in range(NYL // 8):
        r0 = ROW0 + 8 * j
        col = [ext[base - PAD + i, r0 : r0 + 8, :] for i in range(GROUP + 2 * PAD)]
        for xi in range(GROUP):
            acc = depth[g * GROUP + xi, 8 * j : 8 * j + 8, :]
            for k in range(1, 5):
                beside = (
                    col[xi + PAD + k]
                    + col[xi + PAD - k]
                    + (
                        ext[base + xi, r0 + k : r0 + k + 8, :]
                        + ext[base + xi, r0 - k : r0 - k + 8, :]
                    )
                )
                acc = acc + STENCIL[k] * beside
            emit(xi, j, acc)


def send_rows(send_lo, send_hi, read):
    def body(t, carry):
        for half in range(2):
            send_lo[t, 4 * half : 4 * half + 4, :] = read(2 * t + half, slice(0, 4))
            send_hi[t, 4 * half : 4 * half + 4, :] = read(2 * t + half, slice(NYL - 4, NYL))
        return carry

    lax.fori_loop(0, NX // 2, body, 0, unroll=4)


def add_source(spots, amount, new):
    @pl.when(spots[1] == 1)
    def _():
        x, y, z = spots[2], spots[3], spots[4]
        lanes = lax.broadcasted_iota(jnp.int32, (1, NZ), 1)
        row = new[x, pl.ds(y, 1), :]
        new[x, pl.ds(y, 1), :] = row + jnp.where(lanes == z, amount[0], 0.0)


def advance(ext, depth, oper, prev, r2, lap, new):
    apply_depth(ext, oper, depth)

    def body(g, carry):
        def emit(xi, j, value):
            rows = slice(8 * j, 8 * j + 8)
            x = g * GROUP + xi
            lap[x, rows, :] = value
            here = ext[PAD + x, ROW0 + 8 * j : ROW0 + 8 * j + 8, :]
            new[x, rows, :] = 2.0 * here - prev[x, rows, :] + r2[x, rows, :] * value

        laplace_group(ext, depth, g, emit)
        return carry

    lax.fori_loop(0, NX // GROUP, body, 0)


OWN_X, OWN_Y = slice(PAD, PAD + NX), slice(ROW0, ROW0 + NYL)


def first_kernel(
    spots, amount, turned, r2, oper, lap, new, send_lo, send_hi, now, late, later, ext, depth, prev, edge, sems
):
    def take(n, off, rows, dst):
        return pltpu.make_async_copy(turned.at[:, off : off + rows, :], dst, sems.at[n])

    copies = [
        take(0, NOW, NYL, ext.at[OWN_X, OWN_Y, :]),
        take(1, EDGES, 8, edge),
        take(2, PREV, NYL, prev),
        take(3, LATE, NYL, late),
        take(4, LATER, NYL, later),
        take(5, NOW, NYL, now),
    ]
    for c in copies:
        c.start()
    clear_ends(ext)
    for c in copies[:3]:
        c.wait()

    def fill(x, carry):
        ext[PAD + x, ROW0 - 4 : ROW0, :] = edge[x, 0:4, :]
        ext[PAD + x, ROW0 + NYL : ROW0 + NYL + 4, :] = edge[x, 4:8, :]
        return carry

    lax.fori_loop(0, NX, fill, 0, unroll=4)
    advance(ext, depth, oper, prev, r2, lap, new)
    add_source(spots, amount, new)
    send_rows(send_lo.at[0], send_hi.at[0], lambda x, rows: new[x, rows, :])
    for c in copies[3:]:
        c.wait()
    send_rows(send_lo.at[1], send_hi.at[1], lambda x, rows: late[x, rows, :] * r2[x, rows, :])


def forward_kernel(last, spots, amount, now, prev, r2, oper, halo_lo, halo_hi, *rest):
    if last:
        lap, new, ext, depth = rest
    else:
        lap, new, send_lo, send_hi, ext, depth = rest
    clear_ends(ext)
    ext[OWN_X, OWN_Y, :] = now[...]
    fill_edges(ext, spots, halo_lo.at[0], halo_hi.at[0])
    advance(ext, depth, oper, prev, r2, lap, new)
    add_source(spots, amount, new)
    if not last:
        send_rows(send_lo.at[0], send_hi.at[0], lambda x, rows: new[x, rows, :])


def adjoint_kernel(
    begin, last, spots, late, later, r2, halo_lo, halo_hi, oper, count, data, wave, lap, *rest
):
    rest = list(rest)
    total_in = None if begin else rest.pop(0)
    if last:
        total, ext, depth = rest
    else:
        total, new, send_lo, send_hi, ext, depth = rest
    first = spots[0]

    clear_ends(ext)

    ext[OWN_X, OWN_Y, :] = late[...] * r2[...]
    which = 1 if begin else 0
    fill_edges(ext, spots, halo_lo.at[which], halo_hi.at[which])
    apply_depth(ext, oper, depth)

    def body(g, carry):
        slot = lax.rem(first + g, GROUP)

        def emit(xi, j, value):
            rows = slice(8 * j, 8 * j + 8)
            x = g * GROUP + xi
            mu = 2.0 * late[x, rows, :] + value - later[x, rows, :]
            mu = mu + (count[x, rows, :] * wave[x, rows, :] - data[x, rows, :])
            part = mu * lap[x, rows, :]
            if total_in is not None:
                part = part + total_in[x, rows, :]
            if last:
                total[slot, xi, rows, :] = part
            else:
                total[x, rows, :] = part
                new[x, rows, :] = mu

        laplace_group(ext, depth, g, emit)
        return carry

    lax.fori_loop(0, NX // GROUP, body, 0)
    if not last:
        send_rows(send_lo.at[0], send_hi.at[0], lambda x, rows: new[x, rows, :] * r2[x, rows, :])


NOW, PREV, LATE, LATER, EDGES, TURNED = 0, 32, 64, 96, 128, 136


def pack_kernel(now, prev, late, later, out, near, edge, sems):
    bring = pltpu.make_async_copy(now, near, sems.at[32])
    bring.start()
    copies = []
    for p in range(8):
        for f, (off, field) in enumerate(((NOW, now), (PREV, prev), (LATE, late), (LATER, later))):
            copies.append(
                pltpu.make_async_copy(
                    field.at[:, NYL * p : NYL * p + NYL, :], out.at[p, :, off : off + NYL, :], sems.at[4 * p + f]
                )
            )
    for c in copies:
        c.start()
    none = jnp.zeros((4, NZ), F32)
    bring.wait()

    def body(xi, carry):
        for p in range(8):
            lo = NYL * p
            edge[p, xi, 0:4, :] = near[xi, lo - 4 : lo, :] if p > 0 else none
            edge[p, xi, 4:8, :] = near[xi, lo + NYL : lo + NYL + 4, :] if p < 7 else none
        return carry

    lax.fori_loop(0, GROUP, body, 0)
    ends = pltpu.make_async_copy(edge, out.at[:, :, EDGES : EDGES + 8, :], sems.at[33])
    ends.start()
    for c in copies:
        c.wait()
    ends.wait()


def copy_block(dst, src):
    def body(x, carry):
        dst[x] = src[x]
        return carry

    lax.fori_loop(0, GROUP, body, 0, unroll=4)


def select_kernel(slots, here, piece, other, piece_c, other_c, *outs):
    half, core = here[0], here[1]
    for k in range(4):
        for j in range(2):
            m = slots[2 * k + j]
            row = m // 2
            own_half = lax.rem(m, 2) == half
            own_core = core == j
            for src, same_half, same_core in (
                (piece, True, True),
                (other, False, True),
                (piece_c, True, False),
                (other_c, False, False),
            ):

                @pl.when(jnp.logical_and(own_half == same_half, own_core == same_core))
                def _():
                    copy_block(outs[k].at[j], src.at[row])


def assemble_kernel(places, r0, r1, r2, r3, out):
    for k, src in enumerate((r0, r1, r2, r3)):
        for j in range(2):
            copy_block(out.at[places[2 * k + j]], src.at[j])


def receivers_kernel(cells, mine, observed, count, *datas):
    zeros = jnp.zeros((NYL, NZ), F32)

    def clear(x, carry):
        count[x] = zeros
        for d in datas:
            d[x] = zeros
        return carry

    lax.fori_loop(0, NX, clear, 0)
    lanes = lax.broadcasted_iota(jnp.int32, (1, NZ), 1)

    def body(r, carry):
        @pl.when(mine[r] == 1)
        def _():
            cell = cells[r]
            x = cell // (256 * NZ)
            y = lax.rem(cell // NZ, NYL)
            hit = lanes == lax.rem(cell, NZ)
            count[x, pl.ds(y, 1), :] = count[x, pl.ds(y, 1), :] + jnp.where(hit, 1.0, 0.0)
            for n, d in enumerate(datas):
                d[x, pl.ds(y, 1), :] = d[x, pl.ds(y, 1), :] + jnp.where(hit, observed[n, r], 0.0)

        return carry

    lax.fori_loop(0, cells.shape[0], body, 0)


def bins_kernel(slots, half, recv, keep, give):
    zeros = jnp.zeros((GROUP, NYL, NZ), F32)
    for i in range(2):
        keep[i] = zeros
        give[i] = zeros
    mine = half[0]
    for t in range(GROUP):
        m = slots[t]
        i = m // 2

        @pl.when(lax.rem(m, 2) == mine)
        def _():
            keep[i] = keep[i] + recv[t]

        @pl.when(lax.rem(m, 2) != mine)
        def _():
            give[i] = give[i] + recv[t]


FIELD = jax.ShapeDtypeStruct((NX, NYL, NZ), F32)
EDGE = jax.ShapeDtypeStruct((1, NX // 2, 8, NZ), F32)
EDGE2 = jax.ShapeDtypeStruct((2, NX // 2, 8, NZ), F32)
BLOCKS = jax.ShapeDtypeStruct((8, GROUP, NYL, NZ), F32)
PAIR = jax.ShapeDtypeStruct((2, GROUP, NYL, NZ), F32)
SCRATCH = [pltpu.VMEM((NX + 2 * PAD, ROWS, NZ), F32), pltpu.VMEM((NX, NYL, NZ), F32)]
PARAMS = pltpu.CompilerParams(vmem_limit_bytes=14 * 1024 * 1024)


def call(kernel, specs, outs, scratch=(), flops=0, moved=0, out_spec=VMEM):
    return pl.pallas_call(
        kernel,
        in_specs=specs,
        out_specs=[out_spec] * len(outs),
        out_shape=outs,
        scratch_shapes=list(scratch),
        compiler_params=PARAMS,
        cost_estimate=pl.CostEstimate(flops=flops, bytes_accessed=moved, transcendentals=0),
    )


def per_device(
    courant_squared,
    wave_now,
    wave_prev,
    adj_late,
    adj_later,
    wavelet,
    sources,
    receivers,
    observed,
    apertures,
):
    me = lax.axis_index("shot")
    part = lax.axis_index("sub")
    half, clas = me // 8, me % 8
    row, core = clas // 2, clas % 2
    starts = apertures[:, 0]
    first = starts[me]
    oper = jnp.asarray(depth_operator())
    up = [(i, (i + 1) % 8) for i in range(8)]
    down = [((i + 1) % 8, i) for i in range(8)]
    across = [(i, (i + 8) % 16) for i in range(16)]
    chip = [(i, i ^ 1) for i in range(16)]
    halves = [list(range(8)), list(range(8, 16))]

    def along(k):
        return [(8 * h + 2 * y + c, 8 * h + 2 * ((y + k) % 4) + c) for h in range(2) for y in range(4) for c in range(2)]

    def edges(lo, hi):
        return lax.ppermute(hi, "sub", up), lax.ppermute(lo, "sub", down)

    piece = courant_squared[:, 0]
    other = lax.ppermute(piece, "shot", across)
    piece_c = lax.ppermute(piece, "shot", chip)
    other_c = lax.ppermute(other, "shot", chip)
    ahead = jnp.arange(4)
    two = jnp.arange(2)
    want = starts[half * 8 + (row + ahead) % 4 * 2 + core][:, None]
    have = (2 * row + two)[None, :]
    chosen = ((want + (have - want) % 8) // 8).reshape(8).astype(jnp.int32)
    here = jnp.stack([half, core]).astype(jnp.int32)
    blocks = call(select_kernel, [SMEM] * 2 + [VMEM] * 4, [PAIR] * 4, moved=2 << 20)(chosen, here, piece, other, piece_c, other_c)
    come = [blocks[0]] + [lax.ppermute(blocks[k], "shot", along(k)) for k in (1, 2, 3)]
    from_class = ((row - ahead) % 4 * 2)[:, None] + two[None, :]
    places = ((from_class - first) % 8).reshape(8).astype(jnp.int32)

    (packed,) = call(
        pack_kernel,
        [ANY] * 4,
        [jax.ShapeDtypeStruct((8, GROUP, TURNED, NZ), F32)],
        [pltpu.VMEM((GROUP, 256, NZ), F32), pltpu.VMEM((8, GROUP, 8, NZ), F32), pltpu.SemaphoreType.DMA((34,))],
        moved=8 << 20,
        out_spec=ANY,
    )(wave_now[0], wave_prev[0], adj_late[0], adj_later[0])
    packed, other = lax.optimization_barrier((packed, other))
    turned = lax.all_to_all(packed, "sub", 0, 0, tiled=True).reshape(NX, TURNED, NZ)
    (r2,) = call(assemble_kernel, [SMEM] + [VMEM] * 4, [BLOCKS], moved=2 << 20)(places, *come)
    r2 = r2.reshape(NX, NYL, NZ)

    cell = sources[0]
    line = (cell // NZ) % 256
    spots = jnp.stack(
        [
            first % 8,
            (line // NYL == part).astype(jnp.int32),
            cell // (256 * NZ),
            line % NYL,
            cell % NZ,
            (part > 0).astype(jnp.int32),
            (part < 7).astype(jnp.int32),
        ]
    )
    cells = receivers[0]
    mine = ((cells // NZ) % 256 // NYL == part).astype(jnp.int32)
    count, *datas = call(receivers_kernel, [SMEM] * 3, [FIELD] * 5, moved=6 << 20)(cells, mine, observed[0])

    r2, count = lax.optimization_barrier((r2, count))

    lap, new, *more = call(
        first_kernel,
        [SMEM, SMEM, ANY, VMEM, VMEM],
        [FIELD, FIELD, EDGE2, EDGE2, FIELD, FIELD, FIELD],
        SCRATCH + [pltpu.VMEM((NX, NYL, NZ), F32), pltpu.VMEM((NX, 8, NZ), F32), pltpu.SemaphoreType.DMA((6,))],
        flops=10 << 20,
        moved=8 << 20,
    )(spots, wavelet[0, 0:1], turned, r2, oper)
    send, (prev, late, later) = more[:2], more[2:]
    laps, fields = [lap], [new]
    now = new
    halo = held = edges(*send)
    for step in range(1, STEPS):
        last = step == STEPS - 1
        args = [spots, wavelet[0, step : step + 1], now, prev, r2, oper, *halo]
        lap, new, *send = call(
            functools.partial(forward_kernel, last),
            [SMEM, SMEM] + [VMEM] * (len(args) - 2),
            [FIELD, FIELD] + ([] if last else [EDGE, EDGE]),
            SCRATCH,
            flops=10 << 20,
            moved=6 << 20,
        )(*args)
        laps.append(lap)
        fields.append(new)
        now, prev = new, now
        if not last:
            halo = edges(*send)

    halo = held
    total = None
    for step in range(STEPS, 0, -1):
        begin, last = step == STEPS, step == 1
        outs = [BLOCKS] if last else [FIELD, FIELD, EDGE, EDGE]
        args = [spots, late, later, r2, *halo, oper, count, datas[step - 1], fields[step - 1], laps[step - 1]]
        if not begin:
            args.append(total)
        total, *more = call(
            functools.partial(adjoint_kernel, begin, last),
            [SMEM] + [VMEM] * (len(args) - 1),
            outs,
            SCRATCH,
            flops=10 << 20,
            moved=8 << 20,
        )(*args)
        if not last:
            late, later = more[0], late
            halo = edges(*more[1:])

    recv = lax.all_to_all(total, "shot", 0, 0, axis_index_groups=halves, tiled=True)
    group = starts[half * 8 + jnp.arange(8)]
    slots = ((group + (clas - group) % 8) // 8).astype(jnp.int32)
    keep, give = call(bins_kernel, [SMEM, SMEM, VMEM], [PAIR, PAIR], moved=2 << 20)(slots, half[None], recv)
    result = keep + lax.ppermute(give, "shot", across)
    return result[:, None]


def solution(mesh):
    in_specs = (
        P(None, "shot", None, "sub", None),
        P("shot", "sub", None, None),
        P("shot", "sub", None, None),
        P("shot", "sub", None, None),
        P("shot", "sub", None, None),
        P("shot", None),
        P("shot"),
        P("shot", None),
        P("shot", None, None),
        P(),
    )
    out_specs = P(None, "shot", None, "sub", None)
    return jax.shard_map(
        per_device, mesh=mesh, in_specs=in_specs, out_specs=out_specs, check_vma=False
    )
```

```python
import functools

import jax
import jax.numpy as jnp
import ml_dtypes
import numpy as np
from jax import lax
from jax.experimental import pallas as pl
from jax.experimental.pallas import tpu as pltpu
from jax.sharding import PartitionSpec as P

STEPS = 4
STENCIL = (-205.0 / 72.0, 8.0 / 5.0, -1.0 / 5.0, 8.0 / 315.0, -1.0 / 560.0)
F32 = jnp.float32
BF16 = jnp.bfloat16
SMEM = pl.BlockSpec(memory_space=pltpu.SMEM)
VMEM = pl.BlockSpec(memory_space=pltpu.VMEM)
ANY = pl.BlockSpec(memory_space=pltpu.HBM)
NX, NYL, NZ = 64, 32, 128
GROUP = 8
PAD = 4
ROWS = 64
OWN0, OWN1 = 16, 48
WIDE0, WIDE1 = 8, 56
WIDE = WIDE1 - WIDE0
OWN_X, OWN_Y = slice(PAD, PAD + NX), slice(OWN0, OWN1)
CHUNK = 16
OWN, WITH_HALO = range(4), range(-1, 5)


def depth_operator():
    band = np.zeros((NZ, NZ), np.float32)
    for i in range(NZ):
        band[i, i] = np.float32(3.0 * STENCIL[0])
        for k in range(1, 5):
            for j in (i - k, i + k):
                if 0 <= j < NZ:
                    band[j, i] = np.float32(STENCIL[k])
    high = band.astype(ml_dtypes.bfloat16)
    low = (band - high.astype(np.float32)).astype(ml_dtypes.bfloat16)
    zero = np.zeros_like(high)
    return np.block([[high, low], [high, zero]])


def clear_ends(ext):
    zeros = jnp.zeros((PAD, ROWS, NZ), F32)
    ext[0:PAD] = zeros
    ext[PAD + NX : 2 * PAD + NX] = zeros


def planes(body):
    def step(x, carry):
        body(x)
        return carry

    lax.fori_loop(0, NX, step, 0, unroll=4)


def fill_edges(ext, spots, halo_lo, halo_hi):
    has_lo, has_hi = spots[5] == 1, spots[6] == 1

    def body(t, carry):
        lo = jnp.where(has_lo, halo_lo[t], 0.0)
        hi = jnp.where(has_hi, halo_hi[t], 0.0)
        for half in range(2):
            x = PAD + 2 * t + half
            ext[x, OWN0 - 4 : OWN0, :] = lo[4 * half : 4 * half + 4]
            ext[x, OWN1 : OWN1 + 4, :] = hi[4 * half : 4 * half + 4]
        return carry

    lax.fori_loop(0, NX // 2, body, 0, unroll=4)


def fill_tiles(ext, spots, lo, hi):
    has_lo, has_hi = spots[5] == 1, spots[6] == 1

    def body(x):
        ext[PAD + x, WIDE0:OWN0, :] = jnp.where(has_lo, lo(x), 0.0)
        ext[PAD + x, OWN1:WIDE1, :] = jnp.where(has_hi, hi(x), 0.0)

    planes(body)


def fill_ring(ext, edge):
    def body(x):
        ext[PAD + x, OWN0 - 4 : OWN0, :] = edge[x, 0:4, :]
        ext[PAD + x, OWN1 : OWN1 + 4, :] = edge[x, 4:8, :]

    planes(body)


def apply_depth(ext, oper, depth, wide=False):
    r0, r1 = (WIDE0, WIDE1) if wide else (OWN0, OWN1)
    n = CHUNK
    for at in range(0, NX, n):
        rows = ext[PAD + at : PAD + at + n, r0:r1, :].reshape(n * (r1 - r0), NZ)
        high = rows.astype(BF16)
        low = (rows - high.astype(F32)).astype(BF16)
        prod = jnp.dot(jnp.concatenate([high, low], axis=1), oper[...], preferred_element_type=F32)
        depth[at : at + n, r0 - WIDE0 : r1 - WIDE0, :] = (prod[:, :NZ] + prod[:, NZ:]).reshape(n, r1 - r0, NZ)


def laplace(ext, depth, tiles, emit):
    def body(g, carry):
        base = PAD + g * GROUP
        for j in tiles:
            r0 = OWN0 + 8 * j
            col = [ext[base - PAD + i, r0 : r0 + 8, :] for i in range(GROUP + 2 * PAD)]
            for xi in range(GROUP):
                acc = depth[g * GROUP + xi, r0 - WIDE0 : r0 - WIDE0 + 8, :]
                for k in range(1, 5):
                    beside = (
                        col[xi + PAD + k]
                        + col[xi + PAD - k]
                        + (
                            ext[base + xi, r0 + k : r0 + k + 8, :]
                            + ext[base + xi, r0 - k : r0 - k + 8, :]
                        )
                    )
                    acc = acc + STENCIL[k] * beside
                emit(g * GROUP + xi, g, xi, j, acc)
        return carry

    lax.fori_loop(0, NX // GROUP, body, 0)


def tile(j):
    return slice(8 * j, 8 * j + 8)


def ext_tile(j):
    return slice(OWN0 + 8 * j, OWN0 + 8 * j + 8)


def send_rows(send_lo, send_hi, read):
    def body(t, carry):
        for half in range(2):
            send_lo[t, 4 * half : 4 * half + 4, :] = read(2 * t + half, slice(0, 4))
            send_hi[t, 4 * half : 4 * half + 4, :] = read(2 * t + half, slice(NYL - 4, NYL))
        return carry

    lax.fori_loop(0, NX // 2, body, 0, unroll=4)


def send_tiles(send_lo, send_hi, field):
    def body(x):
        send_lo[x] = field[x, 0:8, :]
        send_hi[x] = field[x, NYL - 8 : NYL, :]

    planes(body)


def add_source(spots, amount, ref, x0, y0, wide=False):
    @pl.when(spots[7 if wide else 1] == 1)
    def _():
        x, y, z = x0 + spots[2], y0 + spots[3], spots[4]
        lanes = lax.broadcasted_iota(jnp.int32, (1, NZ), 1)
        row = ref[x, pl.ds(y, 1), :]
        ref[x, pl.ds(y, 1), :] = row + jnp.where(lanes == z, amount, 0.0)


NOW, PREV, EDGES, TURNED = 0, 32, 64, 72


def unpack(turned, sems, now, edge, prev, extra):
    copies = []
    for n, (off, rows, dst) in enumerate(
        ((NOW, NYL, now), (EDGES, 8, edge), (PREV, NYL, prev), (NOW, NYL, extra))
    ):
        copies.append(pltpu.make_async_copy(turned.at[:, off : off + rows, :], dst, sems.at[n]))
    for c in copies:
        c.start()
    return copies


def first_kernel(spots, wavelet, turned, r2, oper, lap, new, send_lo, send_hi, now, edge, ext, depth, prev, sems):
    copies = unpack(turned, sems, ext.at[OWN_X, OWN_Y, :], edge, prev, now)
    clear_ends(ext)
    for c in copies[:3]:
        c.wait()
    fill_ring(ext, edge)
    apply_depth(ext, oper, depth)

    def emit(x, g, xi, j, value):
        lap[x, tile(j), :] = value
        new[x, tile(j), :] = 2.0 * ext[PAD + x, ext_tile(j), :] - prev[x, tile(j), :] + r2[x, tile(j), :] * value

    laplace(ext, depth, OWN, emit)
    add_source(spots, wavelet[0], new, 0, 0)
    send_tiles(send_lo, send_hi, new)
    copies[3].wait()


def spread_edges(edge, lo, hi):
    def body(x):
        lo[x, 4:8, :] = edge[x, 0:4, :]
        hi[x, 0:4, :] = edge[x, 4:8, :]

    planes(body)


def spread_halos(halo_lo, halo_hi, lo, hi):
    def body(t, carry):
        for half in range(2):
            lo[2 * t + half, 4:8, :] = halo_lo[t, 4 * half : 4 * half + 4, :]
            hi[2 * t + half, 0:4, :] = halo_hi[t, 4 * half : 4 * half + 4, :]
        return carry

    lax.fori_loop(0, NX // 2, body, 0, unroll=4)


def middle_kernel(
    spots, wavelet, now, now_lo, now_hi, prev, edge, r2, r2_lo, r2_hi, oper,
    lap_a, new_a, lap_b, new_b, send_lo, send_hi, ext, ext2, depth, old_lo, old_hi,
):
    has = (spots[5] == 1, spots[6] == 1)
    clear_ends(ext)
    clear_ends(ext2)
    ext[OWN_X, OWN_Y, :] = now[...]
    fill_tiles(ext, spots, lambda x: now_lo[x], lambda x: now_hi[x])
    spread_edges(edge, old_lo, old_hi)
    apply_depth(ext, oper, depth, True)

    def emit(x, g, xi, j, value):
        twice = 2.0 * ext[PAD + x, ext_tile(j), :]
        if j in OWN:
            u = twice - prev[x, tile(j), :] + r2[x, tile(j), :] * value
            lap_a[x, tile(j), :] = value
            new_a[x, tile(j), :] = u
        else:
            old, weight, there = (old_lo, r2_lo, has[0]) if j < 0 else (old_hi, r2_hi, has[1])
            u = jnp.where(there, twice - old[x] + weight[x] * value, 0.0)
        ext2[PAD + x, ext_tile(j), :] = u

    laplace(ext, depth, WITH_HALO, emit)
    add_source(spots, wavelet[1], new_a, 0, 0)
    add_source(spots, wavelet[1], ext2, PAD, OWN0, True)
    apply_depth(ext2, oper, depth)

    def emit_b(x, g, xi, j, value):
        lap_b[x, tile(j), :] = value
        new_b[x, tile(j), :] = 2.0 * ext2[PAD + x, ext_tile(j), :] - now[x, tile(j), :] + r2[x, tile(j), :] * value

    laplace(ext2, depth, OWN, emit_b)
    add_source(spots, wavelet[2], new_b, 0, 0)
    send_rows(send_lo, send_hi, lambda x, rows: new_b[x, rows, :])


def late_kernel(spots, turned, r2, r2_lo, r2_hi, oper, mu, late, edge, ext, depth, later, sems):
    copies = unpack(turned, sems, late, edge, later, ext.at[OWN_X, OWN_Y, :])
    clear_ends(ext)
    for c in copies:
        c.wait()

    def weigh(x):
        ext[PAD + x, OWN_Y, :] = late[x] * r2[x]
        ext[PAD + x, OWN0 - 4 : OWN0, :] = edge[x, 0:4, :] * r2_lo[x, 4:8, :]
        ext[PAD + x, OWN1 : OWN1 + 4, :] = edge[x, 4:8, :] * r2_hi[x, 0:4, :]

    planes(weigh)
    apply_depth(ext, oper, depth)

    def emit(x, g, xi, j, value):
        mu[x, tile(j), :] = 2.0 * late[x, tile(j), :] + value - later[x, tile(j), :]

    laplace(ext, depth, OWN, emit)


def turn_kernel(
    spots, wavelet, now, halo_lo, halo_hi, prev, r2, oper, part, count, data, total, mu, send_lo, send_hi, ext, depth, new
):
    clear_ends(ext)
    ext[OWN_X, OWN_Y, :] = now[...]
    fill_edges(ext, spots, halo_lo, halo_hi)
    apply_depth(ext, oper, depth)

    def emit(x, g, xi, j, value):
        new[x, tile(j), :] = 2.0 * ext[PAD + x, ext_tile(j), :] - prev[x, tile(j), :] + r2[x, tile(j), :] * value
        total[x, tile(j), :] = value

    laplace(ext, depth, OWN, emit)
    add_source(spots, wavelet[3], new, 0, 0)

    def finish(x):
        m = part[x] + (count[x, 8 : 8 + NYL, :] * new[x] - data[x])
        mu[x] = m
        total[x] = m * total[x]

    planes(finish)
    send_tiles(send_lo, send_hi, mu)


def back_kernel(
    spots, late, late_lo, late_hi, later, edge, r2, r2_lo, r2_hi, oper, count, data_a, data_b,
    wave_a, wave_lo, wave_hi, wave_b, lap_a, lap_b, total_in,
    total, mu_a, mu_b, send_lo, send_hi, ext, ext2, depth, old_lo, old_hi, u_lo, u_hi,
):
    has = (spots[5] == 1, spots[6] == 1)
    clear_ends(ext)
    clear_ends(ext2)
    ext[OWN_X, OWN_Y, :] = late[...] * r2[...]
    fill_tiles(ext, spots, lambda x: late_lo[x] * r2_lo[x], lambda x: late_hi[x] * r2_hi[x])
    spread_edges(edge, old_lo, old_hi)
    spread_halos(wave_lo, wave_hi, u_lo, u_hi)
    apply_depth(ext, oper, depth, True)

    def emit(x, g, xi, j, value):
        wide = slice(8 + 8 * j, 16 + 8 * j)
        many, heard = count[x, wide, :], data_a[x, wide, :]
        if j in OWN:
            mu = 2.0 * late[x, tile(j), :] + value - later[x, tile(j), :]
            mu = mu + (many * wave_a[x, tile(j), :] - heard)
            mu_a[x, tile(j), :] = mu
            total[x, tile(j), :] = total_in[x, tile(j), :] + mu * lap_a[x, tile(j), :]
            w = mu * r2[x, tile(j), :]
        else:
            near, old, u, weight, there = (
                (late_lo, old_lo, u_lo, r2_lo, has[0]) if j < 0 else (late_hi, old_hi, u_hi, r2_hi, has[1])
            )
            mu = 2.0 * near[x] + value - old[x] + (many * u[x] - heard)
            w = jnp.where(there, mu * weight[x], 0.0)
        ext2[PAD + x, ext_tile(j), :] = w

    laplace(ext, depth, WITH_HALO, emit)
    apply_depth(ext2, oper, depth)

    def emit_b(x, g, xi, j, value):
        mu = 2.0 * mu_a[x, tile(j), :] + value - late[x, tile(j), :]
        mu = mu + (count[x, 8 + 8 * j : 16 + 8 * j, :] * wave_b[x, tile(j), :] - data_b[x, tile(j), :])
        mu_b[x, tile(j), :] = mu
        total[x, tile(j), :] = total[x, tile(j), :] + mu * lap_b[x, tile(j), :]

    laplace(ext2, depth, OWN, emit_b)
    send_rows(send_lo, send_hi, lambda x, rows: mu_b[x, rows, :] * r2[x, rows, :])


def last_kernel(
    spots, late, later, r2, halo_lo, halo_hi, oper, count, data, wave, lap, total_in, total, ext, depth
):
    first = spots[0]
    clear_ends(ext)
    ext[OWN_X, OWN_Y, :] = late[...] * r2[...]
    fill_edges(ext, spots, halo_lo, halo_hi)
    apply_depth(ext, oper, depth)

    def emit(x, g, xi, j, value):
        mu = 2.0 * late[x, tile(j), :] + value - later[x, tile(j), :]
        mu = mu + (count[x, 8 + 8 * j : 16 + 8 * j, :] * wave[x, tile(j), :] - data[x, tile(j), :])
        total[lax.rem(first + g, GROUP), xi, tile(j), :] = total_in[x, tile(j), :] + mu * lap[x, tile(j), :]

    laplace(ext, depth, OWN, emit)


def pack_kernel(now, prev, out, near, edge, sems):
    bring = pltpu.make_async_copy(now, near, sems.at[16])
    bring.start()
    copies = []
    for p in range(8):
        for f, (off, field) in enumerate(((NOW, now), (PREV, prev))):
            copies.append(
                pltpu.make_async_copy(
                    field.at[:, NYL * p : NYL * p + NYL, :], out.at[p, :, off : off + NYL, :], sems.at[2 * p + f]
                )
            )
    for c in copies:
        c.start()
    none = jnp.zeros((4, NZ), F32)
    bring.wait()

    def body(xi, carry):
        for p in range(8):
            lo = NYL * p
            edge[p, xi, 0:4, :] = near[xi, lo - 4 : lo, :] if p > 0 else none
            edge[p, xi, 4:8, :] = near[xi, lo + NYL : lo + NYL + 4, :] if p < 7 else none
        return carry

    lax.fori_loop(0, GROUP, body, 0)
    ends = pltpu.make_async_copy(edge, out.at[:, :, EDGES : EDGES + 8, :], sems.at[17])
    ends.start()
    for c in copies:
        c.wait()
    ends.wait()


def copy_block(dst, src):
    def body(x, carry):
        dst[x] = src[x]
        return carry

    lax.fori_loop(0, GROUP, body, 0, unroll=4)


def split_shot(me):
    return me // 8, lax.rem(me // 2, 4), lax.rem(me, 2)


def slot_of(start, which):
    return (start + lax.rem(which - start + 32, 8)) // 8


def select_kernel(ids, apertures, piece, other, piece_c, other_c, *outs):
    half, y, core = split_shot(ids[0])
    for k in range(4):
        start = apertures[8 * half + 2 * lax.rem(y + k, 4) + core, 0]
        for j in range(2):
            m = slot_of(start, 2 * y + j)
            row = m // 2
            own_half = lax.rem(m, 2) == half
            own_core = core == j
            for src, same_half, same_core in (
                (piece, True, True),
                (other, False, True),
                (piece_c, True, False),
                (other_c, False, False),
            ):

                @pl.when(jnp.logical_and(own_half == same_half, own_core == same_core))
                def _():
                    copy_block(outs[k].at[j], src.at[row])


def assemble_kernel(ids, apertures, r0, r1, r2, r3, out, send_lo, send_hi):
    _, y, _ = split_shot(ids[0])
    first = apertures[ids[0], 0]
    for k, src in enumerate((r0, r1, r2, r3)):
        for j in range(2):
            at = lax.rem(2 * lax.rem(y - k + 4, 4) + j - first + 32, 8)
            copy_block(out.at[pl.ds(at * GROUP, GROUP)], src.at[j])
    send_tiles(send_lo, send_hi, out)


def receivers_kernel(cells, lines, observed, count, data3, data1, data2, data4):
    zeros = jnp.zeros((NYL, NZ), F32)
    zeros_wide = jnp.zeros((WIDE, NZ), F32)

    def clear(x):
        for d in (count, data3):
            d[x] = zeros_wide
        for d in (data1, data2, data4):
            d[x] = zeros

    planes(clear)
    lanes = lax.broadcasted_iota(jnp.int32, (1, NZ), 1)

    def body(r, carry):
        y = lines[r]

        @pl.when(jnp.logical_and(y >= -8, y < NYL + 8))
        def _():
            cell = cells[r]
            x = cell // (256 * NZ)
            hit = lanes == lax.rem(cell, NZ)
            row = pl.ds(y + 8, 1)
            count[x, row, :] = count[x, row, :] + jnp.where(hit, 1.0, 0.0)
            data3[x, row, :] = data3[x, row, :] + jnp.where(hit, observed[2, r], 0.0)

            @pl.when(jnp.logical_and(y >= 0, y < NYL))
            def _():
                own = pl.ds(y, 1)
                for n, d in ((0, data1), (1, data2), (3, data4)):
                    d[x, own, :] = d[x, own, :] + jnp.where(hit, observed[n, r], 0.0)

        return carry

    lax.fori_loop(0, cells.shape[0], body, 0)


def bins_kernel(ids, apertures, recv, keep, give):
    mine, which = ids[0] // 8, lax.rem(ids[0], 8)
    zeros = jnp.zeros((GROUP, NYL, NZ), F32)
    for i in range(2):
        keep[i] = zeros
        give[i] = zeros
    for t in range(GROUP):
        m = slot_of(apertures[8 * mine + t, 0], which)
        i = m // 2

        @pl.when(lax.rem(m, 2) == mine)
        def _():
            keep[i] = keep[i] + recv[t]

        @pl.when(lax.rem(m, 2) != mine)
        def _():
            give[i] = give[i] + recv[t]


FIELD = jax.ShapeDtypeStruct((NX, NYL, NZ), F32)
WIDE_FIELD = jax.ShapeDtypeStruct((NX, WIDE, NZ), F32)
EDGE = jax.ShapeDtypeStruct((NX // 2, 8, NZ), F32)
TILE = jax.ShapeDtypeStruct((NX, 8, NZ), F32)
BLOCKS = jax.ShapeDtypeStruct((8, GROUP, NYL, NZ), F32)
PAIR = jax.ShapeDtypeStruct((2, GROUP, NYL, NZ), F32)
EXT = pltpu.VMEM((NX + 2 * PAD, ROWS, NZ), F32)
DEPTH = pltpu.VMEM((NX, WIDE, NZ), F32)
FIELD_VMEM = pltpu.VMEM((NX, NYL, NZ), F32)
TILE_VMEM = pltpu.VMEM((NX, 8, NZ), F32)
PARAMS = pltpu.CompilerParams(vmem_limit_bytes=12 * 1024 * 1024)


def call(kernel, specs, outs, scratch=(), flops=0, moved=0, out_spec=VMEM):
    return pl.pallas_call(
        kernel,
        in_specs=specs,
        out_specs=[out_spec] * len(outs),
        out_shape=outs,
        scratch_shapes=list(scratch),
        compiler_params=PARAMS,
        cost_estimate=pl.CostEstimate(flops=flops, bytes_accessed=moved, transcendentals=0),
    )


def per_device(
    courant_squared,
    wave_now,
    wave_prev,
    adj_late,
    adj_later,
    wavelet,
    sources,
    receivers,
    observed,
    apertures,
):
    me = lax.axis_index("shot")
    part = lax.axis_index("sub")
    ids = jnp.stack([me, part]).astype(jnp.int32)
    first = apertures[me, 0]
    oper = jnp.asarray(depth_operator())
    up = [(i, (i + 1) % 8) for i in range(8)]
    down = [((i + 1) % 8, i) for i in range(8)]
    across = [(i, (i + 8) % 16) for i in range(16)]
    chip = [(i, i ^ 1) for i in range(16)]
    halves = [list(range(8)), list(range(8, 16))]

    def along(k):
        return [(8 * h + 2 * y + c, 8 * h + 2 * ((y + k) % 4) + c) for h in range(2) for y in range(4) for c in range(2)]

    def edges(lo, hi):
        return lax.ppermute(hi, "sub", up), lax.ppermute(lo, "sub", down)

    piece = courant_squared[:, 0]
    other = lax.ppermute(piece, "shot", across)
    piece_c = lax.ppermute(piece, "shot", chip)
    other_c = lax.ppermute(other, "shot", chip)
    blocks = call(select_kernel, [SMEM] * 2 + [VMEM] * 4, [PAIR] * 4, moved=2 << 20)(
        ids, apertures, piece, other, piece_c, other_c
    )
    come = [blocks[0]] + [lax.ppermute(blocks[k], "shot", along(k)) for k in (1, 2, 3)]

    def turn(a, b):
        (packed,) = call(
            pack_kernel,
            [ANY] * 2,
            [jax.ShapeDtypeStruct((8, GROUP, TURNED, NZ), F32)],
            [pltpu.VMEM((GROUP, 256, NZ), F32), pltpu.VMEM((8, GROUP, 8, NZ), F32), pltpu.SemaphoreType.DMA((18,))],
            moved=5 << 20,
            out_spec=ANY,
        )(a, b)
        return packed

    def exchange(packed):
        return lax.all_to_all(packed, "sub", 0, 0, tiled=True).reshape(NX, TURNED, NZ)

    packed, other = lax.optimization_barrier((turn(wave_now[0], wave_prev[0]), other))
    waves = exchange(packed)
    r2, *r2_send = call(assemble_kernel, [SMEM] * 2 + [VMEM] * 4, [FIELD, TILE, TILE], moved=2 << 20)(
        ids, apertures, *come
    )
    r2_halo = edges(*r2_send)

    cell = sources[0]
    line = (cell // NZ) % 256 - NYL * part
    spots = jnp.stack(
        [
            first % 8,
            ((line >= 0) & (line < NYL)).astype(jnp.int32),
            cell // (256 * NZ),
            line,
            cell % NZ,
            (part > 0).astype(jnp.int32),
            (part < 7).astype(jnp.int32),
            ((line >= -8) & (line < NYL + 8)).astype(jnp.int32),
        ]
    )
    amounts = wavelet[0]
    cells = receivers[0]
    lines = (cells // NZ) % 256 - NYL * part

    lap0, u1, lo, hi, u0, u0_edge = call(
        first_kernel,
        [SMEM, SMEM, ANY, VMEM, VMEM],
        [FIELD, FIELD, TILE, TILE, FIELD, TILE],
        [EXT, DEPTH, FIELD_VMEM, pltpu.SemaphoreType.DMA((4,))],
        flops=10 << 20,
        moved=8 << 20,
    )(spots, amounts, waves, r2, oper)
    u1_halo = edges(lo, hi)
    adjs = exchange(turn(adj_late[0], adj_later[0]))
    count, data3, data1, data2, data4 = call(
        receivers_kernel, [SMEM] * 3, [WIDE_FIELD, WIDE_FIELD] + [FIELD] * 3, moved=6 << 20
    )(cells, lines, observed[0])
    lap1, u2, lap2, u3, lo, hi = call(
        middle_kernel,
        [SMEM, SMEM] + [VMEM] * 9,
        [FIELD] * 4 + [EDGE] * 2,
        [EXT, EXT, DEPTH, TILE_VMEM, TILE_VMEM],
        flops=20 << 20,
        moved=12 << 20,
    )(spots, amounts, u1, *u1_halo, u0, u0_edge, r2, *r2_halo, oper)
    u3_halo = edges(lo, hi)
    part4, mu5, mu5_edge = call(
        late_kernel,
        [SMEM, ANY] + [VMEM] * 4,
        [FIELD, FIELD, TILE],
        [EXT, DEPTH, FIELD_VMEM, pltpu.SemaphoreType.DMA((4,))],
        flops=10 << 20,
        moved=6 << 20,
    )(spots, adjs, r2, *r2_halo, oper)

    total, mu4, lo, hi = call(
        turn_kernel,
        [SMEM, SMEM] + [VMEM] * 9,
        [FIELD, FIELD, TILE, TILE],
        [EXT, DEPTH, FIELD_VMEM],
        flops=10 << 20,
        moved=8 << 20,
    )(spots, amounts, u3, *u3_halo, u2, r2, oper, part4, count, data4)
    mu4_halo = edges(lo, hi)
    total, mu3, mu2, lo, hi = call(
        back_kernel,
        [SMEM] + [VMEM] * 19,
        [FIELD] * 3 + [EDGE] * 2,
        [EXT, EXT, DEPTH] + [TILE_VMEM] * 4,
        flops=20 << 20,
        moved=16 << 20,
    )(
        spots, mu4, *mu4_halo, mu5, mu5_edge, r2, *r2_halo, oper, count, data3, data2,
        u3, *u3_halo, u2, lap2, lap1, total,
    )
    mu2_halo = edges(lo, hi)
    (total,) = call(last_kernel, [SMEM] + [VMEM] * 11, [BLOCKS], [EXT, DEPTH], flops=10 << 20, moved=8 << 20)(
        spots, mu2, mu3, r2, *mu2_halo, oper, count, data1, u1, lap0, total
    )

    recv = lax.all_to_all(total, "shot", 0, 0, axis_index_groups=halves, tiled=True)
    keep, give = call(bins_kernel, [SMEM, SMEM, VMEM], [PAIR, PAIR], moved=2 << 20)(ids, apertures, recv)
    result = keep + lax.ppermute(give, "shot", across)
    return result[:, None]


def solution(mesh):
    in_specs = (
        P(None, "shot", None, "sub", None),
        P("shot", "sub", None, None),
        P("shot", "sub", None, None),
        P("shot", "sub", None, None),
        P("shot", "sub", None, None),
        P("shot", None),
        P("shot"),
        P("shot", None),
        P("shot", None, None),
        P(),
    )
    out_specs = P(None, "shot", None, "sub", None)
    return jax.shard_map(
        per_device, mesh=mesh, in_specs=in_specs, out_specs=out_specs, check_vma=False
    )
```

```python
import functools

import jax
import jax.numpy as jnp
import ml_dtypes
import numpy as np
from jax import lax
from jax.experimental import pallas as pl
from jax.experimental.pallas import tpu as pltpu
from jax.sharding import PartitionSpec as P

STEPS = 4
STENCIL = (-205.0 / 72.0, 8.0 / 5.0, -1.0 / 5.0, 8.0 / 315.0, -1.0 / 560.0)
F32 = jnp.float32
BF16 = jnp.bfloat16
SMEM = pl.BlockSpec(memory_space=pltpu.SMEM)
VMEM = pl.BlockSpec(memory_space=pltpu.VMEM)
ANY = pl.BlockSpec(memory_space=pltpu.HBM)
NX, NYL, NZ = 64, 32, 128
GROUP = 8
PAD = 4
ROWS = 64
OWN0, OWN1 = 16, 48
WIDE0, WIDE1 = 8, 56
WIDE = WIDE1 - WIDE0
OWN_X, OWN_Y = slice(PAD, PAD + NX), slice(OWN0, OWN1)
CHUNK = 16
OWN, WITH_HALO = range(4), range(-1, 5)


def depth_operator():
    band = np.zeros((NZ, NZ), np.float32)
    for i in range(NZ):
        band[i, i] = np.float32(3.0 * STENCIL[0])
        for k in range(1, 5):
            for j in (i - k, i + k):
                if 0 <= j < NZ:
                    band[j, i] = np.float32(STENCIL[k])
    high = band.astype(ml_dtypes.bfloat16)
    low = (band - high.astype(np.float32)).astype(ml_dtypes.bfloat16)
    zero = np.zeros_like(high)
    return np.block([[high, low], [high, zero]])


def clear_ends(ext):
    zeros = jnp.zeros((PAD, ROWS, NZ), F32)
    ext[0:PAD] = zeros
    ext[PAD + NX : 2 * PAD + NX] = zeros


def planes(body):
    def step(x, carry):
        body(x)
        return carry

    lax.fori_loop(0, NX, step, 0, unroll=4)


def fill_edges(ext, spots, halo_lo, halo_hi):
    has_lo, has_hi = spots[5] == 1, spots[6] == 1

    def body(t, carry):
        lo = jnp.where(has_lo, halo_lo[t], 0.0)
        hi = jnp.where(has_hi, halo_hi[t], 0.0)
        for half in range(2):
            x = PAD + 2 * t + half
            ext[x, OWN0 - 4 : OWN0, :] = lo[4 * half : 4 * half + 4]
            ext[x, OWN1 : OWN1 + 4, :] = hi[4 * half : 4 * half + 4]
        return carry

    lax.fori_loop(0, NX // 2, body, 0, unroll=4)


def fill_tiles(ext, spots, lo, hi):
    has_lo, has_hi = spots[5] == 1, spots[6] == 1

    def body(x):
        ext[PAD + x, WIDE0:OWN0, :] = jnp.where(has_lo, lo(x), 0.0)
        ext[PAD + x, OWN1:WIDE1, :] = jnp.where(has_hi, hi(x), 0.0)

    planes(body)


def fill_ring(ext, edge):
    def body(x):
        ext[PAD + x, OWN0 - 4 : OWN0, :] = edge[x, 0:4, :]
        ext[PAD + x, OWN1 : OWN1 + 4, :] = edge[x, 4:8, :]

    planes(body)


def apply_depth(ext, oper, depth, wide=False):
    r0, r1 = (WIDE0, WIDE1) if wide else (OWN0, OWN1)
    n = CHUNK
    for at in range(0, NX, n):
        rows = ext[PAD + at : PAD + at + n, r0:r1, :].reshape(n * (r1 - r0), NZ)
        high = rows.astype(BF16)
        low = (rows - high.astype(F32)).astype(BF16)
        prod = jnp.dot(jnp.concatenate([high, low], axis=1), oper[...], preferred_element_type=F32)
        depth[at : at + n, r0 - WIDE0 : r1 - WIDE0, :] = (prod[:, :NZ] + prod[:, NZ:]).reshape(n, r1 - r0, NZ)


def laplace(ext, depth, tiles, emit):
    def body(g, carry):
        base = PAD + g * GROUP
        for j in tiles:
            r0 = OWN0 + 8 * j
            col = [ext[base - PAD + i, r0 : r0 + 8, :] for i in range(GROUP + 2 * PAD)]
            for xi in range(GROUP):
                acc = depth[g * GROUP + xi, r0 - WIDE0 : r0 - WIDE0 + 8, :]
                for k in range(1, 5):
                    beside = (
                        col[xi + PAD + k]
                        + col[xi + PAD - k]
                        + (
                            ext[base + xi, r0 + k : r0 + k + 8, :]
                            + ext[base + xi, r0 - k : r0 - k + 8, :]
                        )
                    )
                    acc = acc + STENCIL[k] * beside
                emit(g * GROUP + xi, g, xi, j, acc)
        return carry

    lax.fori_loop(0, NX // GROUP, body, 0)


def tile(j):
    return slice(8 * j, 8 * j + 8)


def ext_tile(j):
    return slice(OWN0 + 8 * j, OWN0 + 8 * j + 8)


def send_rows(send_lo, send_hi, read):
    def body(t, carry):
        for half in range(2):
            send_lo[t, 4 * half : 4 * half + 4, :] = read(2 * t + half, slice(0, 4))
            send_hi[t, 4 * half : 4 * half + 4, :] = read(2 * t + half, slice(NYL - 4, NYL))
        return carry

    lax.fori_loop(0, NX // 2, body, 0, unroll=4)


def send_tiles(send_lo, send_hi, field):
    def body(x):
        send_lo[x] = field[x, 0:8, :]
        send_hi[x] = field[x, NYL - 8 : NYL, :]

    planes(body)


def add_source(spots, amount, ref, x0, y0, wide=False):
    @pl.when(spots[7 if wide else 1] == 1)
    def _():
        x, y, z = x0 + spots[2], y0 + spots[3], spots[4]
        lanes = lax.broadcasted_iota(jnp.int32, (1, NZ), 1)
        row = ref[x, pl.ds(y, 1), :]
        ref[x, pl.ds(y, 1), :] = row + jnp.where(lanes == z, amount, 0.0)


NOW, PREV, EDGES, HALF, TURNED = 0, 32, 64, 72, 144


def unpack(turned, base, sems, now, edge, prev, extra):
    copies = []
    for n, (off, rows, dst) in enumerate(
        ((NOW, NYL, now), (EDGES, 8, edge), (PREV, NYL, prev), (NOW, NYL, extra))
    ):
        copies.append(pltpu.make_async_copy(turned.at[:, base + off : base + off + rows, :], dst, sems.at[n]))
    for c in copies:
        c.start()
    return copies


def first_kernel(spots, wavelet, turned, r2, oper, lap, new, send_lo, send_hi, now, edge, ext, depth, prev, sems):
    copies = unpack(turned, 0, sems, ext.at[OWN_X, OWN_Y, :], edge, prev, now)
    clear_ends(ext)
    for c in copies[:3]:
        c.wait()
    fill_ring(ext, edge)
    apply_depth(ext, oper, depth)

    def emit(x, g, xi, j, value):
        lap[x, tile(j), :] = value
        new[x, tile(j), :] = 2.0 * ext[PAD + x, ext_tile(j), :] - prev[x, tile(j), :] + r2[x, tile(j), :] * value

    laplace(ext, depth, OWN, emit)
    add_source(spots, wavelet[0], new, 0, 0)
    send_tiles(send_lo, send_hi, new)
    copies[3].wait()


def spread_edges(edge, lo, hi):
    def body(x):
        lo[x, 4:8, :] = edge[x, 0:4, :]
        hi[x, 0:4, :] = edge[x, 4:8, :]

    planes(body)


def spread_halos(halo_lo, halo_hi, lo, hi):
    def body(t, carry):
        for half in range(2):
            lo[2 * t + half, 4:8, :] = halo_lo[t, 4 * half : 4 * half + 4, :]
            hi[2 * t + half, 0:4, :] = halo_hi[t, 4 * half : 4 * half + 4, :]
        return carry

    lax.fori_loop(0, NX // 2, body, 0, unroll=4)


def middle_kernel(
    spots, wavelet, now, now_lo, now_hi, prev, edge, r2, r2_lo, r2_hi, oper,
    lap_a, new_a, lap_b, new_b, send_lo, send_hi, ext, ext2, depth, old_lo, old_hi,
):
    has = (spots[5] == 1, spots[6] == 1)
    clear_ends(ext)
    clear_ends(ext2)
    ext[OWN_X, OWN_Y, :] = now[...]
    fill_tiles(ext, spots, lambda x: now_lo[x], lambda x: now_hi[x])
    spread_edges(edge, old_lo, old_hi)
    apply_depth(ext, oper, depth, True)

    def emit(x, g, xi, j, value):
        twice = 2.0 * ext[PAD + x, ext_tile(j), :]
        if j in OWN:
            u = twice - prev[x, tile(j), :] + r2[x, tile(j), :] * value
            lap_a[x, tile(j), :] = value
            new_a[x, tile(j), :] = u
        else:
            old, weight, there = (old_lo, r2_lo, has[0]) if j < 0 else (old_hi, r2_hi, has[1])
            u = jnp.where(there, twice - old[x] + weight[x] * value, 0.0)
        ext2[PAD + x, ext_tile(j), :] = u

    laplace(ext, depth, WITH_HALO, emit)
    add_source(spots, wavelet[1], new_a, 0, 0)
    add_source(spots, wavelet[1], ext2, PAD, OWN0, True)
    apply_depth(ext2, oper, depth)

    def emit_b(x, g, xi, j, value):
        lap_b[x, tile(j), :] = value
        new_b[x, tile(j), :] = 2.0 * ext2[PAD + x, ext_tile(j), :] - now[x, tile(j), :] + r2[x, tile(j), :] * value

    laplace(ext2, depth, OWN, emit_b)
    add_source(spots, wavelet[2], new_b, 0, 0)
    send_rows(send_lo, send_hi, lambda x, rows: new_b[x, rows, :])


def late_kernel(spots, turned, r2, r2_lo, r2_hi, oper, mu, late, edge, ext, depth, later, sems):
    copies = unpack(turned, HALF, sems, late, edge, later, ext.at[OWN_X, OWN_Y, :])
    clear_ends(ext)
    for c in copies:
        c.wait()

    def weigh(x):
        ext[PAD + x, OWN_Y, :] = late[x] * r2[x]
        ext[PAD + x, OWN0 - 4 : OWN0, :] = edge[x, 0:4, :] * r2_lo[x, 4:8, :]
        ext[PAD + x, OWN1 : OWN1 + 4, :] = edge[x, 4:8, :] * r2_hi[x, 0:4, :]

    planes(weigh)
    apply_depth(ext, oper, depth)

    def emit(x, g, xi, j, value):
        mu[x, tile(j), :] = 2.0 * late[x, tile(j), :] + value - later[x, tile(j), :]

    laplace(ext, depth, OWN, emit)


def turn_kernel(
    spots, wavelet, now, halo_lo, halo_hi, prev, r2, oper, part, count, data, total, mu, send_lo, send_hi, ext, depth, new
):
    clear_ends(ext)
    ext[OWN_X, OWN_Y, :] = now[...]
    fill_edges(ext, spots, halo_lo, halo_hi)
    apply_depth(ext, oper, depth)

    def emit(x, g, xi, j, value):
        new[x, tile(j), :] = 2.0 * ext[PAD + x, ext_tile(j), :] - prev[x, tile(j), :] + r2[x, tile(j), :] * value
        total[x, tile(j), :] = value

    laplace(ext, depth, OWN, emit)
    add_source(spots, wavelet[3], new, 0, 0)

    def finish(x):
        m = part[x] + (count[x, 8 : 8 + NYL, :] * new[x] - data[x])
        mu[x] = m
        total[x] = m * total[x]

    planes(finish)
    send_tiles(send_lo, send_hi, mu)


def back_kernel(
    spots, late, late_lo, late_hi, later, edge, r2, r2_lo, r2_hi, oper, count, data_a, data_b,
    wave_a, wave_lo, wave_hi, wave_b, lap_a, lap_b, total_in,
    total, mu_a, mu_b, send_lo, send_hi, ext, ext2, depth, old_lo, old_hi, u_lo, u_hi,
):
    has = (spots[5] == 1, spots[6] == 1)
    clear_ends(ext)
    clear_ends(ext2)
    ext[OWN_X, OWN_Y, :] = late[...] * r2[...]
    fill_tiles(ext, spots, lambda x: late_lo[x] * r2_lo[x], lambda x: late_hi[x] * r2_hi[x])
    spread_edges(edge, old_lo, old_hi)
    spread_halos(wave_lo, wave_hi, u_lo, u_hi)
    apply_depth(ext, oper, depth, True)

    def emit(x, g, xi, j, value):
        wide = slice(8 + 8 * j, 16 + 8 * j)
        many, heard = count[x, wide, :], data_a[x, wide, :]
        if j in OWN:
            mu = 2.0 * late[x, tile(j), :] + value - later[x, tile(j), :]
            mu = mu + (many * wave_a[x, tile(j), :] - heard)
            mu_a[x, tile(j), :] = mu
            total[x, tile(j), :] = total_in[x, tile(j), :] + mu * lap_a[x, tile(j), :]
            w = mu * r2[x, tile(j), :]
        else:
            near, old, u, weight, there = (
                (late_lo, old_lo, u_lo, r2_lo, has[0]) if j < 0 else (late_hi, old_hi, u_hi, r2_hi, has[1])
            )
            mu = 2.0 * near[x] + value - old[x] + (many * u[x] - heard)
            w = jnp.where(there, mu * weight[x], 0.0)
        ext2[PAD + x, ext_tile(j), :] = w

    laplace(ext, depth, WITH_HALO, emit)
    apply_depth(ext2, oper, depth)

    def emit_b(x, g, xi, j, value):
        mu = 2.0 * mu_a[x, tile(j), :] + value - late[x, tile(j), :]
        mu = mu + (count[x, 8 + 8 * j : 16 + 8 * j, :] * wave_b[x, tile(j), :] - data_b[x, tile(j), :])
        mu_b[x, tile(j), :] = mu
        total[x, tile(j), :] = total[x, tile(j), :] + mu * lap_b[x, tile(j), :]

    laplace(ext2, depth, OWN, emit_b)
    send_rows(send_lo, send_hi, lambda x, rows: mu_b[x, rows, :] * r2[x, rows, :])


def last_kernel(
    spots, late, later, r2, halo_lo, halo_hi, oper, count, data, wave, lap, total_in, total, ext, depth
):
    first = spots[0]
    clear_ends(ext)
    ext[OWN_X, OWN_Y, :] = late[...] * r2[...]
    fill_edges(ext, spots, halo_lo, halo_hi)
    apply_depth(ext, oper, depth)

    def emit(x, g, xi, j, value):
        mu = 2.0 * late[x, tile(j), :] + value - later[x, tile(j), :]
        mu = mu + (count[x, 8 + 8 * j : 16 + 8 * j, :] * wave[x, tile(j), :] - data[x, tile(j), :])
        total[lax.rem(first + g, GROUP), xi, tile(j), :] = total_in[x, tile(j), :] + mu * lap[x, tile(j), :]

    laplace(ext, depth, OWN, emit)


def pack_kernel(now, prev, late, later, out, near, edge, sems):
    order = ((0, now, NOW), (2, late, HALF + NOW), (1, prev, PREV), (3, later, HALF + PREV))
    bring = {f: pltpu.make_async_copy(field, near.at[f], sems.at[f]) for f, field, _ in order}
    for f, _, _ in order:
        bring[f].start()
    none = jnp.zeros((4, NZ), F32)
    sent = []
    for f, _, off in order:
        bring[f].wait()
        for p in range(8):
            sent.append(
                pltpu.make_async_copy(
                    near.at[f, :, NYL * p : NYL * p + NYL, :], out.at[p, :, off : off + NYL, :], sems.at[4 + 8 * f + p]
                )
            )
            sent[-1].start()
        if f % 2 == 0:

            def body(xi, carry):
                for p in range(8):
                    lo = NYL * p
                    edge[f // 2, p, xi, 0:4, :] = near[f, xi, lo - 4 : lo, :] if p > 0 else none
                    edge[f // 2, p, xi, 4:8, :] = near[f, xi, lo + NYL : lo + NYL + 4, :] if p < 7 else none
                return carry

            lax.fori_loop(0, GROUP, body, 0)
            at = f // 2 * HALF + EDGES
            sent.append(pltpu.make_async_copy(edge.at[f // 2], out.at[:, :, at : at + 8, :], sems.at[36 + f // 2]))
            sent[-1].start()
    for c in sent:
        c.wait()


def copy_block(dst, src):
    def body(x, carry):
        dst[x] = src[x]
        return carry

    lax.fori_loop(0, GROUP, body, 0, unroll=4)


def split_shot(me):
    return me // 8, lax.rem(me // 2, 4), lax.rem(me, 2)


def slot_of(start, which):
    return (start + lax.rem(which - start + 32, 8)) // 8


def select_kernel(ids, apertures, piece, other, piece_c, other_c, *outs):
    half, y, core = split_shot(ids[0])
    for k in range(4):
        start = apertures[8 * half + 2 * lax.rem(y + k, 4) + core, 0]
        for j in range(2):
            m = slot_of(start, 2 * y + j)
            row = m // 2
            own_half = lax.rem(m, 2) == half
            own_core = core == j
            for src, same_half, same_core in (
                (piece, True, True),
                (other, False, True),
                (piece_c, True, False),
                (other_c, False, False),
            ):

                @pl.when(jnp.logical_and(own_half == same_half, own_core == same_core))
                def _():
                    copy_block(outs[k].at[j], src.at[row])


def assemble_kernel(ids, apertures, r0, r1, r2, r3, out, send_lo, send_hi):
    _, y, _ = split_shot(ids[0])
    first = apertures[ids[0], 0]
    for k, src in enumerate((r0, r1, r2, r3)):
        for j in range(2):
            at = lax.rem(2 * lax.rem(y - k + 4, 4) + j - first + 32, 8)
            copy_block(out.at[pl.ds(at * GROUP, GROUP)], src.at[j])
    send_tiles(send_lo, send_hi, out)


def receivers_kernel(cells, lines, observed, count, data3, data1, data2, data4):
    zeros = jnp.zeros((NYL, NZ), F32)
    zeros_wide = jnp.zeros((WIDE, NZ), F32)

    def clear(x):
        for d in (count, data3):
            d[x] = zeros_wide
        for d in (data1, data2, data4):
            d[x] = zeros

    planes(clear)
    lanes = lax.broadcasted_iota(jnp.int32, (1, NZ), 1)

    def body(r, carry):
        y = lines[r]

        @pl.when(jnp.logical_and(y >= -8, y < NYL + 8))
        def _():
            cell = cells[r]
            x = cell // (256 * NZ)
            hit = lanes == lax.rem(cell, NZ)
            row = pl.ds(y + 8, 1)
            count[x, row, :] = count[x, row, :] + jnp.where(hit, 1.0, 0.0)
            data3[x, row, :] = data3[x, row, :] + jnp.where(hit, observed[2, r], 0.0)

            @pl.when(jnp.logical_and(y >= 0, y < NYL))
            def _():
                own = pl.ds(y, 1)
                for n, d in ((0, data1), (1, data2), (3, data4)):
                    d[x, own, :] = d[x, own, :] + jnp.where(hit, observed[n, r], 0.0)

        return carry

    lax.fori_loop(0, cells.shape[0], body, 0)


def bins_kernel(ids, apertures, recv, keep, give):
    mine, which = ids[0] // 8, lax.rem(ids[0], 8)
    zeros = jnp.zeros((GROUP, NYL, NZ), F32)
    for i in range(2):
        keep[i] = zeros
        give[i] = zeros
    for t in range(GROUP):
        m = slot_of(apertures[8 * mine + t, 0], which)
        i = m // 2

        @pl.when(lax.rem(m, 2) == mine)
        def _():
            keep[i] = keep[i] + recv[t]

        @pl.when(lax.rem(m, 2) != mine)
        def _():
            give[i] = give[i] + recv[t]


FIELD = jax.ShapeDtypeStruct((NX, NYL, NZ), F32)
WIDE_FIELD = jax.ShapeDtypeStruct((NX, WIDE, NZ), F32)
EDGE = jax.ShapeDtypeStruct((NX // 2, 8, NZ), F32)
TILE = jax.ShapeDtypeStruct((NX, 8, NZ), F32)
BLOCKS = jax.ShapeDtypeStruct((8, GROUP, NYL, NZ), F32)
PAIR = jax.ShapeDtypeStruct((2, GROUP, NYL, NZ), F32)
EXT = pltpu.VMEM((NX + 2 * PAD, ROWS, NZ), F32)
DEPTH = pltpu.VMEM((NX, WIDE, NZ), F32)
FIELD_VMEM = pltpu.VMEM((NX, NYL, NZ), F32)
TILE_VMEM = pltpu.VMEM((NX, 8, NZ), F32)


def call(kernel, specs, outs, scratch=(), flops=0, moved=0, out_spec=VMEM, limit=12):
    return pl.pallas_call(
        kernel,
        in_specs=specs,
        out_specs=[out_spec] * len(outs),
        out_shape=outs,
        scratch_shapes=list(scratch),
        compiler_params=pltpu.CompilerParams(vmem_limit_bytes=limit << 20),
        cost_estimate=pl.CostEstimate(flops=flops, bytes_accessed=moved, transcendentals=0),
    )


def per_device(
    courant_squared,
    wave_now,
    wave_prev,
    adj_late,
    adj_later,
    wavelet,
    sources,
    receivers,
    observed,
    apertures,
):
    me = lax.axis_index("shot")
    part = lax.axis_index("sub")
    ids = jnp.stack([me, part]).astype(jnp.int32)
    first = apertures[me, 0]
    oper = jnp.asarray(depth_operator())
    up = [(i, (i + 1) % 8) for i in range(8)]
    down = [((i + 1) % 8, i) for i in range(8)]
    across = [(i, (i + 8) % 16) for i in range(16)]
    chip = [(i, i ^ 1) for i in range(16)]
    halves = [list(range(8)), list(range(8, 16))]

    def along(k):
        return [(8 * h + 2 * y + c, 8 * h + 2 * ((y + k) % 4) + c) for h in range(2) for y in range(4) for c in range(2)]

    def edges(lo, hi):
        return lax.ppermute(hi, "sub", up), lax.ppermute(lo, "sub", down)

    piece = courant_squared[:, 0]
    other = lax.ppermute(piece, "shot", across)
    piece_c = lax.ppermute(piece, "shot", chip)
    other_c = lax.ppermute(other, "shot", chip)
    blocks = call(select_kernel, [SMEM] * 2 + [VMEM] * 4, [PAIR] * 4, moved=2 << 20)(
        ids, apertures, piece, other, piece_c, other_c
    )
    come = [blocks[0]] + [lax.ppermute(blocks[k], "shot", along(k)) for k in (1, 2, 3)]

    (packed,) = call(
        pack_kernel,
        [ANY] * 4,
        [jax.ShapeDtypeStruct((8, GROUP, TURNED, NZ), F32)],
        [
            pltpu.VMEM((4, GROUP, 256, NZ), F32),
            pltpu.VMEM((2, 8, GROUP, 8, NZ), F32),
            pltpu.SemaphoreType.DMA((38,)),
        ],
        moved=9 << 20,
        out_spec=ANY,
        limit=58,
    )(wave_now[0], wave_prev[0], adj_late[0], adj_later[0])
    packed, other = lax.optimization_barrier((packed, other))
    turned = lax.all_to_all(packed, "sub", 0, 0, tiled=True).reshape(NX, TURNED, NZ)
    r2, *r2_send = call(assemble_kernel, [SMEM] * 2 + [VMEM] * 4, [FIELD, TILE, TILE], moved=2 << 20)(
        ids, apertures, *come
    )
    r2_halo = edges(*r2_send)

    cell = sources[0]
    line = (cell // NZ) % 256 - NYL * part
    spots = jnp.stack(
        [
            first % 8,
            ((line >= 0) & (line < NYL)).astype(jnp.int32),
            cell // (256 * NZ),
            line,
            cell % NZ,
            (part > 0).astype(jnp.int32),
            (part < 7).astype(jnp.int32),
            ((line >= -8) & (line < NYL + 8)).astype(jnp.int32),
        ]
    )
    amounts = wavelet[0]
    cells = receivers[0]
    lines = (cells // NZ) % 256 - NYL * part

    count, data3, data1, data2, data4 = call(
        receivers_kernel, [SMEM] * 3, [WIDE_FIELD, WIDE_FIELD] + [FIELD] * 3, moved=6 << 20
    )(cells, lines, observed[0])
    r2, count = lax.optimization_barrier((r2, count))

    lap0, u1, lo, hi, u0, u0_edge = call(
        first_kernel,
        [SMEM, SMEM, ANY, VMEM, VMEM],
        [FIELD, FIELD, TILE, TILE, FIELD, TILE],
        [EXT, DEPTH, FIELD_VMEM, pltpu.SemaphoreType.DMA((4,))],
        flops=10 << 20,
        moved=8 << 20,
    )(spots, amounts, turned, r2, oper)
    u1_halo = edges(lo, hi)
    part4, mu5, mu5_edge = call(
        late_kernel,
        [SMEM, ANY] + [VMEM] * 4,
        [FIELD, FIELD, TILE],
        [EXT, DEPTH, FIELD_VMEM, pltpu.SemaphoreType.DMA((4,))],
        flops=10 << 20,
        moved=6 << 20,
    )(spots, turned, r2, *r2_halo, oper)
    u1, part4 = lax.optimization_barrier((u1, part4))
    lap1, u2, lap2, u3, lo, hi = call(
        middle_kernel,
        [SMEM, SMEM] + [VMEM] * 9,
        [FIELD] * 4 + [EDGE] * 2,
        [EXT, EXT, DEPTH, TILE_VMEM, TILE_VMEM],
        flops=20 << 20,
        moved=12 << 20,
    )(spots, amounts, u1, *u1_halo, u0, u0_edge, r2, *r2_halo, oper)
    u3_halo = edges(lo, hi)
    total, mu4, lo, hi = call(
        turn_kernel,
        [SMEM, SMEM] + [VMEM] * 9,
        [FIELD, FIELD, TILE, TILE],
        [EXT, DEPTH, FIELD_VMEM],
        flops=10 << 20,
        moved=8 << 20,
    )(spots, amounts, u3, *u3_halo, u2, r2, oper, part4, count, data4)
    mu4_halo = edges(lo, hi)
    total, mu3, mu2, lo, hi = call(
        back_kernel,
        [SMEM] + [VMEM] * 19,
        [FIELD] * 3 + [EDGE] * 2,
        [EXT, EXT, DEPTH] + [TILE_VMEM] * 4,
        flops=20 << 20,
        moved=16 << 20,
    )(
        spots, mu4, *mu4_halo, mu5, mu5_edge, r2, *r2_halo, oper, count, data3, data2,
        u3, *u3_halo, u2, lap2, lap1, total,
    )
    mu2_halo = edges(lo, hi)
    (total,) = call(last_kernel, [SMEM] + [VMEM] * 11, [BLOCKS], [EXT, DEPTH], flops=10 << 20, moved=8 << 20)(
        spots, mu2, mu3, r2, *mu2_halo, oper, count, data1, u1, lap0, total
    )

    recv = lax.all_to_all(total, "shot", 0, 0, axis_index_groups=halves, tiled=True)
    keep, give = call(bins_kernel, [SMEM, SMEM, VMEM], [PAIR, PAIR], moved=2 << 20)(ids, apertures, recv)
    result = keep + lax.ppermute(give, "shot", across)
    return result[:, None]


def solution(mesh):
    in_specs = (
        P(None, "shot", None, "sub", None),
        P("shot", "sub", None, None),
        P("shot", "sub", None, None),
        P("shot", "sub", None, None),
        P("shot", "sub", None, None),
        P("shot", None),
        P("shot"),
        P("shot", None),
        P("shot", None, None),
        P(),
    )
    out_specs = P(None, "shot", None, "sub", None)
    return jax.shard_map(
        per_device, mesh=mesh, in_specs=in_specs, out_specs=out_specs, check_vma=False
    )
```

```python
import functools

import jax
import jax.numpy as jnp
import ml_dtypes
import numpy as np
from jax import lax
from jax.experimental import pallas as pl
from jax.experimental.pallas import tpu as pltpu
from jax.sharding import PartitionSpec as P

STEPS = 4
STENCIL = (-205.0 / 72.0, 8.0 / 5.0, -1.0 / 5.0, 8.0 / 315.0, -1.0 / 560.0)
F32 = jnp.float32
BF16 = jnp.bfloat16
SMEM = pl.BlockSpec(memory_space=pltpu.SMEM)
VMEM = pl.BlockSpec(memory_space=pltpu.VMEM)
ANY = pl.BlockSpec(memory_space=pltpu.HBM)
NX, NYL, NZ = 64, 32, 128
GROUP = 8
PAD = 4
ROWS = 64
OWN0, OWN1 = 16, 48
WIDE0, WIDE1 = 8, 56
WIDE = WIDE1 - WIDE0
OWN_X, OWN_Y = slice(PAD, PAD + NX), slice(OWN0, OWN1)
CHUNK = 16
OWN, WITH_HALO = range(4), range(-1, 5)


def depth_operator():
    band = np.zeros((NZ, NZ), np.float32)
    for i in range(NZ):
        band[i, i] = np.float32(3.0 * STENCIL[0])
        for k in range(1, 5):
            for j in (i - k, i + k):
                if 0 <= j < NZ:
                    band[j, i] = np.float32(STENCIL[k])
    high = band.astype(ml_dtypes.bfloat16)
    low = (band - high.astype(np.float32)).astype(ml_dtypes.bfloat16)
    zero = np.zeros_like(high)
    return np.block([[high, low], [high, zero]])


def clear_ends(ext):
    zeros = jnp.zeros((PAD, ROWS, NZ), F32)
    ext[0:PAD] = zeros
    ext[PAD + NX : 2 * PAD + NX] = zeros


def planes(body):
    def step(x, carry):
        body(x)
        return carry

    lax.fori_loop(0, NX, step, 0, unroll=4)


def fill_edges(ext, spots, halo_lo, halo_hi):
    has_lo, has_hi = spots[5] == 1, spots[6] == 1

    def body(t, carry):
        lo = jnp.where(has_lo, halo_lo[t], 0.0)
        hi = jnp.where(has_hi, halo_hi[t], 0.0)
        for half in range(2):
            x = PAD + 2 * t + half
            ext[x, OWN0 - 4 : OWN0, :] = lo[4 * half : 4 * half + 4]
            ext[x, OWN1 : OWN1 + 4, :] = hi[4 * half : 4 * half + 4]
        return carry

    lax.fori_loop(0, NX // 2, body, 0, unroll=4)


def fill_tiles(ext, spots, lo, hi):
    has_lo, has_hi = spots[5] == 1, spots[6] == 1

    def body(x):
        ext[PAD + x, WIDE0:OWN0, :] = jnp.where(has_lo, lo(x), 0.0)
        ext[PAD + x, OWN1:WIDE1, :] = jnp.where(has_hi, hi(x), 0.0)

    planes(body)


def fill_ring(ext, edge):
    def body(x):
        ext[PAD + x, OWN0 - 4 : OWN0, :] = edge[x, 0:4, :]
        ext[PAD + x, OWN1 : OWN1 + 4, :] = edge[x, 4:8, :]

    planes(body)


def apply_depth(ext, oper, depth, wide=False):
    r0, r1 = (WIDE0, WIDE1) if wide else (OWN0, OWN1)
    n = CHUNK
    for at in range(0, NX, n):
        rows = ext[PAD + at : PAD + at + n, r0:r1, :].reshape(n * (r1 - r0), NZ)
        high = rows.astype(BF16)
        low = (rows - high.astype(F32)).astype(BF16)
        prod = jnp.dot(jnp.concatenate([high, low], axis=1), oper[...], preferred_element_type=F32)
        depth[at : at + n, r0 - WIDE0 : r1 - WIDE0, :] = (prod[:, :NZ] + prod[:, NZ:]).reshape(n, r1 - r0, NZ)


def laplace(ext, depth, tiles, emit):
    def body(g, carry):
        base = PAD + g * GROUP
        for j in tiles:
            r0 = OWN0 + 8 * j
            col = [ext[base - PAD + i, r0 : r0 + 8, :] for i in range(GROUP + 2 * PAD)]
            for xi in range(GROUP):
                acc = depth[g * GROUP + xi, r0 - WIDE0 : r0 - WIDE0 + 8, :]
                for k in range(1, 5):
                    beside = (
                        col[xi + PAD + k]
                        + col[xi + PAD - k]
                        + (
                            ext[base + xi, r0 + k : r0 + k + 8, :]
                            + ext[base + xi, r0 - k : r0 - k + 8, :]
                        )
                    )
                    acc = acc + STENCIL[k] * beside
                emit(g * GROUP + xi, g, xi, j, acc)
        return carry

    lax.fori_loop(0, NX // GROUP, body, 0)


def tile(j):
    return slice(8 * j, 8 * j + 8)


def ext_tile(j):
    return slice(OWN0 + 8 * j, OWN0 + 8 * j + 8)


def send_rows(send_lo, send_hi, read):
    def body(t, carry):
        for half in range(2):
            send_lo[t, 4 * half : 4 * half + 4, :] = read(2 * t + half, slice(0, 4))
            send_hi[t, 4 * half : 4 * half + 4, :] = read(2 * t + half, slice(NYL - 4, NYL))
        return carry

    lax.fori_loop(0, NX // 2, body, 0, unroll=4)


def send_tiles(send_lo, send_hi, field):
    def body(x):
        send_lo[x] = field[x, 0:8, :]
        send_hi[x] = field[x, NYL - 8 : NYL, :]

    planes(body)


def add_source(spots, amount, ref, x0, y0, wide=False):
    @pl.when(spots[7 if wide else 1] == 1)
    def _():
        x, y, z = x0 + spots[2], y0 + spots[3], spots[4]
        lanes = lax.broadcasted_iota(jnp.int32, (1, NZ), 1)
        row = ref[x, pl.ds(y, 1), :]
        ref[x, pl.ds(y, 1), :] = row + jnp.where(lanes == z, amount, 0.0)


NOW, PREV, EDGES, HALF, TURNED = 0, 32, 64, 72, 144


def unpack(turned, base, sems, now, edge, prev, extra):
    copies = []
    for n, (off, rows, dst) in enumerate(
        ((NOW, NYL, now), (EDGES, 8, edge), (PREV, NYL, prev), (NOW, NYL, extra))
    ):
        copies.append(pltpu.make_async_copy(turned.at[:, base + off : base + off + rows, :], dst, sems.at[n]))
    for c in copies:
        c.start()
    return copies


def first_kernel(spots, wavelet, turned, r2, oper, lap, new, send_lo, send_hi, now, edge, ext, depth, prev, sems):
    copies = unpack(turned, 0, sems, ext.at[OWN_X, OWN_Y, :], edge, prev, now)
    clear_ends(ext)
    for c in copies[:3]:
        c.wait()
    fill_ring(ext, edge)
    apply_depth(ext, oper, depth)

    def emit(x, g, xi, j, value):
        lap[x, tile(j), :] = value
        new[x, tile(j), :] = 2.0 * ext[PAD + x, ext_tile(j), :] - prev[x, tile(j), :] + r2[x, tile(j), :] * value

    laplace(ext, depth, OWN, emit)
    add_source(spots, wavelet[0], new, 0, 0)
    send_tiles(send_lo, send_hi, new)
    copies[3].wait()


def spread_edges(edge, lo, hi):
    def body(x):
        lo[x, 4:8, :] = edge[x, 0:4, :]
        hi[x, 0:4, :] = edge[x, 4:8, :]

    planes(body)


def spread_halos(halo_lo, halo_hi, lo, hi):
    def body(t, carry):
        for half in range(2):
            lo[2 * t + half, 4:8, :] = halo_lo[t, 4 * half : 4 * half + 4, :]
            hi[2 * t + half, 0:4, :] = halo_hi[t, 4 * half : 4 * half + 4, :]
        return carry

    lax.fori_loop(0, NX // 2, body, 0, unroll=4)


def middle_kernel(
    spots, wavelet, now, now_lo, now_hi, prev, edge, r2, r2_lo, r2_hi, oper,
    lap_a, new_a, lap_b, new_b, send_lo, send_hi, ext, ext2, depth, old_lo, old_hi,
):
    has = (spots[5] == 1, spots[6] == 1)
    clear_ends(ext)
    clear_ends(ext2)
    ext[OWN_X, OWN_Y, :] = now[...]
    fill_tiles(ext, spots, lambda x: now_lo[x], lambda x: now_hi[x])
    spread_edges(edge, old_lo, old_hi)
    apply_depth(ext, oper, depth, True)

    def emit(x, g, xi, j, value):
        twice = 2.0 * ext[PAD + x, ext_tile(j), :]
        if j in OWN:
            u = twice - prev[x, tile(j), :] + r2[x, tile(j), :] * value
            lap_a[x, tile(j), :] = value
            new_a[x, tile(j), :] = u
        else:
            old, weight, there = (old_lo, r2_lo, has[0]) if j < 0 else (old_hi, r2_hi, has[1])
            u = jnp.where(there, twice - old[x] + weight[x] * value, 0.0)
        ext2[PAD + x, ext_tile(j), :] = u

    laplace(ext, depth, WITH_HALO, emit)
    add_source(spots, wavelet[1], new_a, 0, 0)
    add_source(spots, wavelet[1], ext2, PAD, OWN0, True)
    apply_depth(ext2, oper, depth)

    def emit_b(x, g, xi, j, value):
        lap_b[x, tile(j), :] = value
        new_b[x, tile(j), :] = 2.0 * ext2[PAD + x, ext_tile(j), :] - now[x, tile(j), :] + r2[x, tile(j), :] * value

    laplace(ext2, depth, OWN, emit_b)
    add_source(spots, wavelet[2], new_b, 0, 0)
    send_rows(send_lo, send_hi, lambda x, rows: new_b[x, rows, :])


def late_kernel(spots, turned, r2, r2_lo, r2_hi, oper, mu, late, edge, ext, depth, later, sems):
    copies = unpack(turned, HALF, sems, late, edge, later, ext.at[OWN_X, OWN_Y, :])
    clear_ends(ext)
    for c in copies:
        c.wait()

    def weigh(x):
        ext[PAD + x, OWN_Y, :] = late[x] * r2[x]
        ext[PAD + x, OWN0 - 4 : OWN0, :] = edge[x, 0:4, :] * r2_lo[x, 4:8, :]
        ext[PAD + x, OWN1 : OWN1 + 4, :] = edge[x, 4:8, :] * r2_hi[x, 0:4, :]

    planes(weigh)
    apply_depth(ext, oper, depth)

    def emit(x, g, xi, j, value):
        mu[x, tile(j), :] = 2.0 * late[x, tile(j), :] + value - later[x, tile(j), :]

    laplace(ext, depth, OWN, emit)


def turn_kernel(
    spots, wavelet, now, halo_lo, halo_hi, prev, r2, oper, part, count, data, total, mu, send_lo, send_hi, ext, depth, new
):
    clear_ends(ext)
    ext[OWN_X, OWN_Y, :] = now[...]
    fill_edges(ext, spots, halo_lo, halo_hi)
    apply_depth(ext, oper, depth)

    def emit(x, g, xi, j, value):
        new[x, tile(j), :] = 2.0 * ext[PAD + x, ext_tile(j), :] - prev[x, tile(j), :] + r2[x, tile(j), :] * value
        total[x, tile(j), :] = value

    laplace(ext, depth, OWN, emit)
    add_source(spots, wavelet[3], new, 0, 0)

    def finish(x):
        m = part[x] + (count[x, 8 : 8 + NYL, :] * new[x] - data[x])
        mu[x] = m
        total[x] = m * total[x]

    planes(finish)
    send_tiles(send_lo, send_hi, mu)


def back_kernel(
    spots, late, late_lo, late_hi, later, edge, r2, r2_lo, r2_hi, oper, count, data_a, data_b,
    wave_a, wave_lo, wave_hi, wave_b, lap_a, lap_b, total_in,
    total, mu_a, mu_b, send_lo, send_hi, ext, ext2, depth, old_lo, old_hi, u_lo, u_hi,
):
    has = (spots[5] == 1, spots[6] == 1)
    clear_ends(ext)
    clear_ends(ext2)
    ext[OWN_X, OWN_Y, :] = late[...] * r2[...]
    fill_tiles(ext, spots, lambda x: late_lo[x] * r2_lo[x], lambda x: late_hi[x] * r2_hi[x])
    spread_edges(edge, old_lo, old_hi)
    spread_halos(wave_lo, wave_hi, u_lo, u_hi)
    apply_depth(ext, oper, depth, True)

    def emit(x, g, xi, j, value):
        wide = slice(8 + 8 * j, 16 + 8 * j)
        many, heard = count[x, wide, :], data_a[x, wide, :]
        if j in OWN:
            mu = 2.0 * late[x, tile(j), :] + value - later[x, tile(j), :]
            mu = mu + (many * wave_a[x, tile(j), :] - heard)
            mu_a[x, tile(j), :] = mu
            total[x, tile(j), :] = total_in[x, tile(j), :] + mu * lap_a[x, tile(j), :]
            w = mu * r2[x, tile(j), :]
        else:
            near, old, u, weight, there = (
                (late_lo, old_lo, u_lo, r2_lo, has[0]) if j < 0 else (late_hi, old_hi, u_hi, r2_hi, has[1])
            )
            mu = 2.0 * near[x] + value - old[x] + (many * u[x] - heard)
            w = jnp.where(there, mu * weight[x], 0.0)
        ext2[PAD + x, ext_tile(j), :] = w

    laplace(ext, depth, WITH_HALO, emit)
    apply_depth(ext2, oper, depth)

    def emit_b(x, g, xi, j, value):
        mu = 2.0 * mu_a[x, tile(j), :] + value - late[x, tile(j), :]
        mu = mu + (count[x, 8 + 8 * j : 16 + 8 * j, :] * wave_b[x, tile(j), :] - data_b[x, tile(j), :])
        mu_b[x, tile(j), :] = mu
        total[x, tile(j), :] = total[x, tile(j), :] + mu * lap_b[x, tile(j), :]

    laplace(ext2, depth, OWN, emit_b)
    send_rows(send_lo, send_hi, lambda x, rows: mu_b[x, rows, :] * r2[x, rows, :])


def last_kernel(
    spots, late, later, r2, halo_lo, halo_hi, oper, count, data, wave, lap, total_in, total, ext, depth
):
    first = spots[0]
    clear_ends(ext)
    ext[OWN_X, OWN_Y, :] = late[...] * r2[...]
    fill_edges(ext, spots, halo_lo, halo_hi)
    apply_depth(ext, oper, depth)

    def emit(x, g, xi, j, value):
        mu = 2.0 * late[x, tile(j), :] + value - later[x, tile(j), :]
        mu = mu + (count[x, 8 + 8 * j : 16 + 8 * j, :] * wave[x, tile(j), :] - data[x, tile(j), :])
        total[lax.rem(first + g, GROUP), xi, tile(j), :] = total_in[x, tile(j), :] + mu * lap[x, tile(j), :]

    laplace(ext, depth, OWN, emit)


def pack_kernel(now, prev, late, later, out, near, edge, sems):
    order = ((0, now, NOW), (2, late, HALF + NOW), (1, prev, PREV), (3, later, HALF + PREV))
    bring = {f: pltpu.make_async_copy(field, near.at[f], sems.at[f]) for f, field, _ in order}
    for f, _, _ in order:
        bring[f].start()
    none = jnp.zeros((4, NZ), F32)
    sent = []
    for f, _, off in order:
        bring[f].wait()
        for p in range(8):
            sent.append(
                pltpu.make_async_copy(
                    near.at[f, :, NYL * p : NYL * p + NYL, :], out.at[p, :, off : off + NYL, :], sems.at[4 + 8 * f + p]
                )
            )
            sent[-1].start()
        if f % 2 == 0:

            def body(xi, carry):
                for p in range(8):
                    lo = NYL * p
                    edge[f // 2, p, xi, 0:4, :] = near[f, xi, lo - 4 : lo, :] if p > 0 else none
                    edge[f // 2, p, xi, 4:8, :] = near[f, xi, lo + NYL : lo + NYL + 4, :] if p < 7 else none
                return carry

            lax.fori_loop(0, GROUP, body, 0)
            at = f // 2 * HALF + EDGES
            sent.append(pltpu.make_async_copy(edge.at[f // 2], out.at[:, :, at : at + 8, :], sems.at[36 + f // 2]))
            sent[-1].start()
    for c in sent:
        c.wait()


def copy_block(dst, src):
    def body(x, carry):
        dst[x] = src[x]
        return carry

    lax.fori_loop(0, GROUP, body, 0, unroll=4)


def split_shot(me):
    return me // 8, lax.rem(me // 2, 4), lax.rem(me, 2)


def slot_of(start, which):
    return (start + lax.rem(which - start + 32, 8)) // 8


def select_kernel(ids, apertures, piece, other, piece_c, other_c, *outs):
    half, y, core = split_shot(ids[0])
    for k in range(4):
        start = apertures[8 * half + 2 * lax.rem(y + k, 4) + core, 0]
        for j in range(2):
            m = slot_of(start, 2 * y + j)
            row = m // 2
            own_half = lax.rem(m, 2) == half
            own_core = core == j
            for src, same_half, same_core in (
                (piece, True, True),
                (other, False, True),
                (piece_c, True, False),
                (other_c, False, False),
            ):

                @pl.when(jnp.logical_and(own_half == same_half, own_core == same_core))
                def _():
                    copy_block(outs[k].at[j], src.at[row])


def assemble_kernel(ids, apertures, r0, r1, r2, r3, out, send_lo, send_hi):
    _, y, _ = split_shot(ids[0])
    first = apertures[ids[0], 0]
    for k, src in enumerate((r0, r1, r2, r3)):
        for j in range(2):
            at = lax.rem(2 * lax.rem(y - k + 4, 4) + j - first + 32, 8)
            copy_block(out.at[pl.ds(at * GROUP, GROUP)], src.at[j])
    send_tiles(send_lo, send_hi, out)


def receivers_kernel(cells, lines, observed, count, data3, data1, data2, data4):
    zeros = jnp.zeros((NYL, NZ), F32)
    zeros_wide = jnp.zeros((WIDE, NZ), F32)

    def clear(x):
        for d in (count, data3):
            d[x] = zeros_wide
        for d in (data1, data2, data4):
            d[x] = zeros

    planes(clear)
    lanes = lax.broadcasted_iota(jnp.int32, (1, NZ), 1)

    def body(r, carry):
        y = lines[r]

        @pl.when(jnp.logical_and(y >= -8, y < NYL + 8))
        def _():
            cell = cells[r]
            x = cell // (256 * NZ)
            hit = lanes == lax.rem(cell, NZ)
            row = pl.ds(y + 8, 1)
            count[x, row, :] = count[x, row, :] + jnp.where(hit, 1.0, 0.0)
            data3[x, row, :] = data3[x, row, :] + jnp.where(hit, observed[2, r], 0.0)

            @pl.when(jnp.logical_and(y >= 0, y < NYL))
            def _():
                own = pl.ds(y, 1)
                for n, d in ((0, data1), (1, data2), (3, data4)):
                    d[x, own, :] = d[x, own, :] + jnp.where(hit, observed[n, r], 0.0)

        return carry

    lax.fori_loop(0, cells.shape[0], body, 0)


def bins_kernel(ids, apertures, recv, keep, give):
    mine, which = ids[0] // 8, lax.rem(ids[0], 8)
    zeros = jnp.zeros((GROUP, NYL, NZ), F32)
    for i in range(2):
        keep[i] = zeros
        give[i] = zeros
    for t in range(GROUP):
        m = slot_of(apertures[8 * mine + t, 0], which)
        i = m // 2

        @pl.when(lax.rem(m, 2) == mine)
        def _():
            keep[i] = keep[i] + recv[t]

        @pl.when(lax.rem(m, 2) != mine)
        def _():
            give[i] = give[i] + recv[t]


FIELD = jax.ShapeDtypeStruct((NX, NYL, NZ), F32)
WIDE_FIELD = jax.ShapeDtypeStruct((NX, WIDE, NZ), F32)
EDGE = jax.ShapeDtypeStruct((NX // 2, 8, NZ), F32)
TILE = jax.ShapeDtypeStruct((NX, 8, NZ), F32)
BLOCKS = jax.ShapeDtypeStruct((8, GROUP, NYL, NZ), F32)
PAIR = jax.ShapeDtypeStruct((2, GROUP, NYL, NZ), F32)
EXT = pltpu.VMEM((NX + 2 * PAD, ROWS, NZ), F32)
DEPTH = pltpu.VMEM((NX, WIDE, NZ), F32)
FIELD_VMEM = pltpu.VMEM((NX, NYL, NZ), F32)
TILE_VMEM = pltpu.VMEM((NX, 8, NZ), F32)


def call(kernel, specs, outs, scratch=(), flops=0, moved=0, out_spec=VMEM, limit=12):
    return pl.pallas_call(
        kernel,
        in_specs=specs,
        out_specs=[out_spec] * len(outs),
        out_shape=outs,
        scratch_shapes=list(scratch),
        compiler_params=pltpu.CompilerParams(vmem_limit_bytes=limit << 20),
        cost_estimate=pl.CostEstimate(flops=flops, bytes_accessed=moved, transcendentals=0),
    )


def per_device(
    courant_squared,
    wave_now,
    wave_prev,
    adj_late,
    adj_later,
    wavelet,
    sources,
    receivers,
    observed,
    apertures,
):
    me = lax.axis_index("shot")
    part = lax.axis_index("sub")
    ids = jnp.stack([me, part]).astype(jnp.int32)
    first = apertures[me, 0]
    oper = jnp.asarray(depth_operator())
    up = [(i, (i + 1) % 8) for i in range(8)]
    down = [((i + 1) % 8, i) for i in range(8)]
    across = [(i, (i + 8) % 16) for i in range(16)]
    chip = [(i, i ^ 1) for i in range(16)]
    halves = [list(range(8)), list(range(8, 16))]

    def along(k):
        return [(8 * h + 2 * y + c, 8 * h + 2 * ((y + k) % 4) + c) for h in range(2) for y in range(4) for c in range(2)]

    def edges(lo, hi):
        return lax.ppermute(hi, "sub", up), lax.ppermute(lo, "sub", down)

    piece = courant_squared[:, 0]
    other = lax.ppermute(piece, "shot", across)
    piece_c = lax.ppermute(piece, "shot", chip)
    other_c = lax.ppermute(other, "shot", chip)
    blocks = call(select_kernel, [SMEM] * 2 + [VMEM] * 4, [PAIR] * 4, moved=2 << 20)(
        ids, apertures, piece, other, piece_c, other_c
    )
    come = [blocks[0]] + [lax.ppermute(blocks[k], "shot", along(k)) for k in (1, 2, 3)]

    (packed,) = call(
        pack_kernel,
        [ANY] * 4,
        [jax.ShapeDtypeStruct((8, GROUP, TURNED, NZ), F32)],
        [
            pltpu.VMEM((4, GROUP, 256, NZ), F32),
            pltpu.VMEM((2, 8, GROUP, 8, NZ), F32),
            pltpu.SemaphoreType.DMA((38,)),
        ],
        moved=9 << 20,
        out_spec=ANY,
        limit=58,
    )(wave_now[0], wave_prev[0], adj_late[0], adj_later[0])
    turned = lax.all_to_all(packed, "sub", 0, 0, tiled=True).reshape(NX, TURNED, NZ)
    r2, *r2_send = call(assemble_kernel, [SMEM] * 2 + [VMEM] * 4, [FIELD, TILE, TILE], moved=2 << 20)(
        ids, apertures, *come
    )
    r2_halo = edges(*r2_send)

    cell = sources[0]
    line = (cell // NZ) % 256 - NYL * part
    spots = jnp.stack(
        [
            first % 8,
            ((line >= 0) & (line < NYL)).astype(jnp.int32),
            cell // (256 * NZ),
            line,
            cell % NZ,
            (part > 0).astype(jnp.int32),
            (part < 7).astype(jnp.int32),
            ((line >= -8) & (line < NYL + 8)).astype(jnp.int32),
        ]
    )
    amounts = wavelet[0]
    cells = receivers[0]
    lines = (cells // NZ) % 256 - NYL * part

    count, data3, data1, data2, data4 = call(
        receivers_kernel, [SMEM] * 3, [WIDE_FIELD, WIDE_FIELD] + [FIELD] * 3, flops=1 << 40, moved=6 << 20
    )(cells, lines, observed[0])
    r2, count = lax.optimization_barrier((r2, count))

    lap0, u1, lo, hi, u0, u0_edge = call(
        first_kernel,
        [SMEM, SMEM, ANY, VMEM, VMEM],
        [FIELD, FIELD, TILE, TILE, FIELD, TILE],
        [EXT, DEPTH, FIELD_VMEM, pltpu.SemaphoreType.DMA((4,))],
        flops=10 << 20,
        moved=8 << 20,
    )(spots, amounts, turned, r2, oper)
    u1_halo = edges(lo, hi)
    part4, mu5, mu5_edge = call(
        late_kernel,
        [SMEM, ANY] + [VMEM] * 4,
        [FIELD, FIELD, TILE],
        [EXT, DEPTH, FIELD_VMEM, pltpu.SemaphoreType.DMA((4,))],
        flops=10 << 20,
        moved=6 << 20,
    )(spots, turned, r2, *r2_halo, oper)
    u1, part4 = lax.optimization_barrier((u1, part4))
    lap1, u2, lap2, u3, lo, hi = call(
        middle_kernel,
        [SMEM, SMEM] + [VMEM] * 9,
        [FIELD] * 4 + [EDGE] * 2,
        [EXT, EXT, DEPTH, TILE_VMEM, TILE_VMEM],
        flops=20 << 20,
        moved=12 << 20,
    )(spots, amounts, u1, *u1_halo, u0, u0_edge, r2, *r2_halo, oper)
    u3_halo = edges(lo, hi)
    total, mu4, lo, hi = call(
        turn_kernel,
        [SMEM, SMEM] + [VMEM] * 9,
        [FIELD, FIELD, TILE, TILE],
        [EXT, DEPTH, FIELD_VMEM],
        flops=10 << 20,
        moved=8 << 20,
    )(spots, amounts, u3, *u3_halo, u2, r2, oper, part4, count, data4)
    mu4_halo = edges(lo, hi)
    total, mu3, mu2, lo, hi = call(
        back_kernel,
        [SMEM] + [VMEM] * 19,
        [FIELD] * 3 + [EDGE] * 2,
        [EXT, EXT, DEPTH] + [TILE_VMEM] * 4,
        flops=20 << 20,
        moved=16 << 20,
    )(
        spots, mu4, *mu4_halo, mu5, mu5_edge, r2, *r2_halo, oper, count, data3, data2,
        u3, *u3_halo, u2, lap2, lap1, total,
    )
    mu2_halo = edges(lo, hi)
    (total,) = call(last_kernel, [SMEM] + [VMEM] * 11, [BLOCKS], [EXT, DEPTH], flops=10 << 20, moved=8 << 20)(
        spots, mu2, mu3, r2, *mu2_halo, oper, count, data1, u1, lap0, total
    )

    recv = lax.all_to_all(total, "shot", 0, 0, axis_index_groups=halves, tiled=True)
    keep, give = call(bins_kernel, [SMEM, SMEM, VMEM], [PAIR, PAIR], moved=2 << 20)(ids, apertures, recv)
    result = keep + lax.ppermute(give, "shot", across)
    return result[:, None]


def solution(mesh):
    in_specs = (
        P(None, "shot", None, "sub", None),
        P("shot", "sub", None, None),
        P("shot", "sub", None, None),
        P("shot", "sub", None, None),
        P("shot", "sub", None, None),
        P("shot", None),
        P("shot"),
        P("shot", None),
        P("shot", None, None),
        P(),
    )
    out_specs = P(None, "shot", None, "sub", None)
    return jax.shard_map(
        per_device, mesh=mesh, in_specs=in_specs, out_specs=out_specs, check_vma=False
    )
```

```python
import functools

import jax
import jax.numpy as jnp
import ml_dtypes
import numpy as np
from jax import lax
from jax.experimental import pallas as pl
from jax.experimental.pallas import tpu as pltpu
from jax.sharding import PartitionSpec as P

STEPS = 4
STENCIL = (-205.0 / 72.0, 8.0 / 5.0, -1.0 / 5.0, 8.0 / 315.0, -1.0 / 560.0)
F32 = jnp.float32
BF16 = jnp.bfloat16
SMEM = pl.BlockSpec(memory_space=pltpu.SMEM)
VMEM = pl.BlockSpec(memory_space=pltpu.VMEM)
ANY = pl.BlockSpec(memory_space=pltpu.HBM)
NX, NYL, NZ = 64, 32, 128
GROUP = 8
PAD = 4
ROWS = 64
OWN0, OWN1 = 16, 48
WIDE0, WIDE1 = 8, 56
WIDE = WIDE1 - WIDE0
OWN_X, OWN_Y = slice(PAD, PAD + NX), slice(OWN0, OWN1)
CHUNK = 16
OWN, WITH_HALO = range(4), range(-1, 5)


def depth_operator():
    band = np.zeros((NZ, NZ), np.float32)
    for i in range(NZ):
        band[i, i] = np.float32(3.0 * STENCIL[0])
        for k in range(1, 5):
            for j in (i - k, i + k):
                if 0 <= j < NZ:
                    band[j, i] = np.float32(STENCIL[k])
    high = band.astype(ml_dtypes.bfloat16)
    low = (band - high.astype(np.float32)).astype(ml_dtypes.bfloat16)
    zero = np.zeros_like(high)
    return np.block([[high, low], [high, zero]])


def clear_ends(ext):
    zeros = jnp.zeros((PAD, ROWS, NZ), F32)
    ext[0:PAD] = zeros
    ext[PAD + NX : 2 * PAD + NX] = zeros


def planes(body):
    def step(x, carry):
        body(x)
        return carry

    lax.fori_loop(0, NX, step, 0, unroll=16)


def fill_edges(ext, spots, halo_lo, halo_hi):
    has_lo, has_hi = spots[5] == 1, spots[6] == 1

    def body(t, carry):
        lo = jnp.where(has_lo, halo_lo[t], 0.0)
        hi = jnp.where(has_hi, halo_hi[t], 0.0)
        for half in range(2):
            x = PAD + 2 * t + half
            ext[x, OWN0 - 4 : OWN0, :] = lo[4 * half : 4 * half + 4]
            ext[x, OWN1 : OWN1 + 4, :] = hi[4 * half : 4 * half + 4]
        return carry

    lax.fori_loop(0, NX // 2, body, 0, unroll=8)


def fill_tiles(ext, spots, lo, hi):
    has_lo, has_hi = spots[5] == 1, spots[6] == 1

    def body(x):
        ext[PAD + x, WIDE0:OWN0, :] = jnp.where(has_lo, lo(x), 0.0)
        ext[PAD + x, OWN1:WIDE1, :] = jnp.where(has_hi, hi(x), 0.0)

    planes(body)


def fill_ring(ext, edge):
    def body(x):
        ext[PAD + x, OWN0 - 4 : OWN0, :] = edge[x, 0:4, :]
        ext[PAD + x, OWN1 : OWN1 + 4, :] = edge[x, 4:8, :]

    planes(body)


def no_edges(ext):
    zeros = jnp.zeros((4, NZ), F32)

    def body(x):
        ext[PAD + x, OWN0 - 4 : OWN0, :] = zeros
        ext[PAD + x, OWN1 : OWN1 + 4, :] = zeros

    planes(body)


def halo_taps(strip, x, j):
    way = -1 if j == 0 else 1
    acc = None
    for k in range(1, 5):
        term = STENCIL[k] * strip[x, 8 + way * k : 16 + way * k, :]
        acc = term if acc is None else acc + term
    return acc


def fill_strip(strip, spots, halo_lo, halo_hi):
    has_lo, has_hi = spots[5] == 1, spots[6] == 1
    zeros = jnp.zeros((8, NZ), F32)

    def body(t, carry):
        lo = jnp.where(has_lo, halo_lo[t], 0.0)
        hi = jnp.where(has_hi, halo_hi[t], 0.0)
        for half in range(2):
            strip[2 * t + half, 4:8, :] = lo[4 * half : 4 * half + 4]
            strip[2 * t + half, 8:16, :] = zeros
            strip[2 * t + half, 16:20, :] = hi[4 * half : 4 * half + 4]
        return carry

    lax.fori_loop(0, NX // 2, body, 0, unroll=8)


def apply_depth(ext, oper, depth, wide=False, span=None):
    r0, r1 = span or ((WIDE0, WIDE1) if wide else (OWN0, OWN1))
    n = CHUNK
    for at in range(0, NX, n):
        rows = ext[PAD + at : PAD + at + n, r0:r1, :].reshape(n * (r1 - r0), NZ)
        high = rows.astype(BF16)
        low = (rows - high.astype(F32)).astype(BF16)
        prod = jnp.dot(jnp.concatenate([high, low], axis=1), oper[...], preferred_element_type=F32)
        depth[at : at + n, r0 - WIDE0 : r1 - WIDE0, :] = (prod[:, :NZ] + prod[:, NZ:]).reshape(n, r1 - r0, NZ)


def laplace(ext, depth, tiles, emit):
    def body(g, carry):
        base = PAD + g * GROUP
        for j in tiles:
            r0 = OWN0 + 8 * j
            col = [ext[base - PAD + i, r0 : r0 + 8, :] for i in range(GROUP + 2 * PAD)]
            for xi in range(GROUP):
                acc = depth[g * GROUP + xi, r0 - WIDE0 : r0 - WIDE0 + 8, :]
                for k in range(1, 5):
                    beside = (
                        col[xi + PAD + k]
                        + col[xi + PAD - k]
                        + (
                            ext[base + xi, r0 + k : r0 + k + 8, :]
                            + ext[base + xi, r0 - k : r0 - k + 8, :]
                        )
                    )
                    acc = acc + STENCIL[k] * beside
                emit(g * GROUP + xi, g, xi, j, acc)
        return carry

    lax.fori_loop(0, NX // GROUP, body, 0)


def tile(j):
    return slice(8 * j, 8 * j + 8)


def ext_tile(j):
    return slice(OWN0 + 8 * j, OWN0 + 8 * j + 8)


def send_rows(send_lo, send_hi, read):
    def body(t, carry):
        for half in range(2):
            send_lo[t, 4 * half : 4 * half + 4, :] = read(2 * t + half, slice(0, 4))
            send_hi[t, 4 * half : 4 * half + 4, :] = read(2 * t + half, slice(NYL - 4, NYL))
        return carry

    lax.fori_loop(0, NX // 2, body, 0, unroll=8)


def send_tiles(send_lo, send_hi, field):
    def body(x):
        send_lo[x] = field[x, 0:8, :]
        send_hi[x] = field[x, NYL - 8 : NYL, :]

    planes(body)


def add_source(spots, amount, ref, x0, y0, wide=False):
    @pl.when(spots[7 if wide else 1] == 1)
    def _():
        x, y, z = x0 + spots[2], y0 + spots[3], spots[4]
        lanes = lax.broadcasted_iota(jnp.int32, (1, NZ), 1)
        row = ref[x, pl.ds(y, 1), :]
        ref[x, pl.ds(y, 1), :] = row + jnp.where(lanes == z, amount, 0.0)


NOW, PREV, EDGES, HALF, TURNED = 0, 32, 64, 72, 144


def unpack(turned, base, sems, now, edge, prev, extra):
    copies = []
    for n, (off, rows, dst) in enumerate(
        ((NOW, NYL, now), (EDGES, 8, edge), (PREV, NYL, prev), (NOW, NYL, extra))
    ):
        copies.append(pltpu.make_async_copy(turned.at[:, base + off : base + off + rows, :], dst, sems.at[n]))
    for c in copies:
        c.start()
    return copies


def first_kernel(spots, wavelet, turned, r2, oper, lap, new, send_lo, send_hi, now, edge, ext, depth, prev, sems):
    copies = unpack(turned, 0, sems, ext.at[OWN_X, OWN_Y, :], edge, prev, now)
    clear_ends(ext)
    for c in copies[:3]:
        c.wait()
    fill_ring(ext, edge)
    apply_depth(ext, oper, depth)

    def emit(x, g, xi, j, value):
        lap[x, tile(j), :] = value
        new[x, tile(j), :] = 2.0 * ext[PAD + x, ext_tile(j), :] - prev[x, tile(j), :] + r2[x, tile(j), :] * value

    laplace(ext, depth, OWN, emit)
    add_source(spots, wavelet[0], new, 0, 0)
    send_tiles(send_lo, send_hi, new)
    copies[3].wait()


def spread_edges(edge, lo, hi):
    def body(x):
        lo[x, 4:8, :] = edge[x, 0:4, :]
        hi[x, 0:4, :] = edge[x, 4:8, :]

    planes(body)


def spread_halos(halo_lo, halo_hi, lo, hi):
    def body(t, carry):
        for half in range(2):
            lo[2 * t + half, 4:8, :] = halo_lo[t, 4 * half : 4 * half + 4, :]
            hi[2 * t + half, 0:4, :] = halo_hi[t, 4 * half : 4 * half + 4, :]
        return carry

    lax.fori_loop(0, NX // 2, body, 0, unroll=8)


def middle_kernel(
    spots, wavelet, now, now_lo, now_hi, prev, edge, r2, r2_lo, r2_hi, oper,
    lap_a, new_a, lap_b, new_b, send_lo, send_hi, ext, ext2, depth, old_lo, old_hi,
):
    has = (spots[5] == 1, spots[6] == 1)
    clear_ends(ext)
    clear_ends(ext2)
    ext[OWN_X, OWN_Y, :] = now[...]
    fill_tiles(ext, spots, lambda x: now_lo[x], lambda x: now_hi[x])
    spread_edges(edge, old_lo, old_hi)
    apply_depth(ext, oper, depth, True)

    def emit(x, g, xi, j, value):
        twice = 2.0 * ext[PAD + x, ext_tile(j), :]
        if j in OWN:
            u = twice - prev[x, tile(j), :] + r2[x, tile(j), :] * value
            lap_a[x, tile(j), :] = value
            new_a[x, tile(j), :] = u
        else:
            old, weight, there = (old_lo, r2_lo, has[0]) if j < 0 else (old_hi, r2_hi, has[1])
            u = jnp.where(there, twice - old[x] + weight[x] * value, 0.0)
        ext2[PAD + x, ext_tile(j), :] = u

    laplace(ext, depth, WITH_HALO, emit)
    add_source(spots, wavelet[1], new_a, 0, 0)
    add_source(spots, wavelet[1], ext2, PAD, OWN0, True)
    apply_depth(ext2, oper, depth)

    def emit_b(x, g, xi, j, value):
        lap_b[x, tile(j), :] = value
        new_b[x, tile(j), :] = 2.0 * ext2[PAD + x, ext_tile(j), :] - now[x, tile(j), :] + r2[x, tile(j), :] * value

    laplace(ext2, depth, OWN, emit_b)
    add_source(spots, wavelet[2], new_b, 0, 0)
    send_rows(send_lo, send_hi, lambda x, rows: new_b[x, rows, :])


def late_kernel(spots, turned, r2, r2_lo, r2_hi, oper, mu, late, edge, ext, depth, later, sems):
    copies = unpack(turned, HALF, sems, late, edge, later, ext.at[OWN_X, OWN_Y, :])
    clear_ends(ext)
    for c in copies:
        c.wait()

    def weigh(x):
        ext[PAD + x, OWN_Y, :] = late[x] * r2[x]
        ext[PAD + x, OWN0 - 4 : OWN0, :] = edge[x, 0:4, :] * r2_lo[x, 4:8, :]
        ext[PAD + x, OWN1 : OWN1 + 4, :] = edge[x, 4:8, :] * r2_hi[x, 0:4, :]

    planes(weigh)
    apply_depth(ext, oper, depth)

    def emit(x, g, xi, j, value):
        mu[x, tile(j), :] = 2.0 * late[x, tile(j), :] + value - later[x, tile(j), :]

    laplace(ext, depth, OWN, emit)


def turn_kernel(spots, wavelet, now, prev, r2, oper, part, count, data, lap, mu, ext, depth, new):
    clear_ends(ext)
    no_edges(ext)
    ext[OWN_X, OWN_Y, :] = now[...]
    apply_depth(ext, oper, depth)

    def emit(x, g, xi, j, value):
        new[x, tile(j), :] = 2.0 * ext[PAD + x, ext_tile(j), :] - prev[x, tile(j), :] + r2[x, tile(j), :] * value
        lap[x, tile(j), :] = value

    laplace(ext, depth, OWN, emit)
    add_source(spots, wavelet[3], new, 0, 0)

    def finish(x):
        mu[x] = part[x] + (count[x, 8 : 8 + NYL, :] * new[x] - data[x])

    planes(finish)


def turn_end_kernel(spots, halo_lo, halo_hi, r2, count, lap, mu_in, total, mu, send_lo, send_hi, strip):
    fill_strip(strip, spots, halo_lo, halo_hi)

    def body(x):
        for j in OWN:
            m, value = mu_in[x, tile(j), :], lap[x, tile(j), :]
            if j in (0, 3):
                more = halo_taps(strip, x, j)
                value = value + more
                m = m + count[x, 8 + 8 * j : 16 + 8 * j, :] * (r2[x, tile(j), :] * more)
                (send_hi if j else send_lo)[x] = m
            mu[x, tile(j), :] = m
            total[x, tile(j), :] = m * value

    planes(body)


def back_kernel(spots, late, later, r2, oper, count, data, wave, lap, total_in, total, mu, ext, depth):
    clear_ends(ext)
    no_edges(ext)
    ext[OWN_X, OWN_Y, :] = late[...] * r2[...]
    apply_depth(ext, oper, depth)

    def emit(x, g, xi, j, value):
        wide = slice(8 + 8 * j, 16 + 8 * j)
        m = 2.0 * late[x, tile(j), :] + value - later[x, tile(j), :]
        m = m + (count[x, wide, :] * wave[x, tile(j), :] - data[x, wide, :])
        mu[x, tile(j), :] = m
        total[x, tile(j), :] = total_in[x, tile(j), :] + m * lap[x, tile(j), :]

    laplace(ext, depth, OWN, emit)


def back_end_kernel(
    spots, late, late_lo, late_hi, edge, r2, r2_lo, r2_hi, oper, count, data_a, data_b,
    wave_lo, wave_hi, wave_b, lap_a, lap_b, mu_in, total_in,
    total, mu_a, mu_b, send_lo, send_hi, ext, ext2, depth, old_lo, old_hi, u_lo, u_hi, strip,
):
    has = (spots[5] == 1, spots[6] == 1)
    clear_ends(ext)
    clear_ends(ext2)
    ext[OWN_X, OWN_Y, :] = late[...] * r2[...]
    fill_tiles(ext, spots, lambda x: late_lo[x] * r2_lo[x], lambda x: late_hi[x] * r2_hi[x])
    spread_edges(edge, old_lo, old_hi)
    spread_halos(wave_lo, wave_hi, u_lo, u_hi)
    zeros = jnp.zeros((8, NZ), F32)

    def near(x):
        strip[x, 4:8, :] = ext[PAD + x, OWN0 - 4 : OWN0, :]
        strip[x, 8:16, :] = zeros
        strip[x, 16:20, :] = ext[PAD + x, OWN1 : OWN1 + 4, :]

    planes(near)
    apply_depth(ext, oper, depth, span=(WIDE0, OWN0))
    apply_depth(ext, oper, depth, span=(OWN1, WIDE1))

    def own(x):
        for j in OWN:
            mu, sofar = mu_in[x, tile(j), :], total_in[x, tile(j), :]
            if j in (0, 3):
                more = halo_taps(strip, x, j)
                mu = mu + more
                sofar = sofar + more * lap_a[x, tile(j), :]
            mu_a[x, tile(j), :] = mu
            total[x, tile(j), :] = sofar
            ext2[PAD + x, ext_tile(j), :] = mu * r2[x, tile(j), :]

    planes(own)

    def emit(x, g, xi, j, value):
        wide = slice(8 + 8 * j, 16 + 8 * j)
        close, old, u, weight, there = (
            (late_lo, old_lo, u_lo, r2_lo, has[0]) if j < 0 else (late_hi, old_hi, u_hi, r2_hi, has[1])
        )
        mu = 2.0 * close[x] + value - old[x] + (count[x, wide, :] * u[x] - data_a[x, wide, :])
        ext2[PAD + x, ext_tile(j), :] = jnp.where(there, mu * weight[x], 0.0)

    laplace(ext, depth, (-1, 4), emit)
    apply_depth(ext2, oper, depth)

    def emit_b(x, g, xi, j, value):
        mu = 2.0 * mu_a[x, tile(j), :] + value - late[x, tile(j), :]
        mu = mu + (count[x, 8 + 8 * j : 16 + 8 * j, :] * wave_b[x, tile(j), :] - data_b[x, tile(j), :])
        mu_b[x, tile(j), :] = mu
        total[x, tile(j), :] = total[x, tile(j), :] + mu * lap_b[x, tile(j), :]

    laplace(ext2, depth, OWN, emit_b)
    send_rows(send_lo, send_hi, lambda x, rows: mu_b[x, rows, :] * r2[x, rows, :])


def last_kernel(
    spots, late, later, r2, oper, count, data, wave, lap, total_in, total, ext, depth
):
    first = spots[0]
    clear_ends(ext)
    ext[OWN_X, OWN_Y, :] = late[...] * r2[...]
    no_edges(ext)
    apply_depth(ext, oper, depth)

    def emit(x, g, xi, j, value):
        mu = 2.0 * late[x, tile(j), :] + value - later[x, tile(j), :]
        mu = mu + (count[x, 8 + 8 * j : 16 + 8 * j, :] * wave[x, tile(j), :] - data[x, tile(j), :])
        total[lax.rem(first + g, GROUP), xi, tile(j), :] = total_in[x, tile(j), :] + mu * lap[x, tile(j), :]

    laplace(ext, depth, OWN, emit)


def last_end_kernel(spots, halo_lo, halo_hi, lap, total_in, total, strip):
    fill_strip(strip, spots, halo_lo, halo_hi)
    first = spots[0]

    def body(x):
        slot, xi = lax.rem(first + x // GROUP, GROUP), lax.rem(x, GROUP)
        for j in OWN:
            value = total_in[slot, xi, tile(j), :]
            if j in (0, 3):
                value = value + lap[x, tile(j), :] * halo_taps(strip, x, j)
            total[slot, xi, tile(j), :] = value

    planes(body)


def pack_kernel(now, prev, late, later, out, near, edge, sems):
    order = ((0, now, NOW), (2, late, HALF + NOW), (1, prev, PREV), (3, later, HALF + PREV))
    bring = {f: pltpu.make_async_copy(field, near.at[f], sems.at[f]) for f, field, _ in order}
    for f, _, _ in order:
        bring[f].start()
    none = jnp.zeros((4, NZ), F32)
    sent = []
    for f, _, off in order:
        bring[f].wait()
        for p in range(8):
            sent.append(
                pltpu.make_async_copy(
                    near.at[f, :, NYL * p : NYL * p + NYL, :], out.at[p, :, off : off + NYL, :], sems.at[4 + 8 * f + p]
                )
            )
            sent[-1].start()
        if f % 2 == 0:

            def body(xi, carry):
                for p in range(8):
                    lo = NYL * p
                    edge[f // 2, p, xi, 0:4, :] = near[f, xi, lo - 4 : lo, :] if p > 0 else none
                    edge[f // 2, p, xi, 4:8, :] = near[f, xi, lo + NYL : lo + NYL + 4, :] if p < 7 else none
                return carry

            lax.fori_loop(0, GROUP, body, 0)
            at = f // 2 * HALF + EDGES
            sent.append(pltpu.make_async_copy(edge.at[f // 2], out.at[:, :, at : at + 8, :], sems.at[36 + f // 2]))
            sent[-1].start()
    for c in sent:
        c.wait()


def copy_block(dst, src):
    def body(x, carry):
        dst[x] = src[x]
        return carry

    lax.fori_loop(0, GROUP, body, 0, unroll=4)


def split_shot(me):
    return me // 8, lax.rem(me // 2, 4), lax.rem(me, 2)


def slot_of(start, which):
    return (start + lax.rem(which - start + 32, 8)) // 8


def select_kernel(ids, apertures, piece, other, piece_c, other_c, *outs):
    half, y, core = split_shot(ids[0])
    for k in range(4):
        start = apertures[8 * half + 2 * lax.rem(y + k, 4) + core, 0]
        for j in range(2):
            m = slot_of(start, 2 * y + j)
            row = m // 2
            own_half = lax.rem(m, 2) == half
            own_core = core == j
            for src, same_half, same_core in (
                (piece, True, True),
                (other, False, True),
                (piece_c, True, False),
                (other_c, False, False),
            ):

                @pl.when(jnp.logical_and(own_half == same_half, own_core == same_core))
                def _():
                    copy_block(outs[k].at[j], src.at[row])


def assemble_kernel(ids, apertures, r0, r1, r2, r3, out, send_lo, send_hi):
    _, y, _ = split_shot(ids[0])
    first = apertures[ids[0], 0]
    for k, src in enumerate((r0, r1, r2, r3)):
        for j in range(2):
            at = lax.rem(2 * lax.rem(y - k + 4, 4) + j - first + 32, 8)
            copy_block(out.at[pl.ds(at * GROUP, GROUP)], src.at[j])
    send_tiles(send_lo, send_hi, out)


def receivers_kernel(cells, lines, observed, count, data3, data1, data2, data4):
    zeros = jnp.zeros((NYL, NZ), F32)
    zeros_wide = jnp.zeros((WIDE, NZ), F32)

    def clear(x):
        for d in (count, data3):
            d[x] = zeros_wide
        for d in (data1, data2, data4):
            d[x] = zeros

    planes(clear)
    lanes = lax.broadcasted_iota(jnp.int32, (1, NZ), 1)

    def body(r, carry):
        y = lines[r]

        @pl.when(jnp.logical_and(y >= -8, y < NYL + 8))
        def _():
            cell = cells[r]
            x = cell // (256 * NZ)
            hit = lanes == lax.rem(cell, NZ)
            row = pl.ds(y + 8, 1)
            count[x, row, :] = count[x, row, :] + jnp.where(hit, 1.0, 0.0)
            data3[x, row, :] = data3[x, row, :] + jnp.where(hit, observed[2, r], 0.0)

            @pl.when(jnp.logical_and(y >= 0, y < NYL))
            def _():
                own = pl.ds(y, 1)
                for n, d in ((0, data1), (1, data2), (3, data4)):
                    d[x, own, :] = d[x, own, :] + jnp.where(hit, observed[n, r], 0.0)

        return carry

    lax.fori_loop(0, cells.shape[0], body, 0)


def bins_kernel(ids, apertures, recv, keep, give):
    mine, which = ids[0] // 8, lax.rem(ids[0], 8)
    zeros = jnp.zeros((GROUP, NYL, NZ), F32)
    for i in range(2):
        keep[i] = zeros
        give[i] = zeros
    for t in range(GROUP):
        m = slot_of(apertures[8 * mine + t, 0], which)
        i = m // 2

        @pl.when(lax.rem(m, 2) == mine)
        def _():
            keep[i] = keep[i] + recv[t]

        @pl.when(lax.rem(m, 2) != mine)
        def _():
            give[i] = give[i] + recv[t]


FIELD = jax.ShapeDtypeStruct((NX, NYL, NZ), F32)
WIDE_FIELD = jax.ShapeDtypeStruct((NX, WIDE, NZ), F32)
EDGE = jax.ShapeDtypeStruct((NX // 2, 8, NZ), F32)
TILE = jax.ShapeDtypeStruct((NX, 8, NZ), F32)
BLOCKS = jax.ShapeDtypeStruct((8, GROUP, NYL, NZ), F32)
PAIR = jax.ShapeDtypeStruct((2, GROUP, NYL, NZ), F32)
EXT = pltpu.VMEM((NX + 2 * PAD, ROWS, NZ), F32)
DEPTH = pltpu.VMEM((NX, WIDE, NZ), F32)
FIELD_VMEM = pltpu.VMEM((NX, NYL, NZ), F32)
STRIP = pltpu.VMEM((NX, 24, NZ), F32)
MAIN = 10 << 20
TILE_VMEM = pltpu.VMEM((NX, 8, NZ), F32)


def call(kernel, specs, outs, scratch=(), flops=0, moved=0, out_spec=VMEM, limit=12):
    return pl.pallas_call(
        kernel,
        in_specs=specs,
        out_specs=[out_spec] * len(outs),
        out_shape=outs,
        scratch_shapes=list(scratch),
        compiler_params=pltpu.CompilerParams(vmem_limit_bytes=limit << 20),
        cost_estimate=pl.CostEstimate(flops=flops, bytes_accessed=moved, transcendentals=0),
    )


def per_device(
    courant_squared,
    wave_now,
    wave_prev,
    adj_late,
    adj_later,
    wavelet,
    sources,
    receivers,
    observed,
    apertures,
):
    me = lax.axis_index("shot")
    part = lax.axis_index("sub")
    ids = jnp.stack([me, part]).astype(jnp.int32)
    first = apertures[me, 0]
    oper = jnp.asarray(depth_operator())
    up = [(i, (i + 1) % 8) for i in range(8)]
    down = [((i + 1) % 8, i) for i in range(8)]
    across = [(i, (i + 8) % 16) for i in range(16)]
    chip = [(i, i ^ 1) for i in range(16)]
    halves = [list(range(8)), list(range(8, 16))]

    def along(k):
        return [(8 * h + 2 * y + c, 8 * h + 2 * ((y + k) % 4) + c) for h in range(2) for y in range(4) for c in range(2)]

    def edges(lo, hi):
        return lax.ppermute(hi, "sub", up), lax.ppermute(lo, "sub", down)

    piece = courant_squared[:, 0]
    other = lax.ppermute(piece, "shot", across)
    piece_c = lax.ppermute(piece, "shot", chip)
    other_c = lax.ppermute(other, "shot", chip)
    blocks = call(select_kernel, [SMEM] * 2 + [VMEM] * 4, [PAIR] * 4, moved=2 << 20)(
        ids, apertures, piece, other, piece_c, other_c
    )
    come = [blocks[0]] + [lax.ppermute(blocks[k], "shot", along(k)) for k in (1, 2, 3)]

    (packed,) = call(
        pack_kernel,
        [ANY] * 4,
        [jax.ShapeDtypeStruct((8, GROUP, TURNED, NZ), F32)],
        [
            pltpu.VMEM((4, GROUP, 256, NZ), F32),
            pltpu.VMEM((2, 8, GROUP, 8, NZ), F32),
            pltpu.SemaphoreType.DMA((38,)),
        ],
        moved=9 << 20,
        out_spec=ANY,
        limit=58,
    )(wave_now[0], wave_prev[0], adj_late[0], adj_later[0])
    turned = lax.all_to_all(packed, "sub", 0, 0, tiled=True).reshape(NX, TURNED, NZ)
    r2, *r2_send = call(assemble_kernel, [SMEM] * 2 + [VMEM] * 4, [FIELD, TILE, TILE], moved=2 << 20)(
        ids, apertures, *come
    )
    r2_halo = edges(*r2_send)

    cell = sources[0]
    line = (cell // NZ) % 256 - NYL * part
    spots = jnp.stack(
        [
            first % 8,
            ((line >= 0) & (line < NYL)).astype(jnp.int32),
            cell // (256 * NZ),
            line,
            cell % NZ,
            (part > 0).astype(jnp.int32),
            (part < 7).astype(jnp.int32),
            ((line >= -8) & (line < NYL + 8)).astype(jnp.int32),
        ]
    )
    amounts = wavelet[0]
    cells = receivers[0]
    lines = (cells // NZ) % 256 - NYL * part

    count, data3, data1, data2, data4 = call(
        receivers_kernel, [SMEM] * 3, [WIDE_FIELD, WIDE_FIELD] + [FIELD] * 3, flops=1 << 40, moved=6 << 20
    )(cells, lines, observed[0])
    r2, count = lax.optimization_barrier((r2, count))

    lap0, u1, lo, hi, u0, u0_edge = call(
        first_kernel,
        [SMEM, SMEM, ANY, VMEM, VMEM],
        [FIELD, FIELD, TILE, TILE, FIELD, TILE],
        [EXT, DEPTH, FIELD_VMEM, pltpu.SemaphoreType.DMA((4,))],
        flops=10 << 20,
        moved=8 << 20,
    )(spots, amounts, turned, r2, oper)
    u1_halo = edges(lo, hi)
    part4, mu5, mu5_edge = call(
        late_kernel,
        [SMEM, ANY] + [VMEM] * 4,
        [FIELD, FIELD, TILE],
        [EXT, DEPTH, FIELD_VMEM, pltpu.SemaphoreType.DMA((4,))],
        flops=10 << 20,
        moved=6 << 20,
    )(spots, turned, r2, *r2_halo, oper)
    u1, part4 = lax.optimization_barrier((u1, part4))
    lap1, u2, lap2, u3, lo, hi = call(
        middle_kernel,
        [SMEM, SMEM] + [VMEM] * 9,
        [FIELD] * 4 + [EDGE] * 2,
        [EXT, EXT, DEPTH, TILE_VMEM, TILE_VMEM],
        flops=20 << 20,
        moved=12 << 20,
    )(spots, amounts, u1, *u1_halo, u0, u0_edge, r2, *r2_halo, oper)
    u3_halo = edges(lo, hi)
    lap3, mu4 = call(
        turn_kernel,
        [SMEM, SMEM] + [VMEM] * 7,
        [FIELD, FIELD],
        [EXT, DEPTH, FIELD_VMEM],
        flops=MAIN,
        moved=8 << 20,
    )(spots, amounts, u3, u2, r2, oper, part4, count, data4)
    total, mu4, lo, hi = call(
        turn_end_kernel, [SMEM] + [VMEM] * 6, [FIELD, FIELD, TILE, TILE], [STRIP], flops=1 << 20, moved=4 << 20
    )(spots, *u3_halo, r2, count, lap3, mu4)
    mu4_halo = edges(lo, hi)
    total, mu3 = call(
        back_kernel, [SMEM] + [VMEM] * 9, [FIELD, FIELD], [EXT, DEPTH], flops=MAIN, moved=8 << 20
    )(spots, mu4, mu5, r2, oper, count, data3, u3, lap2, total)
    total, mu3, mu2, lo, hi = call(
        back_end_kernel,
        [SMEM] + [VMEM] * 18,
        [FIELD] * 3 + [EDGE] * 2,
        [EXT, EXT, DEPTH] + [TILE_VMEM] * 4 + [STRIP],
        flops=20 << 20,
        moved=16 << 20,
    )(
        spots, mu4, *mu4_halo, mu5_edge, r2, *r2_halo, oper, count, data3, data2,
        *u3_halo, u2, lap2, lap1, mu3, total,
    )
    mu2_halo = edges(lo, hi)
    (total,) = call(last_kernel, [SMEM] + [VMEM] * 9, [BLOCKS], [EXT, DEPTH], flops=MAIN, moved=8 << 20)(
        spots, mu2, mu3, r2, oper, count, data1, u1, lap0, total
    )
    (total,) = call(last_end_kernel, [SMEM] + [VMEM] * 4, [BLOCKS], [STRIP], flops=1 << 20, moved=3 << 20)(
        spots, *mu2_halo, lap0, total
    )

    recv = lax.all_to_all(total, "shot", 0, 0, axis_index_groups=halves, tiled=True)
    keep, give = call(bins_kernel, [SMEM, SMEM, VMEM], [PAIR, PAIR], moved=2 << 20)(ids, apertures, recv)
    result = keep + lax.ppermute(give, "shot", across)
    return result[:, None]


def solution(mesh):
    in_specs = (
        P(None, "shot", None, "sub", None),
        P("shot", "sub", None, None),
        P("shot", "sub", None, None),
        P("shot", "sub", None, None),
        P("shot", "sub", None, None),
        P("shot", None),
        P("shot"),
        P("shot", None),
        P("shot", None, None),
        P(),
    )
    out_specs = P(None, "shot", None, "sub", None)
    return jax.shard_map(
        per_device, mesh=mesh, in_specs=in_specs, out_specs=out_specs, check_vma=False
    )
```

```python
import functools

import jax
import jax.numpy as jnp
import ml_dtypes
import numpy as np
from jax import lax
from jax.experimental import pallas as pl
from jax.experimental.pallas import tpu as pltpu
from jax.sharding import PartitionSpec as P

STEPS = 4
STENCIL = (-205.0 / 72.0, 8.0 / 5.0, -1.0 / 5.0, 8.0 / 315.0, -1.0 / 560.0)
F32 = jnp.float32
BF16 = jnp.bfloat16
SMEM = pl.BlockSpec(memory_space=pltpu.SMEM)
VMEM = pl.BlockSpec(memory_space=pltpu.VMEM)
ANY = pl.BlockSpec(memory_space=pltpu.HBM)
NX, NYL, NZ = 64, 32, 128
GROUP = 8
PAD = 4
ROWS = 64
OWN0, OWN1 = 16, 48
WIDE0, WIDE1 = 8, 56
WIDE = WIDE1 - WIDE0
OWN_X, OWN_Y = slice(PAD, PAD + NX), slice(OWN0, OWN1)
CHUNK = 16
OWN, WITH_HALO = range(4), range(-1, 5)


def depth_operator():
    band = np.zeros((NZ, NZ), np.float32)
    for i in range(NZ):
        band[i, i] = np.float32(3.0 * STENCIL[0])
        for k in range(1, 5):
            for j in (i - k, i + k):
                if 0 <= j < NZ:
                    band[j, i] = np.float32(STENCIL[k])
    high = band.astype(ml_dtypes.bfloat16)
    low = (band - high.astype(np.float32)).astype(ml_dtypes.bfloat16)
    zero = np.zeros_like(high)
    return np.block([[high, low], [high, zero]])


def clear_ends(ext):
    zeros = jnp.zeros((PAD, ROWS, NZ), F32)
    ext[0:PAD] = zeros
    ext[PAD + NX : 2 * PAD + NX] = zeros


def planes(body):
    def step(x, carry):
        body(x)
        return carry

    lax.fori_loop(0, NX, step, 0, unroll=16)


def fill_edges(ext, spots, halo_lo, halo_hi):
    has_lo, has_hi = spots[5] == 1, spots[6] == 1

    def body(t, carry):
        lo = jnp.where(has_lo, halo_lo[t], 0.0)
        hi = jnp.where(has_hi, halo_hi[t], 0.0)
        for half in range(2):
            x = PAD + 2 * t + half
            ext[x, OWN0 - 4 : OWN0, :] = lo[4 * half : 4 * half + 4]
            ext[x, OWN1 : OWN1 + 4, :] = hi[4 * half : 4 * half + 4]
        return carry

    lax.fori_loop(0, NX // 2, body, 0, unroll=8)


def fill_tiles(ext, spots, lo, hi):
    has_lo, has_hi = spots[5] == 1, spots[6] == 1

    def body(x):
        ext[PAD + x, WIDE0:OWN0, :] = jnp.where(has_lo, lo(x), 0.0)
        ext[PAD + x, OWN1:WIDE1, :] = jnp.where(has_hi, hi(x), 0.0)

    planes(body)


def fill_ring(ext, edge):
    def body(x):
        ext[PAD + x, OWN0 - 4 : OWN0, :] = edge[x, 0:4, :]
        ext[PAD + x, OWN1 : OWN1 + 4, :] = edge[x, 4:8, :]

    planes(body)


def no_edges(ext):
    zeros = jnp.zeros((4, NZ), F32)

    def body(x):
        ext[PAD + x, OWN0 - 4 : OWN0, :] = zeros
        ext[PAD + x, OWN1 : OWN1 + 4, :] = zeros

    planes(body)


def halo_taps(strip, x, j):
    way = -1 if j == 0 else 1
    acc = None
    for k in range(1, 5):
        term = STENCIL[k] * strip[x, 8 + way * k : 16 + way * k, :]
        acc = term if acc is None else acc + term
    return acc


def fill_strip(strip, spots, halo_lo, halo_hi):
    has_lo, has_hi = spots[5] == 1, spots[6] == 1
    zeros = jnp.zeros((8, NZ), F32)

    def body(t, carry):
        lo = jnp.where(has_lo, halo_lo[t], 0.0)
        hi = jnp.where(has_hi, halo_hi[t], 0.0)
        for half in range(2):
            strip[2 * t + half, 4:8, :] = lo[4 * half : 4 * half + 4]
            strip[2 * t + half, 8:16, :] = zeros
            strip[2 * t + half, 16:20, :] = hi[4 * half : 4 * half + 4]
        return carry

    lax.fori_loop(0, NX // 2, body, 0, unroll=8)


def apply_depth(ext, oper, depth, wide=False, span=None):
    r0, r1 = span or ((WIDE0, WIDE1) if wide else (OWN0, OWN1))
    n = CHUNK
    for at in range(0, NX, n):
        rows = ext[PAD + at : PAD + at + n, r0:r1, :].reshape(n * (r1 - r0), NZ)
        high = rows.astype(BF16)
        low = (rows - high.astype(F32)).astype(BF16)
        prod = jnp.dot(jnp.concatenate([high, low], axis=1), oper[...], preferred_element_type=F32)
        depth[at : at + n, r0 - WIDE0 : r1 - WIDE0, :] = (prod[:, :NZ] + prod[:, NZ:]).reshape(n, r1 - r0, NZ)


def laplace(ext, depth, tiles, emit):
    def body(g, carry):
        base = PAD + g * GROUP
        for j in tiles:
            r0 = OWN0 + 8 * j
            col = [ext[base - PAD + i, r0 : r0 + 8, :] for i in range(GROUP + 2 * PAD)]
            for xi in range(GROUP):
                acc = depth[g * GROUP + xi, r0 - WIDE0 : r0 - WIDE0 + 8, :]
                for k in range(1, 5):
                    beside = (
                        col[xi + PAD + k]
                        + col[xi + PAD - k]
                        + (
                            ext[base + xi, r0 + k : r0 + k + 8, :]
                            + ext[base + xi, r0 - k : r0 - k + 8, :]
                        )
                    )
                    acc = acc + STENCIL[k] * beside
                emit(g * GROUP + xi, g, xi, j, acc)
        return carry

    lax.fori_loop(0, NX // GROUP, body, 0)


def tile(j):
    return slice(8 * j, 8 * j + 8)


def ext_tile(j):
    return slice(OWN0 + 8 * j, OWN0 + 8 * j + 8)


def send_rows(send_lo, send_hi, read):
    def body(t, carry):
        for half in range(2):
            send_lo[t, 4 * half : 4 * half + 4, :] = read(2 * t + half, slice(0, 4))
            send_hi[t, 4 * half : 4 * half + 4, :] = read(2 * t + half, slice(NYL - 4, NYL))
        return carry

    lax.fori_loop(0, NX // 2, body, 0, unroll=8)


def send_tiles(send_lo, send_hi, field):
    def body(x):
        send_lo[x] = field[x, 0:8, :]
        send_hi[x] = field[x, NYL - 8 : NYL, :]

    planes(body)


def add_source(spots, amount, ref, x0, y0, wide=False):
    @pl.when(spots[7 if wide else 1] == 1)
    def _():
        x, y, z = x0 + spots[2], y0 + spots[3], spots[4]
        lanes = lax.broadcasted_iota(jnp.int32, (1, NZ), 1)
        row = ref[x, pl.ds(y, 1), :]
        ref[x, pl.ds(y, 1), :] = row + jnp.where(lanes == z, amount, 0.0)


NOW, PREV, EDGES, HALF, TURNED = 0, 32, 64, 72, 144


def unpack(turned, base, sems, now, edge, prev, extra):
    copies = []
    for n, (off, rows, dst) in enumerate(
        ((NOW, NYL, now), (EDGES, 8, edge), (PREV, NYL, prev), (NOW, NYL, extra))
    ):
        copies.append(pltpu.make_async_copy(turned.at[:, base + off : base + off + rows, :], dst, sems.at[n]))
    for c in copies:
        c.start()
    return copies


def first_kernel(spots, wavelet, turned, r2, oper, lap, new, send_lo, send_hi, now, edge, ext, depth, prev, sems):
    copies = unpack(turned, 0, sems, ext.at[OWN_X, OWN_Y, :], edge, prev, now)
    clear_ends(ext)
    for c in copies[:3]:
        c.wait()
    fill_ring(ext, edge)
    apply_depth(ext, oper, depth)

    def emit(x, g, xi, j, value):
        lap[x, tile(j), :] = value
        new[x, tile(j), :] = 2.0 * ext[PAD + x, ext_tile(j), :] - prev[x, tile(j), :] + r2[x, tile(j), :] * value

    laplace(ext, depth, OWN, emit)
    add_source(spots, wavelet[0], new, 0, 0)
    send_tiles(send_lo, send_hi, new)
    copies[3].wait()


def spread_edges(edge, lo, hi):
    def body(x):
        lo[x, 4:8, :] = edge[x, 0:4, :]
        hi[x, 0:4, :] = edge[x, 4:8, :]

    planes(body)


def spread_halos(halo_lo, halo_hi, lo, hi):
    def body(t, carry):
        for half in range(2):
            lo[2 * t + half, 4:8, :] = halo_lo[t, 4 * half : 4 * half + 4, :]
            hi[2 * t + half, 0:4, :] = halo_hi[t, 4 * half : 4 * half + 4, :]
        return carry

    lax.fori_loop(0, NX // 2, body, 0, unroll=8)


def middle_kernel(
    spots, wavelet, now, now_lo, now_hi, prev, edge, r2, r2_lo, r2_hi, oper,
    lap_a, new_a, lap_b, new_b, send_lo, send_hi, ext, ext2, depth, old_lo, old_hi,
):
    has = (spots[5] == 1, spots[6] == 1)
    clear_ends(ext)
    clear_ends(ext2)
    ext[OWN_X, OWN_Y, :] = now[...]
    fill_tiles(ext, spots, lambda x: now_lo[x], lambda x: now_hi[x])
    spread_edges(edge, old_lo, old_hi)
    apply_depth(ext, oper, depth, True)

    def emit(x, g, xi, j, value):
        twice = 2.0 * ext[PAD + x, ext_tile(j), :]
        if j in OWN:
            u = twice - prev[x, tile(j), :] + r2[x, tile(j), :] * value
            lap_a[x, tile(j), :] = value
            new_a[x, tile(j), :] = u
        else:
            old, weight, there = (old_lo, r2_lo, has[0]) if j < 0 else (old_hi, r2_hi, has[1])
            u = jnp.where(there, twice - old[x] + weight[x] * value, 0.0)
        ext2[PAD + x, ext_tile(j), :] = u

    laplace(ext, depth, WITH_HALO, emit)
    add_source(spots, wavelet[1], new_a, 0, 0)
    add_source(spots, wavelet[1], ext2, PAD, OWN0, True)
    apply_depth(ext2, oper, depth)

    def emit_b(x, g, xi, j, value):
        lap_b[x, tile(j), :] = value
        new_b[x, tile(j), :] = 2.0 * ext2[PAD + x, ext_tile(j), :] - now[x, tile(j), :] + r2[x, tile(j), :] * value

    laplace(ext2, depth, OWN, emit_b)
    add_source(spots, wavelet[2], new_b, 0, 0)
    send_rows(send_lo, send_hi, lambda x, rows: new_b[x, rows, :])


def late_kernel(spots, turned, r2, r2_lo, r2_hi, oper, mu, late, edge, ext, depth, later, sems):
    copies = unpack(turned, HALF, sems, late, edge, later, ext.at[OWN_X, OWN_Y, :])
    clear_ends(ext)
    for c in copies:
        c.wait()

    def weigh(x):
        ext[PAD + x, OWN_Y, :] = late[x] * r2[x]
        ext[PAD + x, OWN0 - 4 : OWN0, :] = edge[x, 0:4, :] * r2_lo[x, 4:8, :]
        ext[PAD + x, OWN1 : OWN1 + 4, :] = edge[x, 4:8, :] * r2_hi[x, 0:4, :]

    planes(weigh)
    apply_depth(ext, oper, depth)

    def emit(x, g, xi, j, value):
        mu[x, tile(j), :] = 2.0 * late[x, tile(j), :] + value - later[x, tile(j), :]

    laplace(ext, depth, OWN, emit)


def turn_kernel(spots, wavelet, now, prev, r2, oper, part, count, data, lap, mu, ext, depth, new):
    clear_ends(ext)
    no_edges(ext)
    ext[OWN_X, OWN_Y, :] = now[...]
    apply_depth(ext, oper, depth)

    def emit(x, g, xi, j, value):
        new[x, tile(j), :] = 2.0 * ext[PAD + x, ext_tile(j), :] - prev[x, tile(j), :] + r2[x, tile(j), :] * value
        lap[x, tile(j), :] = value

    laplace(ext, depth, OWN, emit)
    add_source(spots, wavelet[3], new, 0, 0)

    def finish(x):
        mu[x] = part[x] + (count[x, 8 : 8 + NYL, :] * new[x] - data[x])

    planes(finish)


def turn_end_kernel(spots, halo_lo, halo_hi, r2, count, lap, mu_in, total, mu, send_lo, send_hi, strip):
    fill_strip(strip, spots, halo_lo, halo_hi)

    def body(x):
        for j in OWN:
            m, value = mu_in[x, tile(j), :], lap[x, tile(j), :]
            if j in (0, 3):
                more = halo_taps(strip, x, j)
                value = value + more
                m = m + count[x, 8 + 8 * j : 16 + 8 * j, :] * (r2[x, tile(j), :] * more)
                (send_hi if j else send_lo)[x] = m
            mu[x, tile(j), :] = m
            total[x, tile(j), :] = m * value

    planes(body)


def back_kernel(spots, late, later, r2, oper, count, data, wave, lap, total_in, total, mu, ext, depth):
    clear_ends(ext)
    no_edges(ext)
    ext[OWN_X, OWN_Y, :] = late[...] * r2[...]
    apply_depth(ext, oper, depth)

    def emit(x, g, xi, j, value):
        wide = slice(8 + 8 * j, 16 + 8 * j)
        m = 2.0 * late[x, tile(j), :] + value - later[x, tile(j), :]
        m = m + (count[x, wide, :] * wave[x, tile(j), :] - data[x, wide, :])
        mu[x, tile(j), :] = m
        total[x, tile(j), :] = total_in[x, tile(j), :] + m * lap[x, tile(j), :]

    laplace(ext, depth, OWN, emit)


def back_end_kernel(
    spots, late, late_lo, late_hi, edge, r2, r2_lo, r2_hi, oper, count, data_a, data_b,
    wave_lo, wave_hi, wave_b, lap_a, lap_b, mu_in, total_in,
    total, mu_a, mu_b, send_lo, send_hi, ext, ext2, depth, old_lo, old_hi, u_lo, u_hi, strip,
):
    has = (spots[5] == 1, spots[6] == 1)
    clear_ends(ext)
    clear_ends(ext2)
    ext[OWN_X, OWN_Y, :] = late[...] * r2[...]
    fill_tiles(ext, spots, lambda x: late_lo[x] * r2_lo[x], lambda x: late_hi[x] * r2_hi[x])
    spread_edges(edge, old_lo, old_hi)
    spread_halos(wave_lo, wave_hi, u_lo, u_hi)
    zeros = jnp.zeros((8, NZ), F32)

    def near(x):
        strip[x, 4:8, :] = ext[PAD + x, OWN0 - 4 : OWN0, :]
        strip[x, 8:16, :] = zeros
        strip[x, 16:20, :] = ext[PAD + x, OWN1 : OWN1 + 4, :]

    planes(near)
    apply_depth(ext, oper, depth, span=(WIDE0, OWN0))
    apply_depth(ext, oper, depth, span=(OWN1, WIDE1))

    def own(x):
        for j in OWN:
            mu, sofar = mu_in[x, tile(j), :], total_in[x, tile(j), :]
            if j in (0, 3):
                more = halo_taps(strip, x, j)
                mu = mu + more
                sofar = sofar + more * lap_a[x, tile(j), :]
            mu_a[x, tile(j), :] = mu
            total[x, tile(j), :] = sofar
            ext2[PAD + x, ext_tile(j), :] = mu * r2[x, tile(j), :]

    planes(own)

    def emit(x, g, xi, j, value):
        wide = slice(8 + 8 * j, 16 + 8 * j)
        close, old, u, weight, there = (
            (late_lo, old_lo, u_lo, r2_lo, has[0]) if j < 0 else (late_hi, old_hi, u_hi, r2_hi, has[1])
        )
        mu = 2.0 * close[x] + value - old[x] + (count[x, wide, :] * u[x] - data_a[x, wide, :])
        ext2[PAD + x, ext_tile(j), :] = jnp.where(there, mu * weight[x], 0.0)

    laplace(ext, depth, (-1, 4), emit)
    apply_depth(ext2, oper, depth)

    def emit_b(x, g, xi, j, value):
        mu = 2.0 * mu_a[x, tile(j), :] + value - late[x, tile(j), :]
        mu = mu + (count[x, 8 + 8 * j : 16 + 8 * j, :] * wave_b[x, tile(j), :] - data_b[x, tile(j), :])
        mu_b[x, tile(j), :] = mu
        total[x, tile(j), :] = total[x, tile(j), :] + mu * lap_b[x, tile(j), :]

    laplace(ext2, depth, OWN, emit_b)
    send_rows(send_lo, send_hi, lambda x, rows: mu_b[x, rows, :] * r2[x, rows, :])


def last_kernel(
    spots, late, later, r2, oper, count, data, wave, lap, total_in, total, ext, depth
):
    clear_ends(ext)
    ext[OWN_X, OWN_Y, :] = late[...] * r2[...]
    no_edges(ext)
    apply_depth(ext, oper, depth)

    def emit(x, g, xi, j, value):
        mu = 2.0 * late[x, tile(j), :] + value - later[x, tile(j), :]
        mu = mu + (count[x, 8 + 8 * j : 16 + 8 * j, :] * wave[x, tile(j), :] - data[x, tile(j), :])
        total[x, tile(j), :] = total_in[x, tile(j), :] + mu * lap[x, tile(j), :]

    laplace(ext, depth, OWN, emit)


def last_end_kernel(ids, spots, halo_lo, halo_hi, lap, total, *rest):
    outs, strip = rest[:8], rest[8]
    fill_strip(strip, spots, halo_lo, halo_hi)
    _, y, core = split_shot(ids[0])
    for k in range(4):
        for side in range(2):
            cls = 2 * lax.rem(y + k, 4) + (core if side == 0 else 1 - core)
            g = lax.rem(cls - spots[0] + GROUP, GROUP)
            out = outs[2 * k + side]
            for xi in range(GROUP):
                x = g * GROUP + xi
                for j in OWN:
                    value = total[x, tile(j), :]
                    if j in (0, 3):
                        value = value + lap[x, tile(j), :] * halo_taps(strip, x, j)
                    out[xi, tile(j), :] = value


def pack_kernel(now, prev, late, later, out, near, edge, sems):
    order = ((0, now, NOW), (2, late, HALF + NOW), (1, prev, PREV), (3, later, HALF + PREV))
    bring = {f: pltpu.make_async_copy(field, near.at[f], sems.at[f]) for f, field, _ in order}
    for f, _, _ in order:
        bring[f].start()
    none = jnp.zeros((4, NZ), F32)
    sent = []
    for f, _, off in order:
        bring[f].wait()
        for p in range(8):
            sent.append(
                pltpu.make_async_copy(
                    near.at[f, :, NYL * p : NYL * p + NYL, :], out.at[p, :, off : off + NYL, :], sems.at[4 + 8 * f + p]
                )
            )
            sent[-1].start()
        if f % 2 == 0:

            def body(xi, carry):
                for p in range(8):
                    lo = NYL * p
                    edge[f // 2, p, xi, 0:4, :] = near[f, xi, lo - 4 : lo, :] if p > 0 else none
                    edge[f // 2, p, xi, 4:8, :] = near[f, xi, lo + NYL : lo + NYL + 4, :] if p < 7 else none
                return carry

            lax.fori_loop(0, GROUP, body, 0)
            at = f // 2 * HALF + EDGES
            sent.append(pltpu.make_async_copy(edge.at[f // 2], out.at[:, :, at : at + 8, :], sems.at[36 + f // 2]))
            sent[-1].start()
    for c in sent:
        c.wait()


def copy_block(dst, src):
    def body(x, carry):
        dst[x] = src[x]
        return carry

    lax.fori_loop(0, GROUP, body, 0, unroll=4)


def split_shot(me):
    return me // 8, lax.rem(me // 2, 4), lax.rem(me, 2)


def slot_of(start, which):
    return (start + lax.rem(which - start + 32, 8)) // 8


def select_kernel(ids, apertures, piece, other, piece_c, other_c, *outs):
    half, y, core = split_shot(ids[0])
    for k in range(4):
        start = apertures[8 * half + 2 * lax.rem(y + k, 4) + core, 0]
        for j in range(2):
            m = slot_of(start, 2 * y + j)
            row = m // 2
            own_half = lax.rem(m, 2) == half
            own_core = core == j
            for src, same_half, same_core in (
                (piece, True, True),
                (other, False, True),
                (piece_c, True, False),
                (other_c, False, False),
            ):

                @pl.when(jnp.logical_and(own_half == same_half, own_core == same_core))
                def _():
                    copy_block(outs[k].at[j], src.at[row])


def assemble_kernel(ids, apertures, r0, r1, r2, r3, out, send_lo, send_hi):
    _, y, _ = split_shot(ids[0])
    first = apertures[ids[0], 0]
    for k, src in enumerate((r0, r1, r2, r3)):
        for j in range(2):
            at = lax.rem(2 * lax.rem(y - k + 4, 4) + j - first + 32, 8)
            copy_block(out.at[pl.ds(at * GROUP, GROUP)], src.at[j])
    send_tiles(send_lo, send_hi, out)


def receivers_kernel(cells, lines, observed, count, data3, data1, data2, data4):
    zeros = jnp.zeros((NYL, NZ), F32)
    zeros_wide = jnp.zeros((WIDE, NZ), F32)

    def clear(x):
        for d in (count, data3):
            d[x] = zeros_wide
        for d in (data1, data2, data4):
            d[x] = zeros

    planes(clear)
    lanes = lax.broadcasted_iota(jnp.int32, (1, NZ), 1)

    def body(r, carry):
        y = lines[r]

        @pl.when(jnp.logical_and(y >= -8, y < NYL + 8))
        def _():
            cell = cells[r]
            x = cell // (256 * NZ)
            hit = lanes == lax.rem(cell, NZ)
            row = pl.ds(y + 8, 1)
            count[x, row, :] = count[x, row, :] + jnp.where(hit, 1.0, 0.0)
            data3[x, row, :] = data3[x, row, :] + jnp.where(hit, observed[2, r], 0.0)

            @pl.when(jnp.logical_and(y >= 0, y < NYL))
            def _():
                own = pl.ds(y, 1)
                for n, d in ((0, data1), (1, data2), (3, data4)):
                    d[x, own, :] = d[x, own, :] + jnp.where(hit, observed[n, r], 0.0)

        return carry

    lax.fori_loop(0, cells.shape[0], body, 0)


def bins_kernel(ids, apertures, *rest):
    recv, (keep, give) = rest[:8], rest[8:]
    mine, y, core = split_shot(ids[0])
    which = lax.rem(ids[0], 8)
    zeros = jnp.zeros((GROUP, NYL, NZ), F32)
    for i in range(2):
        keep[i] = zeros
        give[i] = zeros
    for t in range(GROUP):
        shot = 8 * mine + 2 * lax.rem(y - t // 2 + 4, 4) + (core if t % 2 == 0 else 1 - core)
        m = slot_of(apertures[shot, 0], which)
        i = m // 2

        @pl.when(lax.rem(m, 2) == mine)
        def _():
            keep[i] = keep[i] + recv[t][...]

        @pl.when(lax.rem(m, 2) != mine)
        def _():
            give[i] = give[i] + recv[t][...]


FIELD = jax.ShapeDtypeStruct((NX, NYL, NZ), F32)
WIDE_FIELD = jax.ShapeDtypeStruct((NX, WIDE, NZ), F32)
EDGE = jax.ShapeDtypeStruct((NX // 2, 8, NZ), F32)
TILE = jax.ShapeDtypeStruct((NX, 8, NZ), F32)
BLOCK = jax.ShapeDtypeStruct((GROUP, NYL, NZ), F32)
PAIR = jax.ShapeDtypeStruct((2, GROUP, NYL, NZ), F32)
EXT = pltpu.VMEM((NX + 2 * PAD, ROWS, NZ), F32)
DEPTH = pltpu.VMEM((NX, WIDE, NZ), F32)
FIELD_VMEM = pltpu.VMEM((NX, NYL, NZ), F32)
STRIP = pltpu.VMEM((NX, 24, NZ), F32)
MAIN = 10 << 20
TILE_VMEM = pltpu.VMEM((NX, 8, NZ), F32)


def call(kernel, specs, outs, scratch=(), flops=0, moved=0, out_spec=VMEM, limit=12):
    return pl.pallas_call(
        kernel,
        in_specs=specs,
        out_specs=[out_spec] * len(outs),
        out_shape=outs,
        scratch_shapes=list(scratch),
        compiler_params=pltpu.CompilerParams(vmem_limit_bytes=limit << 20),
        cost_estimate=pl.CostEstimate(flops=flops, bytes_accessed=moved, transcendentals=0),
    )


def per_device(
    courant_squared,
    wave_now,
    wave_prev,
    adj_late,
    adj_later,
    wavelet,
    sources,
    receivers,
    observed,
    apertures,
):
    me = lax.axis_index("shot")
    part = lax.axis_index("sub")
    ids = jnp.stack([me, part]).astype(jnp.int32)
    first = apertures[me, 0]
    oper = jnp.asarray(depth_operator())
    up = [(i, (i + 1) % 8) for i in range(8)]
    down = [((i + 1) % 8, i) for i in range(8)]
    across = [(i, (i + 8) % 16) for i in range(16)]
    chip = [(i, i ^ 1) for i in range(16)]

    def along(k):
        return [(8 * h + 2 * y + c, 8 * h + 2 * ((y + k) % 4) + c) for h in range(2) for y in range(4) for c in range(2)]

    def edges(lo, hi):
        return lax.ppermute(hi, "sub", up), lax.ppermute(lo, "sub", down)

    piece = courant_squared[:, 0]
    other = lax.ppermute(piece, "shot", across)
    piece_c = lax.ppermute(piece, "shot", chip)
    other_c = lax.ppermute(other, "shot", chip)
    blocks = call(select_kernel, [SMEM] * 2 + [VMEM] * 4, [PAIR] * 4, moved=2 << 20)(
        ids, apertures, piece, other, piece_c, other_c
    )
    come = [blocks[0]] + [lax.ppermute(blocks[k], "shot", along(k)) for k in (1, 2, 3)]

    (packed,) = call(
        pack_kernel,
        [ANY] * 4,
        [jax.ShapeDtypeStruct((8, GROUP, TURNED, NZ), F32)],
        [
            pltpu.VMEM((4, GROUP, 256, NZ), F32),
            pltpu.VMEM((2, 8, GROUP, 8, NZ), F32),
            pltpu.SemaphoreType.DMA((38,)),
        ],
        moved=9 << 20,
        out_spec=ANY,
        limit=58,
    )(wave_now[0], wave_prev[0], adj_late[0], adj_later[0])
    turned = lax.all_to_all(packed, "sub", 0, 0, tiled=True).reshape(NX, TURNED, NZ)
    r2, *r2_send = call(assemble_kernel, [SMEM] * 2 + [VMEM] * 4, [FIELD, TILE, TILE], moved=2 << 20)(
        ids, apertures, *come
    )
    r2_halo = edges(*r2_send)

    cell = sources[0]
    line = (cell // NZ) % 256 - NYL * part
    spots = jnp.stack(
        [
            first % 8,
            ((line >= 0) & (line < NYL)).astype(jnp.int32),
            cell // (256 * NZ),
            line,
            cell % NZ,
            (part > 0).astype(jnp.int32),
            (part < 7).astype(jnp.int32),
            ((line >= -8) & (line < NYL + 8)).astype(jnp.int32),
        ]
    )
    amounts = wavelet[0]
    cells = receivers[0]
    lines = (cells // NZ) % 256 - NYL * part

    count, data3, data1, data2, data4 = call(
        receivers_kernel, [SMEM] * 3, [WIDE_FIELD, WIDE_FIELD] + [FIELD] * 3, flops=1 << 40, moved=6 << 20
    )(cells, lines, observed[0])
    r2, count = lax.optimization_barrier((r2, count))

    lap0, u1, lo, hi, u0, u0_edge = call(
        first_kernel,
        [SMEM, SMEM, ANY, VMEM, VMEM],
        [FIELD, FIELD, TILE, TILE, FIELD, TILE],
        [EXT, DEPTH, FIELD_VMEM, pltpu.SemaphoreType.DMA((4,))],
        flops=10 << 20,
        moved=8 << 20,
    )(spots, amounts, turned, r2, oper)
    u1_halo = edges(lo, hi)
    part4, mu5, mu5_edge = call(
        late_kernel,
        [SMEM, ANY] + [VMEM] * 4,
        [FIELD, FIELD, TILE],
        [EXT, DEPTH, FIELD_VMEM, pltpu.SemaphoreType.DMA((4,))],
        flops=10 << 20,
        moved=6 << 20,
    )(spots, turned, r2, *r2_halo, oper)
    u1, part4 = lax.optimization_barrier((u1, part4))
    lap1, u2, lap2, u3, lo, hi = call(
        middle_kernel,
        [SMEM, SMEM] + [VMEM] * 9,
        [FIELD] * 4 + [EDGE] * 2,
        [EXT, EXT, DEPTH, TILE_VMEM, TILE_VMEM],
        flops=20 << 20,
        moved=12 << 20,
    )(spots, amounts, u1, *u1_halo, u0, u0_edge, r2, *r2_halo, oper)
    u3_halo = edges(lo, hi)
    lap3, mu4 = call(
        turn_kernel,
        [SMEM, SMEM] + [VMEM] * 7,
        [FIELD, FIELD],
        [EXT, DEPTH, FIELD_VMEM],
        flops=MAIN,
        moved=8 << 20,
    )(spots, amounts, u3, u2, r2, oper, part4, count, data4)
    total, mu4, lo, hi = call(
        turn_end_kernel, [SMEM] + [VMEM] * 6, [FIELD, FIELD, TILE, TILE], [STRIP], flops=1 << 20, moved=4 << 20
    )(spots, *u3_halo, r2, count, lap3, mu4)
    mu4_halo = edges(lo, hi)
    total, mu3 = call(
        back_kernel, [SMEM] + [VMEM] * 9, [FIELD, FIELD], [EXT, DEPTH], flops=MAIN, moved=8 << 20
    )(spots, mu4, mu5, r2, oper, count, data3, u3, lap2, total)
    total, mu3, mu2, lo, hi = call(
        back_end_kernel,
        [SMEM] + [VMEM] * 18,
        [FIELD] * 3 + [EDGE] * 2,
        [EXT, EXT, DEPTH] + [TILE_VMEM] * 4 + [STRIP],
        flops=20 << 20,
        moved=16 << 20,
    )(
        spots, mu4, *mu4_halo, mu5_edge, r2, *r2_halo, oper, count, data3, data2,
        *u3_halo, u2, lap2, lap1, mu3, total,
    )
    mu2_halo = edges(lo, hi)
    (total,) = call(last_kernel, [SMEM] + [VMEM] * 9, [FIELD], [EXT, DEPTH], flops=MAIN, moved=8 << 20)(
        spots, mu2, mu3, r2, oper, count, data1, u1, lap0, total
    )
    sent = call(last_end_kernel, [SMEM] * 2 + [VMEM] * 4, [BLOCK] * 8, [STRIP], flops=1 << 20, moved=3 << 20)(
        ids, spots, *mu2_halo, lap0, total
    )

    recv = []
    for k in range(4):
        mine, others = sent[2 * k], lax.ppermute(sent[2 * k + 1], "shot", chip)
        if k:
            mine, others = lax.ppermute(mine, "shot", along(k)), lax.ppermute(others, "shot", along(k))
        recv += [mine, others]
    keep, give = call(bins_kernel, [SMEM] * 2 + [VMEM] * 8, [PAIR, PAIR], moved=2 << 20)(ids, apertures, *recv)
    result = keep + lax.ppermute(give, "shot", across)
    return result[:, None]


def solution(mesh):
    in_specs = (
        P(None, "shot", None, "sub", None),
        P("shot", "sub", None, None),
        P("shot", "sub", None, None),
        P("shot", "sub", None, None),
        P("shot", "sub", None, None),
        P("shot", None),
        P("shot"),
        P("shot", None),
        P("shot", None, None),
        P(),
    )
    out_specs = P(None, "shot", None, "sub", None)
    return jax.shard_map(
        per_device, mesh=mesh, in_specs=in_specs, out_specs=out_specs, check_vma=False
    )
```

```python
import functools

import jax
import jax.numpy as jnp
import ml_dtypes
import numpy as np
from jax import lax
from jax.experimental import pallas as pl
from jax.experimental.pallas import tpu as pltpu
from jax.sharding import PartitionSpec as P

STEPS = 4
STENCIL = (-205.0 / 72.0, 8.0 / 5.0, -1.0 / 5.0, 8.0 / 315.0, -1.0 / 560.0)
F32 = jnp.float32
BF16 = jnp.bfloat16
SMEM = pl.BlockSpec(memory_space=pltpu.SMEM)
VMEM = pl.BlockSpec(memory_space=pltpu.VMEM)
ANY = pl.BlockSpec(memory_space=pltpu.HBM)
NX, NYL, NZ = 64, 32, 128
GROUP = 8
PAD = 4
ROWS = 64
OWN0, OWN1 = 16, 48
WIDE0, WIDE1 = 8, 56
WIDE = WIDE1 - WIDE0
OWN_X, OWN_Y = slice(PAD, PAD + NX), slice(OWN0, OWN1)
CHUNK = 16
OWN, WITH_HALO = range(4), range(-1, 5)


def depth_operator():
    band = np.zeros((NZ, NZ), np.float32)
    for i in range(NZ):
        band[i, i] = np.float32(3.0 * STENCIL[0])
        for k in range(1, 5):
            for j in (i - k, i + k):
                if 0 <= j < NZ:
                    band[j, i] = np.float32(STENCIL[k])
    high = band.astype(ml_dtypes.bfloat16)
    low = (band - high.astype(np.float32)).astype(ml_dtypes.bfloat16)
    zero = np.zeros_like(high)
    return np.block([[high, low], [high, zero]])


def clear_ends(ext):
    zeros = jnp.zeros((PAD, ROWS, NZ), F32)
    ext[0:PAD] = zeros
    ext[PAD + NX : 2 * PAD + NX] = zeros


def planes(body):
    def step(x, carry):
        body(x)
        return carry

    lax.fori_loop(0, NX, step, 0, unroll=16)


def fill_edges(ext, spots, halo_lo, halo_hi):
    has_lo, has_hi = spots[5] == 1, spots[6] == 1

    def body(t, carry):
        lo = jnp.where(has_lo, halo_lo[t], 0.0)
        hi = jnp.where(has_hi, halo_hi[t], 0.0)
        for half in range(2):
            x = PAD + 2 * t + half
            ext[x, OWN0 - 4 : OWN0, :] = lo[4 * half : 4 * half + 4]
            ext[x, OWN1 : OWN1 + 4, :] = hi[4 * half : 4 * half + 4]
        return carry

    lax.fori_loop(0, NX // 2, body, 0, unroll=8)


def fill_tiles(ext, spots, lo, hi):
    has_lo, has_hi = spots[5] == 1, spots[6] == 1

    def body(x):
        ext[PAD + x, WIDE0:OWN0, :] = jnp.where(has_lo, lo(x), 0.0)
        ext[PAD + x, OWN1:WIDE1, :] = jnp.where(has_hi, hi(x), 0.0)

    planes(body)


def fill_ring(ext, edge):
    def body(x):
        ext[PAD + x, OWN0 - 4 : OWN0, :] = edge[x, 0:4, :]
        ext[PAD + x, OWN1 : OWN1 + 4, :] = edge[x, 4:8, :]

    planes(body)


def no_edges(ext):
    zeros = jnp.zeros((4, NZ), F32)

    def body(x):
        ext[PAD + x, OWN0 - 4 : OWN0, :] = zeros
        ext[PAD + x, OWN1 : OWN1 + 4, :] = zeros

    planes(body)


def halo_taps(strip, x, j):
    way = -1 if j == 0 else 1
    acc = None
    for k in range(1, 5):
        term = STENCIL[k] * strip[x, 8 + way * k : 16 + way * k, :]
        acc = term if acc is None else acc + term
    return acc


def fill_strip(strip, spots, halo_lo, halo_hi):
    has_lo, has_hi = spots[5] == 1, spots[6] == 1
    zeros = jnp.zeros((8, NZ), F32)

    def body(t, carry):
        lo = jnp.where(has_lo, halo_lo[t], 0.0)
        hi = jnp.where(has_hi, halo_hi[t], 0.0)
        for half in range(2):
            strip[2 * t + half, 4:8, :] = lo[4 * half : 4 * half + 4]
            strip[2 * t + half, 8:16, :] = zeros
            strip[2 * t + half, 16:20, :] = hi[4 * half : 4 * half + 4]
        return carry

    lax.fori_loop(0, NX // 2, body, 0, unroll=8)


def apply_depth(ext, oper, depth, wide=False, span=None):
    r0, r1 = span or ((WIDE0, WIDE1) if wide else (OWN0, OWN1))
    n = CHUNK
    for at in range(0, NX, n):
        rows = ext[PAD + at : PAD + at + n, r0:r1, :].reshape(n * (r1 - r0), NZ)
        high = rows.astype(BF16)
        low = (rows - high.astype(F32)).astype(BF16)
        prod = jnp.dot(jnp.concatenate([high, low], axis=1), oper[...], preferred_element_type=F32)
        depth[at : at + n, r0 - WIDE0 : r1 - WIDE0, :] = (prod[:, :NZ] + prod[:, NZ:]).reshape(n, r1 - r0, NZ)


def laplace(ext, depth, tiles, emit):
    def body(g, carry):
        base = PAD + g * GROUP
        for j in tiles:
            r0 = OWN0 + 8 * j
            col = [ext[base - PAD + i, r0 : r0 + 8, :] for i in range(GROUP + 2 * PAD)]
            for xi in range(GROUP):
                acc = depth[g * GROUP + xi, r0 - WIDE0 : r0 - WIDE0 + 8, :]
                for k in range(1, 5):
                    beside = (
                        col[xi + PAD + k]
                        + col[xi + PAD - k]
                        + (
                            ext[base + xi, r0 + k : r0 + k + 8, :]
                            + ext[base + xi, r0 - k : r0 - k + 8, :]
                        )
                    )
                    acc = acc + STENCIL[k] * beside
                emit(g * GROUP + xi, g, xi, j, acc)
        return carry

    lax.fori_loop(0, NX // GROUP, body, 0)


def tile(j):
    return slice(8 * j, 8 * j + 8)


def ext_tile(j):
    return slice(OWN0 + 8 * j, OWN0 + 8 * j + 8)


def send_rows(send_lo, send_hi, read):
    def body(t, carry):
        for half in range(2):
            send_lo[t, 4 * half : 4 * half + 4, :] = read(2 * t + half, slice(0, 4))
            send_hi[t, 4 * half : 4 * half + 4, :] = read(2 * t + half, slice(NYL - 4, NYL))
        return carry

    lax.fori_loop(0, NX // 2, body, 0, unroll=8)


def send_tiles(send_lo, send_hi, field):
    def body(x):
        send_lo[x] = field[x, 0:8, :]
        send_hi[x] = field[x, NYL - 8 : NYL, :]

    planes(body)


def add_source(spots, amount, ref, x0, y0, wide=False):
    @pl.when(spots[7 if wide else 1] == 1)
    def _():
        x, y, z = x0 + spots[2], y0 + spots[3], spots[4]
        lanes = lax.broadcasted_iota(jnp.int32, (1, NZ), 1)
        row = ref[x, pl.ds(y, 1), :]
        ref[x, pl.ds(y, 1), :] = row + jnp.where(lanes == z, amount, 0.0)


NOW, PREV, EDGES, HALF, TURNED = 0, 32, 64, 72, 144


def unpack(turned, base, sems, now, edge, prev):
    copies = []
    for n, (off, rows, dst) in enumerate(((NOW, NYL, now), (EDGES, 8, edge), (PREV, NYL, prev))):
        copies.append(pltpu.make_async_copy(turned.at[:, base + off : base + off + rows, :], dst, sems.at[n]))
        copies[n].start()
    return copies


def first_kernel(spots, wavelet, turned, r2, oper, lap, new, send_lo, send_hi, now, edge, ext, depth, prev, sems):
    copies = unpack(turned, 0, sems, now, edge, prev)
    clear_ends(ext)
    copies[0].wait()
    ext[OWN_X, OWN_Y, :] = now[...]
    apply_depth(ext, oper, depth)
    for c in copies[1:]:
        c.wait()
    fill_ring(ext, edge)

    def emit(x, g, xi, j, value):
        lap[x, tile(j), :] = value
        new[x, tile(j), :] = 2.0 * ext[PAD + x, ext_tile(j), :] - prev[x, tile(j), :] + r2[x, tile(j), :] * value

    laplace(ext, depth, OWN, emit)
    add_source(spots, wavelet[0], new, 0, 0)
    send_tiles(send_lo, send_hi, new)


def spread_edges(edge, lo, hi):
    def body(x):
        lo[x, 4:8, :] = edge[x, 0:4, :]
        hi[x, 0:4, :] = edge[x, 4:8, :]

    planes(body)


def spread_halos(halo_lo, halo_hi, lo, hi):
    def body(t, carry):
        for half in range(2):
            lo[2 * t + half, 4:8, :] = halo_lo[t, 4 * half : 4 * half + 4, :]
            hi[2 * t + half, 0:4, :] = halo_hi[t, 4 * half : 4 * half + 4, :]
        return carry

    lax.fori_loop(0, NX // 2, body, 0, unroll=8)


def middle_kernel(
    spots, wavelet, now, now_lo, now_hi, prev, edge, r2, r2_lo, r2_hi, oper,
    lap_a, new_a, lap_b, new_b, send_lo, send_hi, ext, ext2, depth, old_lo, old_hi,
):
    has = (spots[5] == 1, spots[6] == 1)
    clear_ends(ext)
    clear_ends(ext2)
    ext[OWN_X, OWN_Y, :] = now[...]
    fill_tiles(ext, spots, lambda x: now_lo[x], lambda x: now_hi[x])
    spread_edges(edge, old_lo, old_hi)
    apply_depth(ext, oper, depth, True)

    def emit(x, g, xi, j, value):
        twice = 2.0 * ext[PAD + x, ext_tile(j), :]
        if j in OWN:
            u = twice - prev[x, tile(j), :] + r2[x, tile(j), :] * value
            lap_a[x, tile(j), :] = value
            new_a[x, tile(j), :] = u
        else:
            old, weight, there = (old_lo, r2_lo, has[0]) if j < 0 else (old_hi, r2_hi, has[1])
            u = jnp.where(there, twice - old[x] + weight[x] * value, 0.0)
        ext2[PAD + x, ext_tile(j), :] = u

    laplace(ext, depth, WITH_HALO, emit)
    add_source(spots, wavelet[1], new_a, 0, 0)
    add_source(spots, wavelet[1], ext2, PAD, OWN0, True)
    apply_depth(ext2, oper, depth)

    def emit_b(x, g, xi, j, value):
        lap_b[x, tile(j), :] = value
        new_b[x, tile(j), :] = 2.0 * ext2[PAD + x, ext_tile(j), :] - now[x, tile(j), :] + r2[x, tile(j), :] * value

    laplace(ext2, depth, OWN, emit_b)
    add_source(spots, wavelet[2], new_b, 0, 0)
    send_rows(send_lo, send_hi, lambda x, rows: new_b[x, rows, :])


def late_kernel(spots, turned, r2, r2_lo, r2_hi, oper, mu, late, edge, ext, depth, later, sems):
    copies = unpack(turned, HALF, sems, late, edge, later)
    clear_ends(ext)
    for c in copies[:2]:
        c.wait()

    def weigh(x):
        ext[PAD + x, OWN_Y, :] = late[x] * r2[x]
        ext[PAD + x, OWN0 - 4 : OWN0, :] = edge[x, 0:4, :] * r2_lo[x, 4:8, :]
        ext[PAD + x, OWN1 : OWN1 + 4, :] = edge[x, 4:8, :] * r2_hi[x, 0:4, :]

    planes(weigh)
    apply_depth(ext, oper, depth)
    copies[2].wait()

    def emit(x, g, xi, j, value):
        mu[x, tile(j), :] = 2.0 * late[x, tile(j), :] + value - later[x, tile(j), :]

    laplace(ext, depth, OWN, emit)


def turn_kernel(spots, wavelet, now, prev, r2, oper, part, count, data, lap, mu, ext, depth, new):
    clear_ends(ext)
    no_edges(ext)
    ext[OWN_X, OWN_Y, :] = now[...]
    apply_depth(ext, oper, depth)

    def emit(x, g, xi, j, value):
        new[x, tile(j), :] = 2.0 * ext[PAD + x, ext_tile(j), :] - prev[x, tile(j), :] + r2[x, tile(j), :] * value
        lap[x, tile(j), :] = value

    laplace(ext, depth, OWN, emit)
    add_source(spots, wavelet[3], new, 0, 0)

    def finish(x):
        mu[x] = part[x] + (count[x, 8 : 8 + NYL, :] * new[x] - data[x])

    planes(finish)


def turn_end_kernel(spots, halo_lo, halo_hi, r2, count, lap, mu_in, total, mu, send_lo, send_hi, strip):
    fill_strip(strip, spots, halo_lo, halo_hi)

    def body(x):
        for j in OWN:
            m, value = mu_in[x, tile(j), :], lap[x, tile(j), :]
            if j in (0, 3):
                more = halo_taps(strip, x, j)
                value = value + more
                m = m + count[x, 8 + 8 * j : 16 + 8 * j, :] * (r2[x, tile(j), :] * more)
                (send_hi if j else send_lo)[x] = m
            mu[x, tile(j), :] = m
            total[x, tile(j), :] = m * value

    planes(body)


def back_kernel(spots, late, later, r2, oper, count, data, wave, lap, total_in, total, mu, ext, depth):
    clear_ends(ext)
    no_edges(ext)
    ext[OWN_X, OWN_Y, :] = late[...] * r2[...]
    apply_depth(ext, oper, depth)

    def emit(x, g, xi, j, value):
        wide = slice(8 + 8 * j, 16 + 8 * j)
        m = 2.0 * late[x, tile(j), :] + value - later[x, tile(j), :]
        m = m + (count[x, wide, :] * wave[x, tile(j), :] - data[x, wide, :])
        mu[x, tile(j), :] = m
        total[x, tile(j), :] = total_in[x, tile(j), :] + m * lap[x, tile(j), :]

    laplace(ext, depth, OWN, emit)


def back_end_kernel(
    spots, late, late_lo, late_hi, edge, r2, r2_lo, r2_hi, oper, count, data_a, data_b,
    wave_lo, wave_hi, wave_b, lap_a, lap_b, mu_in, total_in,
    total, mu_a, mu_b, send_lo, send_hi, ext, ext2, depth, old_lo, old_hi, u_lo, u_hi, strip,
):
    has = (spots[5] == 1, spots[6] == 1)
    clear_ends(ext)
    clear_ends(ext2)
    ext[OWN_X, OWN_Y, :] = late[...] * r2[...]
    fill_tiles(ext, spots, lambda x: late_lo[x] * r2_lo[x], lambda x: late_hi[x] * r2_hi[x])
    spread_edges(edge, old_lo, old_hi)
    spread_halos(wave_lo, wave_hi, u_lo, u_hi)
    zeros = jnp.zeros((8, NZ), F32)

    def near(x):
        strip[x, 4:8, :] = ext[PAD + x, OWN0 - 4 : OWN0, :]
        strip[x, 8:16, :] = zeros
        strip[x, 16:20, :] = ext[PAD + x, OWN1 : OWN1 + 4, :]

    planes(near)
    apply_depth(ext, oper, depth, span=(WIDE0, OWN0))
    apply_depth(ext, oper, depth, span=(OWN1, WIDE1))

    def own(x):
        for j in OWN:
            mu, sofar = mu_in[x, tile(j), :], total_in[x, tile(j), :]
            if j in (0, 3):
                more = halo_taps(strip, x, j)
                mu = mu + more
                sofar = sofar + more * lap_a[x, tile(j), :]
            mu_a[x, tile(j), :] = mu
            total[x, tile(j), :] = sofar
            ext2[PAD + x, ext_tile(j), :] = mu * r2[x, tile(j), :]

    planes(own)

    def emit(x, g, xi, j, value):
        wide = slice(8 + 8 * j, 16 + 8 * j)
        close, old, u, weight, there = (
            (late_lo, old_lo, u_lo, r2_lo, has[0]) if j < 0 else (late_hi, old_hi, u_hi, r2_hi, has[1])
        )
        mu = 2.0 * close[x] + value - old[x] + (count[x, wide, :] * u[x] - data_a[x, wide, :])
        ext2[PAD + x, ext_tile(j), :] = jnp.where(there, mu * weight[x], 0.0)

    laplace(ext, depth, (-1, 4), emit)
    apply_depth(ext2, oper, depth)

    def emit_b(x, g, xi, j, value):
        mu = 2.0 * mu_a[x, tile(j), :] + value - late[x, tile(j), :]
        mu = mu + (count[x, 8 + 8 * j : 16 + 8 * j, :] * wave_b[x, tile(j), :] - data_b[x, tile(j), :])
        mu_b[x, tile(j), :] = mu
        total[x, tile(j), :] = total[x, tile(j), :] + mu * lap_b[x, tile(j), :]

    laplace(ext2, depth, OWN, emit_b)
    send_rows(send_lo, send_hi, lambda x, rows: mu_b[x, rows, :] * r2[x, rows, :])


def last_kernel(
    spots, late, later, r2, oper, count, data, wave, lap, total_in, total, ext, depth
):
    clear_ends(ext)
    ext[OWN_X, OWN_Y, :] = late[...] * r2[...]
    no_edges(ext)
    apply_depth(ext, oper, depth)

    def emit(x, g, xi, j, value):
        mu = 2.0 * late[x, tile(j), :] + value - later[x, tile(j), :]
        mu = mu + (count[x, 8 + 8 * j : 16 + 8 * j, :] * wave[x, tile(j), :] - data[x, tile(j), :])
        total[x, tile(j), :] = total_in[x, tile(j), :] + mu * lap[x, tile(j), :]

    laplace(ext, depth, OWN, emit)


def last_end_kernel(ids, spots, halo_lo, halo_hi, lap, total, *rest):
    outs, others, strip = rest[:4], rest[4], rest[5]
    fill_strip(strip, spots, halo_lo, halo_hi)
    _, y, core = split_shot(ids[0])
    for k in range(4):
        for side in range(2):
            cls = 2 * lax.rem(y + k, 4) + (core if side == 0 else 1 - core)
            g = lax.rem(cls - spots[0] + GROUP, GROUP)
            out = outs[k] if side == 0 else others.at[k]
            for xi in range(GROUP):
                x = g * GROUP + xi
                for j in OWN:
                    value = total[x, tile(j), :]
                    if j in (0, 3):
                        value = value + lap[x, tile(j), :] * halo_taps(strip, x, j)
                    out[xi, tile(j), :] = value


def pack_kernel(now, prev, late, later, out, near, edge, sems):
    order = ((0, now, NOW), (2, late, HALF + NOW), (1, prev, PREV), (3, later, HALF + PREV))
    bring = {f: pltpu.make_async_copy(field, near.at[f], sems.at[f]) for f, field, _ in order}
    for f, _, _ in order:
        bring[f].start()
    none = jnp.zeros((4, NZ), F32)
    sent = []
    for f, _, off in order:
        bring[f].wait()
        for p in range(8):
            sent.append(
                pltpu.make_async_copy(
                    near.at[f, :, NYL * p : NYL * p + NYL, :], out.at[p, :, off : off + NYL, :], sems.at[4 + 8 * f + p]
                )
            )
            sent[-1].start()
        if f % 2 == 0:

            def body(xi, carry):
                for p in range(8):
                    lo = NYL * p
                    edge[f // 2, p, xi, 0:4, :] = near[f, xi, lo - 4 : lo, :] if p > 0 else none
                    edge[f // 2, p, xi, 4:8, :] = near[f, xi, lo + NYL : lo + NYL + 4, :] if p < 7 else none
                return carry

            lax.fori_loop(0, GROUP, body, 0)
            at = f // 2 * HALF + EDGES
            sent.append(pltpu.make_async_copy(edge.at[f // 2], out.at[:, :, at : at + 8, :], sems.at[36 + f // 2]))
            sent[-1].start()
    for c in sent:
        c.wait()


def copy_block(dst, src):
    def body(x, carry):
        dst[x] = src[x]
        return carry

    lax.fori_loop(0, GROUP, body, 0, unroll=4)


def split_shot(me):
    return me // 8, lax.rem(me // 2, 4), lax.rem(me, 2)


def slot_of(start, which):
    return (start + lax.rem(which - start + 32, 8)) // 8


def select_kernel(ids, apertures, piece, other, piece_c, other_c, *outs):
    half, y, core = split_shot(ids[0])
    for k in range(4):
        start = apertures[8 * half + 2 * lax.rem(y + k, 4) + core, 0]
        for j in range(2):
            m = slot_of(start, 2 * y + j)
            row = m // 2
            own_half = lax.rem(m, 2) == half
            own_core = core == j
            for src, same_half, same_core in (
                (piece, True, True),
                (other, False, True),
                (piece_c, True, False),
                (other_c, False, False),
            ):

                @pl.when(jnp.logical_and(own_half == same_half, own_core == same_core))
                def _():
                    copy_block(outs[k].at[j], src.at[row])


def assemble_kernel(ids, apertures, r0, r1, r2, r3, out, send_lo, send_hi):
    _, y, _ = split_shot(ids[0])
    first = apertures[ids[0], 0]
    for k, src in enumerate((r0, r1, r2, r3)):
        for j in range(2):
            at = lax.rem(2 * lax.rem(y - k + 4, 4) + j - first + 32, 8)
            copy_block(out.at[pl.ds(at * GROUP, GROUP)], src.at[j])
    send_tiles(send_lo, send_hi, out)


def receivers_kernel(cells, lines, observed, count, data3, data1, data2, data4):
    zeros = jnp.zeros((NYL, NZ), F32)
    zeros_wide = jnp.zeros((WIDE, NZ), F32)

    def clear(x):
        for d in (count, data3):
            d[x] = zeros_wide
        for d in (data1, data2, data4):
            d[x] = zeros

    planes(clear)
    lanes = lax.broadcasted_iota(jnp.int32, (1, NZ), 1)

    def body(r, carry):
        y = lines[r]

        @pl.when(jnp.logical_and(y >= -8, y < NYL + 8))
        def _():
            cell = cells[r]
            x = cell // (256 * NZ)
            hit = lanes == lax.rem(cell, NZ)
            row = pl.ds(y + 8, 1)
            count[x, row, :] = count[x, row, :] + jnp.where(hit, 1.0, 0.0)
            data3[x, row, :] = data3[x, row, :] + jnp.where(hit, observed[2, r], 0.0)

            @pl.when(jnp.logical_and(y >= 0, y < NYL))
            def _():
                own = pl.ds(y, 1)
                for n, d in ((0, data1), (1, data2), (3, data4)):
                    d[x, own, :] = d[x, own, :] + jnp.where(hit, observed[n, r], 0.0)

        return carry

    lax.fori_loop(0, cells.shape[0], body, 0)


def bins_kernel(give, ids, apertures, *rest):
    recv, out = rest[:8], rest[8]
    mine, y, core = split_shot(ids[0])
    which = lax.rem(ids[0], 8)
    out[...] = jnp.zeros((2, GROUP, NYL, NZ), F32)
    for t in range(8):
        shot = 8 * mine + 2 * lax.rem(y - t % 4 + 4, 4) + (core if t < 4 else 1 - core)
        m = slot_of(apertures[shot, 0], which)
        i = m // 2
        block = recv[t].at[0] if t == 4 else recv[t]

        @pl.when((lax.rem(m, 2) != mine) if give else (lax.rem(m, 2) == mine))
        def _():
            out[i] = out[i] + block[...]


FIELD = jax.ShapeDtypeStruct((NX, NYL, NZ), F32)
WIDE_FIELD = jax.ShapeDtypeStruct((NX, WIDE, NZ), F32)
EDGE = jax.ShapeDtypeStruct((NX // 2, 8, NZ), F32)
TILE = jax.ShapeDtypeStruct((NX, 8, NZ), F32)
BLOCKS = jax.ShapeDtypeStruct((4, GROUP, NYL, NZ), F32)
BLOCK = jax.ShapeDtypeStruct((GROUP, NYL, NZ), F32)
PAIR = jax.ShapeDtypeStruct((2, GROUP, NYL, NZ), F32)
EXT = pltpu.VMEM((NX + 2 * PAD, ROWS, NZ), F32)
DEPTH = pltpu.VMEM((NX, WIDE, NZ), F32)
FIELD_VMEM = pltpu.VMEM((NX, NYL, NZ), F32)
STRIP = pltpu.VMEM((NX, 24, NZ), F32)
MAIN = 10 << 20
TILE_VMEM = pltpu.VMEM((NX, 8, NZ), F32)


def call(kernel, specs, outs, scratch=(), flops=0, moved=0, out_spec=VMEM, limit=12):
    return pl.pallas_call(
        kernel,
        in_specs=specs,
        out_specs=[out_spec] * len(outs),
        out_shape=outs,
        scratch_shapes=list(scratch),
        compiler_params=pltpu.CompilerParams(vmem_limit_bytes=limit << 20),
        cost_estimate=pl.CostEstimate(flops=flops, bytes_accessed=moved, transcendentals=0),
    )


def per_device(
    courant_squared,
    wave_now,
    wave_prev,
    adj_late,
    adj_later,
    wavelet,
    sources,
    receivers,
    observed,
    apertures,
):
    me = lax.axis_index("shot")
    part = lax.axis_index("sub")
    ids = jnp.stack([me, part]).astype(jnp.int32)
    first = apertures[me, 0]
    oper = jnp.asarray(depth_operator())
    up = [(i, (i + 1) % 8) for i in range(8)]
    down = [((i + 1) % 8, i) for i in range(8)]
    across = [(i, (i + 8) % 16) for i in range(16)]
    chip = [(i, i ^ 1) for i in range(16)]

    def along(k):
        return [(8 * h + 2 * y + c, 8 * h + 2 * ((y + k) % 4) + c) for h in range(2) for y in range(4) for c in range(2)]

    def edges(lo, hi):
        return lax.ppermute(hi, "sub", up), lax.ppermute(lo, "sub", down)

    piece = courant_squared[:, 0]
    other = lax.ppermute(piece, "shot", across)
    piece_c = lax.ppermute(piece, "shot", chip)
    other_c = lax.ppermute(other, "shot", chip)
    blocks = call(select_kernel, [SMEM] * 2 + [VMEM] * 4, [PAIR] * 4, moved=2 << 20)(
        ids, apertures, piece, other, piece_c, other_c
    )
    come = [blocks[0]] + [lax.ppermute(blocks[k], "shot", along(k)) for k in (1, 2, 3)]

    (packed,) = call(
        pack_kernel,
        [ANY] * 4,
        [jax.ShapeDtypeStruct((8, GROUP, TURNED, NZ), F32)],
        [
            pltpu.VMEM((4, GROUP, 256, NZ), F32),
            pltpu.VMEM((2, 8, GROUP, 8, NZ), F32),
            pltpu.SemaphoreType.DMA((38,)),
        ],
        moved=9 << 20,
        out_spec=ANY,
        limit=58,
    )(wave_now[0], wave_prev[0], adj_late[0], adj_later[0])
    turned = lax.all_to_all(packed, "sub", 0, 0, tiled=True).reshape(NX, TURNED, NZ)
    r2, *r2_send = call(assemble_kernel, [SMEM] * 2 + [VMEM] * 4, [FIELD, TILE, TILE], moved=2 << 20)(
        ids, apertures, *come
    )
    r2_halo = edges(*r2_send)

    cell = sources[0]
    line = (cell // NZ) % 256 - NYL * part
    spots = jnp.stack(
        [
            first % 8,
            ((line >= 0) & (line < NYL)).astype(jnp.int32),
            cell // (256 * NZ),
            line,
            cell % NZ,
            (part > 0).astype(jnp.int32),
            (part < 7).astype(jnp.int32),
            ((line >= -8) & (line < NYL + 8)).astype(jnp.int32),
        ]
    )
    amounts = wavelet[0]
    cells = receivers[0]
    lines = (cells // NZ) % 256 - NYL * part

    count, data3, data1, data2, data4 = call(
        receivers_kernel, [SMEM] * 3, [WIDE_FIELD, WIDE_FIELD] + [FIELD] * 3, flops=1 << 40, moved=6 << 20
    )(cells, lines, observed[0])
    r2, count = lax.optimization_barrier((r2, count))

    lap0, u1, lo, hi, u0, u0_edge = call(
        first_kernel,
        [SMEM, SMEM, ANY, VMEM, VMEM],
        [FIELD, FIELD, TILE, TILE, FIELD, TILE],
        [EXT, DEPTH, FIELD_VMEM, pltpu.SemaphoreType.DMA((3,))],
        flops=10 << 20,
        moved=8 << 20,
    )(spots, amounts, turned, r2, oper)
    u1_halo = edges(lo, hi)
    part4, mu5, mu5_edge = call(
        late_kernel,
        [SMEM, ANY] + [VMEM] * 4,
        [FIELD, FIELD, TILE],
        [EXT, DEPTH, FIELD_VMEM, pltpu.SemaphoreType.DMA((3,))],
        flops=10 << 20,
        moved=6 << 20,
    )(spots, turned, r2, *r2_halo, oper)
    u1, part4 = lax.optimization_barrier((u1, part4))
    lap1, u2, lap2, u3, lo, hi = call(
        middle_kernel,
        [SMEM, SMEM] + [VMEM] * 9,
        [FIELD] * 4 + [EDGE] * 2,
        [EXT, EXT, DEPTH, TILE_VMEM, TILE_VMEM],
        flops=20 << 20,
        moved=12 << 20,
    )(spots, amounts, u1, *u1_halo, u0, u0_edge, r2, *r2_halo, oper)
    u3_halo = edges(lo, hi)
    lap3, mu4 = call(
        turn_kernel,
        [SMEM, SMEM] + [VMEM] * 7,
        [FIELD, FIELD],
        [EXT, DEPTH, FIELD_VMEM],
        flops=MAIN,
        moved=8 << 20,
    )(spots, amounts, u3, u2, r2, oper, part4, count, data4)
    total, mu4, lo, hi = call(
        turn_end_kernel, [SMEM] + [VMEM] * 6, [FIELD, FIELD, TILE, TILE], [STRIP], flops=1 << 20, moved=4 << 20
    )(spots, *u3_halo, r2, count, lap3, mu4)
    mu4_halo = edges(lo, hi)
    total, mu3 = call(
        back_kernel, [SMEM] + [VMEM] * 9, [FIELD, FIELD], [EXT, DEPTH], flops=MAIN, moved=8 << 20
    )(spots, mu4, mu5, r2, oper, count, data3, u3, lap2, total)
    total, mu3, mu2, lo, hi = call(
        back_end_kernel,
        [SMEM] + [VMEM] * 18,
        [FIELD] * 3 + [EDGE] * 2,
        [EXT, EXT, DEPTH] + [TILE_VMEM] * 4 + [STRIP],
        flops=20 << 20,
        moved=16 << 20,
    )(
        spots, mu4, *mu4_halo, mu5_edge, r2, *r2_halo, oper, count, data3, data2,
        *u3_halo, u2, lap2, lap1, mu3, total,
    )
    mu2_halo = edges(lo, hi)
    (total,) = call(last_kernel, [SMEM] + [VMEM] * 9, [FIELD], [EXT, DEPTH], flops=MAIN, moved=8 << 20)(
        spots, mu2, mu3, r2, oper, count, data1, u1, lap0, total
    )
    *sent, others = call(
        last_end_kernel, [SMEM] * 2 + [VMEM] * 4, [BLOCK] * 4 + [BLOCKS], [STRIP], flops=1 << 20, moved=3 << 20
    )(ids, spots, *mu2_halo, lap0, total)

    own = [sent[0]] + [lax.ppermute(sent[k], "shot", along(k)) for k in (1, 2, 3)]
    others = lax.ppermute(others, "shot", chip)
    recv = own + [others] + [lax.ppermute(others[k], "shot", along(k)) for k in (1, 2, 3)]
    give, keep = (
        call(functools.partial(bins_kernel, side), [SMEM] * 2 + [VMEM] * 8, [PAIR], moved=1 << 20)(ids, apertures, *recv)[0]
        for side in (True, False)
    )
    result = keep + lax.ppermute(give, "shot", across)
    return result[:, None]


def solution(mesh):
    in_specs = (
        P(None, "shot", None, "sub", None),
        P("shot", "sub", None, None),
        P("shot", "sub", None, None),
        P("shot", "sub", None, None),
        P("shot", "sub", None, None),
        P("shot", None),
        P("shot"),
        P("shot", None),
        P("shot", None, None),
        P(),
    )
    out_specs = P(None, "shot", None, "sub", None)
    return jax.shard_map(
        per_device, mesh=mesh, in_specs=in_specs, out_specs=out_specs, check_vma=False
    )
```

```python
import functools

import jax
import jax.numpy as jnp
import ml_dtypes
import numpy as np
from jax import lax
from jax.experimental import pallas as pl
from jax.experimental.pallas import tpu as pltpu
from jax.sharding import PartitionSpec as P

STEPS = 4
STENCIL = (-205.0 / 72.0, 8.0 / 5.0, -1.0 / 5.0, 8.0 / 315.0, -1.0 / 560.0)
F32 = jnp.float32
BF16 = jnp.bfloat16
SMEM = pl.BlockSpec(memory_space=pltpu.SMEM)
VMEM = pl.BlockSpec(memory_space=pltpu.VMEM)
ANY = pl.BlockSpec(memory_space=pltpu.HBM)
NX, NYL, NZ = 64, 32, 128
GROUP = 8
PAD = 4
ROWS = 64
OWN0, OWN1 = 16, 48
WIDE0, WIDE1 = 8, 56
WIDE = WIDE1 - WIDE0
OWN_X, OWN_Y = slice(PAD, PAD + NX), slice(OWN0, OWN1)
CHUNK = 16
OWN, WITH_HALO = range(4), range(-1, 5)


def depth_operator():
    band = np.zeros((NZ, NZ), np.float32)
    for i in range(NZ):
        band[i, i] = np.float32(3.0 * STENCIL[0])
        for k in range(1, 5):
            for j in (i - k, i + k):
                if 0 <= j < NZ:
                    band[j, i] = np.float32(STENCIL[k])
    high = band.astype(ml_dtypes.bfloat16)
    low = (band - high.astype(np.float32)).astype(ml_dtypes.bfloat16)
    zero = np.zeros_like(high)
    return np.block([[high, low], [high, zero]])


def clear_ends(ext):
    zeros = jnp.zeros((PAD, ROWS, NZ), F32)
    ext[0:PAD] = zeros
    ext[PAD + NX : 2 * PAD + NX] = zeros


def planes(body):
    def step(x, carry):
        body(x)
        return carry

    lax.fori_loop(0, NX, step, 0, unroll=16)


def fill_edges(ext, spots, halo_lo, halo_hi):
    has_lo, has_hi = spots[5] == 1, spots[6] == 1

    def body(t, carry):
        lo = jnp.where(has_lo, halo_lo[t], 0.0)
        hi = jnp.where(has_hi, halo_hi[t], 0.0)
        for half in range(2):
            x = PAD + 2 * t + half
            ext[x, OWN0 - 4 : OWN0, :] = lo[4 * half : 4 * half + 4]
            ext[x, OWN1 : OWN1 + 4, :] = hi[4 * half : 4 * half + 4]
        return carry

    lax.fori_loop(0, NX // 2, body, 0, unroll=8)


def fill_tiles(ext, spots, lo, hi):
    has_lo, has_hi = spots[5] == 1, spots[6] == 1

    def body(x):
        ext[PAD + x, WIDE0:OWN0, :] = jnp.where(has_lo, lo(x), 0.0)
        ext[PAD + x, OWN1:WIDE1, :] = jnp.where(has_hi, hi(x), 0.0)

    planes(body)


def fill_ring(ext, edge):
    def body(x):
        ext[PAD + x, OWN0 - 4 : OWN0, :] = edge[x, 0:4, :]
        ext[PAD + x, OWN1 : OWN1 + 4, :] = edge[x, 4:8, :]

    planes(body)


def no_edges(ext):
    zeros = jnp.zeros((4, NZ), F32)

    def body(x):
        ext[PAD + x, OWN0 - 4 : OWN0, :] = zeros
        ext[PAD + x, OWN1 : OWN1 + 4, :] = zeros

    planes(body)


def halo_taps(strip, x, j):
    way = -1 if j == 0 else 1
    acc = None
    for k in range(1, 5):
        term = STENCIL[k] * strip[x, 8 + way * k : 16 + way * k, :]
        acc = term if acc is None else acc + term
    return acc


def fill_strip(strip, spots, halo_lo, halo_hi):
    has_lo, has_hi = spots[5] == 1, spots[6] == 1
    zeros = jnp.zeros((8, NZ), F32)

    def body(t, carry):
        lo = jnp.where(has_lo, halo_lo[t], 0.0)
        hi = jnp.where(has_hi, halo_hi[t], 0.0)
        for half in range(2):
            strip[2 * t + half, 4:8, :] = lo[4 * half : 4 * half + 4]
            strip[2 * t + half, 8:16, :] = zeros
            strip[2 * t + half, 16:20, :] = hi[4 * half : 4 * half + 4]
        return carry

    lax.fori_loop(0, NX // 2, body, 0, unroll=8)


def apply_depth(ext, oper, depth, wide=False, span=None):
    r0, r1 = span or ((WIDE0, WIDE1) if wide else (OWN0, OWN1))
    n = CHUNK
    for at in range(0, NX, n):
        rows = ext[PAD + at : PAD + at + n, r0:r1, :].reshape(n * (r1 - r0), NZ)
        high = rows.astype(BF16)
        low = (rows - high.astype(F32)).astype(BF16)
        prod = jnp.dot(jnp.concatenate([high, low], axis=1), oper[...], preferred_element_type=F32)
        depth[at : at + n, r0 - WIDE0 : r1 - WIDE0, :] = (prod[:, :NZ] + prod[:, NZ:]).reshape(n, r1 - r0, NZ)


def laplace(ext, depth, tiles, emit):
    def body(g, carry):
        base = PAD + g * GROUP
        for j in tiles:
            r0 = OWN0 + 8 * j
            col = [ext[base - PAD + i, r0 : r0 + 8, :] for i in range(GROUP + 2 * PAD)]
            for xi in range(GROUP):
                acc = depth[g * GROUP + xi, r0 - WIDE0 : r0 - WIDE0 + 8, :]
                for k in range(1, 5):
                    beside = (
                        col[xi + PAD + k]
                        + col[xi + PAD - k]
                        + (
                            ext[base + xi, r0 + k : r0 + k + 8, :]
                            + ext[base + xi, r0 - k : r0 - k + 8, :]
                        )
                    )
                    acc = acc + STENCIL[k] * beside
                emit(g * GROUP + xi, g, xi, j, acc)
        return carry

    lax.fori_loop(0, NX // GROUP, body, 0, unroll=2)


def tile(j):
    return slice(8 * j, 8 * j + 8)


def ext_tile(j):
    return slice(OWN0 + 8 * j, OWN0 + 8 * j + 8)


def send_rows(send_lo, send_hi, read):
    def body(t, carry):
        for half in range(2):
            send_lo[t, 4 * half : 4 * half + 4, :] = read(2 * t + half, slice(0, 4))
            send_hi[t, 4 * half : 4 * half + 4, :] = read(2 * t + half, slice(NYL - 4, NYL))
        return carry

    lax.fori_loop(0, NX // 2, body, 0, unroll=8)


def send_tiles(send_lo, send_hi, field):
    def body(x):
        send_lo[x] = field[x, 0:8, :]
        send_hi[x] = field[x, NYL - 8 : NYL, :]

    planes(body)


def add_source(spots, amount, ref, x0, y0, wide=False):
    @pl.when(spots[7 if wide else 1] == 1)
    def _():
        x, y, z = x0 + spots[2], y0 + spots[3], spots[4]
        lanes = lax.broadcasted_iota(jnp.int32, (1, NZ), 1)
        row = ref[x, pl.ds(y, 1), :]
        ref[x, pl.ds(y, 1), :] = row + jnp.where(lanes == z, amount, 0.0)


NOW, PREV, EDGES, HALF, TURNED = 0, 32, 64, 72, 144


def unpack(turned, base, sems, now, edge, prev):
    copies = []
    for n, (off, rows, dst) in enumerate(((NOW, NYL, now), (EDGES, 8, edge), (PREV, NYL, prev))):
        copies.append(pltpu.make_async_copy(turned.at[:, base + off : base + off + rows, :], dst, sems.at[n]))
        copies[n].start()
    return copies


def first_kernel(spots, wavelet, turned, r2, oper, lap, new, send_lo, send_hi, now, edge, ext, depth, prev, sems):
    copies = unpack(turned, 0, sems, now, edge, prev)
    clear_ends(ext)
    copies[0].wait()
    ext[OWN_X, OWN_Y, :] = now[...]
    apply_depth(ext, oper, depth)
    for c in copies[1:]:
        c.wait()
    fill_ring(ext, edge)

    def emit(x, g, xi, j, value):
        lap[x, tile(j), :] = value
        new[x, tile(j), :] = 2.0 * ext[PAD + x, ext_tile(j), :] - prev[x, tile(j), :] + r2[x, tile(j), :] * value

    laplace(ext, depth, OWN, emit)
    add_source(spots, wavelet[0], new, 0, 0)
    send_tiles(send_lo, send_hi, new)


def spread_edges(edge, lo, hi):
    def body(x):
        lo[x, 4:8, :] = edge[x, 0:4, :]
        hi[x, 0:4, :] = edge[x, 4:8, :]

    planes(body)


def spread_halos(halo_lo, halo_hi, lo, hi):
    def body(t, carry):
        for half in range(2):
            lo[2 * t + half, 4:8, :] = halo_lo[t, 4 * half : 4 * half + 4, :]
            hi[2 * t + half, 0:4, :] = halo_hi[t, 4 * half : 4 * half + 4, :]
        return carry

    lax.fori_loop(0, NX // 2, body, 0, unroll=8)


def middle_kernel(now, prev, r2, oper, lap, new, ext, depth):
    clear_ends(ext)
    no_edges(ext)
    ext[OWN_X, OWN_Y, :] = now[...]
    apply_depth(ext, oper, depth)

    def emit(x, g, xi, j, value):
        lap[x, tile(j), :] = value
        new[x, tile(j), :] = 2.0 * ext[PAD + x, ext_tile(j), :] - prev[x, tile(j), :] + r2[x, tile(j), :] * value

    laplace(ext, depth, OWN, emit)


def middle_end_kernel(
    spots, wavelet, now, now_lo, now_hi, edge, r2, r2_lo, r2_hi, oper, lap_in, new_in,
    lap_a, new_a, lap_b, new_b, send_lo, send_hi, ext, ext2, depth, old_lo, old_hi, strip,
):
    has = (spots[5] == 1, spots[6] == 1)
    clear_ends(ext)
    clear_ends(ext2)
    ext[OWN_X, OWN_Y, :] = now[...]
    fill_tiles(ext, spots, lambda x: now_lo[x], lambda x: now_hi[x])
    spread_edges(edge, old_lo, old_hi)
    zeros = jnp.zeros((8, NZ), F32)

    def near(x):
        strip[x, 4:8, :] = ext[PAD + x, OWN0 - 4 : OWN0, :]
        strip[x, 8:16, :] = zeros
        strip[x, 16:20, :] = ext[PAD + x, OWN1 : OWN1 + 4, :]

    planes(near)
    apply_depth(ext, oper, depth, span=(WIDE0, OWN0))
    apply_depth(ext, oper, depth, span=(OWN1, WIDE1))

    def own(x):
        for j in OWN:
            value, u = lap_in[x, tile(j), :], new_in[x, tile(j), :]
            if j in (0, 3):
                more = halo_taps(strip, x, j)
                value = value + more
                u = u + r2[x, tile(j), :] * more
            lap_a[x, tile(j), :] = value
            new_a[x, tile(j), :] = u
            ext2[PAD + x, ext_tile(j), :] = u

    planes(own)

    def emit(x, g, xi, j, value):
        old, weight, there = (old_lo, r2_lo, has[0]) if j < 0 else (old_hi, r2_hi, has[1])
        u = 2.0 * ext[PAD + x, ext_tile(j), :] - old[x] + weight[x] * value
        ext2[PAD + x, ext_tile(j), :] = jnp.where(there, u, 0.0)

    laplace(ext, depth, (-1, 4), emit)
    add_source(spots, wavelet[1], new_a, 0, 0)
    add_source(spots, wavelet[1], ext2, PAD, OWN0, True)
    apply_depth(ext2, oper, depth)

    def emit_b(x, g, xi, j, value):
        lap_b[x, tile(j), :] = value
        new_b[x, tile(j), :] = 2.0 * ext2[PAD + x, ext_tile(j), :] - now[x, tile(j), :] + r2[x, tile(j), :] * value

    laplace(ext2, depth, OWN, emit_b)
    add_source(spots, wavelet[2], new_b, 0, 0)
    send_rows(send_lo, send_hi, lambda x, rows: new_b[x, rows, :])


def late_kernel(spots, turned, r2, r2_lo, r2_hi, oper, mu, late, edge, ext, depth, later, sems):
    copies = unpack(turned, HALF, sems, late, edge, later)
    clear_ends(ext)
    for c in copies[:2]:
        c.wait()

    def weigh(x):
        ext[PAD + x, OWN_Y, :] = late[x] * r2[x]
        ext[PAD + x, OWN0 - 4 : OWN0, :] = edge[x, 0:4, :] * r2_lo[x, 4:8, :]
        ext[PAD + x, OWN1 : OWN1 + 4, :] = edge[x, 4:8, :] * r2_hi[x, 0:4, :]

    planes(weigh)
    apply_depth(ext, oper, depth)
    copies[2].wait()

    def emit(x, g, xi, j, value):
        mu[x, tile(j), :] = 2.0 * late[x, tile(j), :] + value - later[x, tile(j), :]

    laplace(ext, depth, OWN, emit)


def turn_kernel(spots, wavelet, now, prev, r2, oper, part, count, data, lap, mu, ext, depth, new):
    clear_ends(ext)
    no_edges(ext)
    ext[OWN_X, OWN_Y, :] = now[...]
    apply_depth(ext, oper, depth)

    def emit(x, g, xi, j, value):
        new[x, tile(j), :] = 2.0 * ext[PAD + x, ext_tile(j), :] - prev[x, tile(j), :] + r2[x, tile(j), :] * value
        lap[x, tile(j), :] = value

    laplace(ext, depth, OWN, emit)
    add_source(spots, wavelet[3], new, 0, 0)

    def finish(x):
        mu[x] = part[x] + (count[x, 8 : 8 + NYL, :] * new[x] - data[x])

    planes(finish)


def turn_end_kernel(spots, halo_lo, halo_hi, r2, count, lap, mu_in, total, mu, send_lo, send_hi, strip):
    fill_strip(strip, spots, halo_lo, halo_hi)

    def body(x):
        for j in OWN:
            m, value = mu_in[x, tile(j), :], lap[x, tile(j), :]
            if j in (0, 3):
                more = halo_taps(strip, x, j)
                value = value + more
                m = m + count[x, 8 + 8 * j : 16 + 8 * j, :] * (r2[x, tile(j), :] * more)
                (send_hi if j else send_lo)[x] = m
            mu[x, tile(j), :] = m
            total[x, tile(j), :] = m * value

    planes(body)


def back_kernel(spots, late, later, r2, oper, count, data, wave, lap, total_in, total, mu, ext, depth):
    clear_ends(ext)
    no_edges(ext)
    ext[OWN_X, OWN_Y, :] = late[...] * r2[...]
    apply_depth(ext, oper, depth)

    def emit(x, g, xi, j, value):
        wide = slice(8 + 8 * j, 16 + 8 * j)
        m = 2.0 * late[x, tile(j), :] + value - later[x, tile(j), :]
        m = m + (count[x, wide, :] * wave[x, tile(j), :] - data[x, wide, :])
        mu[x, tile(j), :] = m
        total[x, tile(j), :] = total_in[x, tile(j), :] + m * lap[x, tile(j), :]

    laplace(ext, depth, OWN, emit)


def back_end_kernel(
    spots, late, late_lo, late_hi, edge, r2, r2_lo, r2_hi, oper, count, data_a, data_b,
    wave_lo, wave_hi, wave_b, lap_a, lap_b, mu_in, total_in,
    total, mu_a, mu_b, send_lo, send_hi, ext, ext2, depth, old_lo, old_hi, u_lo, u_hi, strip,
):
    has = (spots[5] == 1, spots[6] == 1)
    clear_ends(ext)
    clear_ends(ext2)
    ext[OWN_X, OWN_Y, :] = late[...] * r2[...]
    fill_tiles(ext, spots, lambda x: late_lo[x] * r2_lo[x], lambda x: late_hi[x] * r2_hi[x])
    spread_edges(edge, old_lo, old_hi)
    spread_halos(wave_lo, wave_hi, u_lo, u_hi)
    zeros = jnp.zeros((8, NZ), F32)

    def near(x):
        strip[x, 4:8, :] = ext[PAD + x, OWN0 - 4 : OWN0, :]
        strip[x, 8:16, :] = zeros
        strip[x, 16:20, :] = ext[PAD + x, OWN1 : OWN1 + 4, :]

    planes(near)
    apply_depth(ext, oper, depth, span=(WIDE0, OWN0))
    apply_depth(ext, oper, depth, span=(OWN1, WIDE1))

    def own(x):
        for j in OWN:
            mu, sofar = mu_in[x, tile(j), :], total_in[x, tile(j), :]
            if j in (0, 3):
                more = halo_taps(strip, x, j)
                mu = mu + more
                sofar = sofar + more * lap_a[x, tile(j), :]
            mu_a[x, tile(j), :] = mu
            total[x, tile(j), :] = sofar
            ext2[PAD + x, ext_tile(j), :] = mu * r2[x, tile(j), :]

    planes(own)

    def emit(x, g, xi, j, value):
        wide = slice(8 + 8 * j, 16 + 8 * j)
        close, old, u, weight, there = (
            (late_lo, old_lo, u_lo, r2_lo, has[0]) if j < 0 else (late_hi, old_hi, u_hi, r2_hi, has[1])
        )
        mu = 2.0 * close[x] + value - old[x] + (count[x, wide, :] * u[x] - data_a[x, wide, :])
        ext2[PAD + x, ext_tile(j), :] = jnp.where(there, mu * weight[x], 0.0)

    laplace(ext, depth, (-1, 4), emit)
    apply_depth(ext2, oper, depth)

    def emit_b(x, g, xi, j, value):
        mu = 2.0 * mu_a[x, tile(j), :] + value - late[x, tile(j), :]
        mu = mu + (count[x, 8 + 8 * j : 16 + 8 * j, :] * wave_b[x, tile(j), :] - data_b[x, tile(j), :])
        mu_b[x, tile(j), :] = mu
        total[x, tile(j), :] = total[x, tile(j), :] + mu * lap_b[x, tile(j), :]

    laplace(ext2, depth, OWN, emit_b)
    send_rows(send_lo, send_hi, lambda x, rows: mu_b[x, rows, :] * r2[x, rows, :])


def last_kernel(
    spots, late, later, r2, oper, count, data, wave, lap, total_in, total, ext, depth
):
    clear_ends(ext)
    ext[OWN_X, OWN_Y, :] = late[...] * r2[...]
    no_edges(ext)
    apply_depth(ext, oper, depth)

    def emit(x, g, xi, j, value):
        mu = 2.0 * late[x, tile(j), :] + value - later[x, tile(j), :]
        mu = mu + (count[x, 8 + 8 * j : 16 + 8 * j, :] * wave[x, tile(j), :] - data[x, tile(j), :])
        total[x, tile(j), :] = total_in[x, tile(j), :] + mu * lap[x, tile(j), :]

    laplace(ext, depth, OWN, emit)


def last_end_kernel(ids, spots, halo_lo, halo_hi, lap, total, *rest):
    outs, others, strip = rest[:4], rest[4], rest[5]
    fill_strip(strip, spots, halo_lo, halo_hi)
    _, y, core = split_shot(ids[0])
    for k in range(4):
        for side in range(2):
            cls = 2 * lax.rem(y + k, 4) + (core if side == 0 else 1 - core)
            g = lax.rem(cls - spots[0] + GROUP, GROUP)
            out = outs[k] if side == 0 else others.at[k]
            for xi in range(GROUP):
                x = g * GROUP + xi
                for j in OWN:
                    value = total[x, tile(j), :]
                    if j in (0, 3):
                        value = value + lap[x, tile(j), :] * halo_taps(strip, x, j)
                    out[xi, tile(j), :] = value


def pack_kernel(now, prev, late, later, out, near, edge, sems):
    order = ((0, now, NOW), (2, late, HALF + NOW), (1, prev, PREV), (3, later, HALF + PREV))
    bring = {f: pltpu.make_async_copy(field, near.at[f], sems.at[f]) for f, field, _ in order}
    for f, _, _ in order:
        bring[f].start()
    none = jnp.zeros((4, NZ), F32)
    sent = []
    for f, _, off in order:
        bring[f].wait()
        for p in range(8):
            sent.append(
                pltpu.make_async_copy(
                    near.at[f, :, NYL * p : NYL * p + NYL, :], out.at[p, :, off : off + NYL, :], sems.at[4 + 8 * f + p]
                )
            )
            sent[-1].start()
        if f % 2 == 0:

            def body(xi, carry):
                for p in range(8):
                    lo = NYL * p
                    edge[f // 2, p, xi, 0:4, :] = near[f, xi, lo - 4 : lo, :] if p > 0 else none
                    edge[f // 2, p, xi, 4:8, :] = near[f, xi, lo + NYL : lo + NYL + 4, :] if p < 7 else none
                return carry

            lax.fori_loop(0, GROUP, body, 0)
            at = f // 2 * HALF + EDGES
            sent.append(pltpu.make_async_copy(edge.at[f // 2], out.at[:, :, at : at + 8, :], sems.at[36 + f // 2]))
            sent[-1].start()
    for c in sent:
        c.wait()


def copy_block(dst, src):
    def body(x, carry):
        dst[x] = src[x]
        return carry

    lax.fori_loop(0, GROUP, body, 0, unroll=4)


def split_shot(me):
    return me // 8, lax.rem(me // 2, 4), lax.rem(me, 2)


def slot_of(start, which):
    return (start + lax.rem(which - start + 32, 8)) // 8


def select_kernel(ids, apertures, piece, other, piece_c, other_c, *outs):
    half, y, core = split_shot(ids[0])
    for k in range(4):
        start = apertures[8 * half + 2 * lax.rem(y + k, 4) + core, 0]
        for j in range(2):
            m = slot_of(start, 2 * y + j)
            row = m // 2
            own_half = lax.rem(m, 2) == half
            own_core = core == j
            for src, same_half, same_core in (
                (piece, True, True),
                (other, False, True),
                (piece_c, True, False),
                (other_c, False, False),
            ):

                @pl.when(jnp.logical_and(own_half == same_half, own_core == same_core))
                def _():
                    copy_block(outs[k].at[j], src.at[row])


def assemble_kernel(ids, apertures, r0, r1, r2, r3, out, send_lo, send_hi):
    _, y, _ = split_shot(ids[0])
    first = apertures[ids[0], 0]
    for k, src in enumerate((r0, r1, r2, r3)):
        for j in range(2):
            at = lax.rem(2 * lax.rem(y - k + 4, 4) + j - first + 32, 8)
            copy_block(out.at[pl.ds(at * GROUP, GROUP)], src.at[j])
    send_tiles(send_lo, send_hi, out)


def receivers_kernel(cells, lines, observed, count, data3, data1, data2, data4):
    zeros = jnp.zeros((NYL, NZ), F32)
    zeros_wide = jnp.zeros((WIDE, NZ), F32)

    def clear(x):
        for d in (count, data3):
            d[x] = zeros_wide
        for d in (data1, data2, data4):
            d[x] = zeros

    planes(clear)
    lanes = lax.broadcasted_iota(jnp.int32, (1, NZ), 1)

    def body(r, carry):
        y = lines[r]

        @pl.when(jnp.logical_and(y >= -8, y < NYL + 8))
        def _():
            cell = cells[r]
            x = cell // (256 * NZ)
            hit = lanes == lax.rem(cell, NZ)
            row = pl.ds(y + 8, 1)
            count[x, row, :] = count[x, row, :] + jnp.where(hit, 1.0, 0.0)
            data3[x, row, :] = data3[x, row, :] + jnp.where(hit, observed[2, r], 0.0)

            @pl.when(jnp.logical_and(y >= 0, y < NYL))
            def _():
                own = pl.ds(y, 1)
                for n, d in ((0, data1), (1, data2), (3, data4)):
                    d[x, own, :] = d[x, own, :] + jnp.where(hit, observed[n, r], 0.0)

        return carry

    lax.fori_loop(0, cells.shape[0], body, 0)


def bins_kernel(give, ids, apertures, *rest):
    recv, out = rest[:8], rest[8]
    mine, y, core = split_shot(ids[0])
    which = lax.rem(ids[0], 8)
    out[...] = jnp.zeros((2, GROUP, NYL, NZ), F32)
    for t in range(8):
        shot = 8 * mine + 2 * lax.rem(y - t % 4 + 4, 4) + (core if t < 4 else 1 - core)
        m = slot_of(apertures[shot, 0], which)
        i = m // 2
        block = recv[t].at[0] if t == 4 else recv[t]

        @pl.when((lax.rem(m, 2) != mine) if give else (lax.rem(m, 2) == mine))
        def _():
            out[i] = out[i] + block[...]


FIELD = jax.ShapeDtypeStruct((NX, NYL, NZ), F32)
WIDE_FIELD = jax.ShapeDtypeStruct((NX, WIDE, NZ), F32)
EDGE = jax.ShapeDtypeStruct((NX // 2, 8, NZ), F32)
TILE = jax.ShapeDtypeStruct((NX, 8, NZ), F32)
BLOCKS = jax.ShapeDtypeStruct((4, GROUP, NYL, NZ), F32)
BLOCK = jax.ShapeDtypeStruct((GROUP, NYL, NZ), F32)
PAIR = jax.ShapeDtypeStruct((2, GROUP, NYL, NZ), F32)
EXT = pltpu.VMEM((NX + 2 * PAD, ROWS, NZ), F32)
DEPTH = pltpu.VMEM((NX, WIDE, NZ), F32)
FIELD_VMEM = pltpu.VMEM((NX, NYL, NZ), F32)
STRIP = pltpu.VMEM((NX, 24, NZ), F32)
MAIN = 10 << 20
TILE_VMEM = pltpu.VMEM((NX, 8, NZ), F32)


def call(kernel, specs, outs, scratch=(), flops=0, moved=0, out_spec=VMEM, limit=12):
    return pl.pallas_call(
        kernel,
        in_specs=specs,
        out_specs=[out_spec] * len(outs),
        out_shape=outs,
        scratch_shapes=list(scratch),
        compiler_params=pltpu.CompilerParams(vmem_limit_bytes=limit << 20),
        cost_estimate=pl.CostEstimate(flops=flops, bytes_accessed=moved, transcendentals=0),
    )


def per_device(
    courant_squared,
    wave_now,
    wave_prev,
    adj_late,
    adj_later,
    wavelet,
    sources,
    receivers,
    observed,
    apertures,
):
    me = lax.axis_index("shot")
    part = lax.axis_index("sub")
    ids = jnp.stack([me, part]).astype(jnp.int32)
    first = apertures[me, 0]
    oper = jnp.asarray(depth_operator())
    up = [(i, (i + 1) % 8) for i in range(8)]
    down = [((i + 1) % 8, i) for i in range(8)]
    across = [(i, (i + 8) % 16) for i in range(16)]
    chip = [(i, i ^ 1) for i in range(16)]

    def along(k):
        return [(8 * h + 2 * y + c, 8 * h + 2 * ((y + k) % 4) + c) for h in range(2) for y in range(4) for c in range(2)]

    def edges(lo, hi):
        return lax.ppermute(hi, "sub", up), lax.ppermute(lo, "sub", down)

    piece = courant_squared[:, 0]
    other = lax.ppermute(piece, "shot", across)
    piece_c = lax.ppermute(piece, "shot", chip)
    other_c = lax.ppermute(other, "shot", chip)
    blocks = call(select_kernel, [SMEM] * 2 + [VMEM] * 4, [PAIR] * 4, moved=2 << 20)(
        ids, apertures, piece, other, piece_c, other_c
    )
    come = [blocks[0]] + [lax.ppermute(blocks[k], "shot", along(k)) for k in (1, 2, 3)]

    (packed,) = call(
        pack_kernel,
        [ANY] * 4,
        [jax.ShapeDtypeStruct((8, GROUP, TURNED, NZ), F32)],
        [
            pltpu.VMEM((4, GROUP, 256, NZ), F32),
            pltpu.VMEM((2, 8, GROUP, 8, NZ), F32),
            pltpu.SemaphoreType.DMA((38,)),
        ],
        moved=9 << 20,
        out_spec=ANY,
        limit=58,
    )(wave_now[0], wave_prev[0], adj_late[0], adj_later[0])
    turned = lax.all_to_all(packed, "sub", 0, 0, tiled=True).reshape(NX, TURNED, NZ)
    r2, *r2_send = call(assemble_kernel, [SMEM] * 2 + [VMEM] * 4, [FIELD, TILE, TILE], moved=2 << 20)(
        ids, apertures, *come
    )
    r2_halo = edges(*r2_send)

    cell = sources[0]
    line = (cell // NZ) % 256 - NYL * part
    spots = jnp.stack(
        [
            first % 8,
            ((line >= 0) & (line < NYL)).astype(jnp.int32),
            cell // (256 * NZ),
            line,
            cell % NZ,
            (part > 0).astype(jnp.int32),
            (part < 7).astype(jnp.int32),
            ((line >= -8) & (line < NYL + 8)).astype(jnp.int32),
        ]
    )
    amounts = wavelet[0]
    cells = receivers[0]
    lines = (cells // NZ) % 256 - NYL * part

    count, data3, data1, data2, data4 = call(
        receivers_kernel, [SMEM] * 3, [WIDE_FIELD, WIDE_FIELD] + [FIELD] * 3, flops=1 << 40, moved=6 << 20
    )(cells, lines, observed[0])
    r2, count = lax.optimization_barrier((r2, count))

    lap0, u1, lo, hi, u0, u0_edge = call(
        first_kernel,
        [SMEM, SMEM, ANY, VMEM, VMEM],
        [FIELD, FIELD, TILE, TILE, FIELD, TILE],
        [EXT, DEPTH, FIELD_VMEM, pltpu.SemaphoreType.DMA((3,))],
        flops=10 << 20,
        moved=8 << 20,
    )(spots, amounts, turned, r2, oper)
    u1_halo = edges(lo, hi)
    part4, mu5, mu5_edge = call(
        late_kernel,
        [SMEM, ANY] + [VMEM] * 4,
        [FIELD, FIELD, TILE],
        [EXT, DEPTH, FIELD_VMEM, pltpu.SemaphoreType.DMA((3,))],
        flops=10 << 20,
        moved=6 << 20,
    )(spots, turned, r2, *r2_halo, oper)
    lap1, u2 = call(middle_kernel, [VMEM] * 4, [FIELD, FIELD], [EXT, DEPTH], flops=MAIN, moved=6 << 20)(u1, u0, r2, oper)
    u2, part4 = lax.optimization_barrier((u2, part4))
    lap1, u2, lap2, u3, lo, hi = call(
        middle_end_kernel,
        [SMEM, SMEM] + [VMEM] * 10,
        [FIELD] * 4 + [EDGE] * 2,
        [EXT, EXT, DEPTH, TILE_VMEM, TILE_VMEM, STRIP],
        flops=20 << 20,
        moved=12 << 20,
    )(spots, amounts, u1, *u1_halo, u0_edge, r2, *r2_halo, oper, lap1, u2)
    u3_halo = edges(lo, hi)
    lap3, mu4 = call(
        turn_kernel,
        [SMEM, SMEM] + [VMEM] * 7,
        [FIELD, FIELD],
        [EXT, DEPTH, FIELD_VMEM],
        flops=MAIN,
        moved=8 << 20,
    )(spots, amounts, u3, u2, r2, oper, part4, count, data4)
    total, mu4, lo, hi = call(
        turn_end_kernel, [SMEM] + [VMEM] * 6, [FIELD, FIELD, TILE, TILE], [STRIP], flops=1 << 20, moved=4 << 20
    )(spots, *u3_halo, r2, count, lap3, mu4)
    mu4_halo = edges(lo, hi)
    total, mu3 = call(
        back_kernel, [SMEM] + [VMEM] * 9, [FIELD, FIELD], [EXT, DEPTH], flops=MAIN, moved=8 << 20
    )(spots, mu4, mu5, r2, oper, count, data3, u3, lap2, total)
    total, mu3, mu2, lo, hi = call(
        back_end_kernel,
        [SMEM] + [VMEM] * 18,
        [FIELD] * 3 + [EDGE] * 2,
        [EXT, EXT, DEPTH] + [TILE_VMEM] * 4 + [STRIP],
        flops=20 << 20,
        moved=16 << 20,
    )(
        spots, mu4, *mu4_halo, mu5_edge, r2, *r2_halo, oper, count, data3, data2,
        *u3_halo, u2, lap2, lap1, mu3, total,
    )
    mu2_halo = edges(lo, hi)
    (total,) = call(last_kernel, [SMEM] + [VMEM] * 9, [FIELD], [EXT, DEPTH], flops=MAIN, moved=8 << 20)(
        spots, mu2, mu3, r2, oper, count, data1, u1, lap0, total
    )
    *sent, others = call(
        last_end_kernel, [SMEM] * 2 + [VMEM] * 4, [BLOCK] * 4 + [BLOCKS], [STRIP], flops=1 << 20, moved=3 << 20
    )(ids, spots, *mu2_halo, lap0, total)

    own = [sent[0]] + [lax.ppermute(sent[k], "shot", along(k)) for k in (1, 2, 3)]
    others = lax.ppermute(others, "shot", chip)
    recv = own + [others] + [lax.ppermute(others[k], "shot", along(k)) for k in (1, 2, 3)]
    give, keep = (
        call(functools.partial(bins_kernel, side), [SMEM] * 2 + [VMEM] * 8, [PAIR], moved=1 << 20)(ids, apertures, *recv)[0]
        for side in (True, False)
    )
    result = keep + lax.ppermute(give, "shot", across)
    return result[:, None]


def solution(mesh):
    in_specs = (
        P(None, "shot", None, "sub", None),
        P("shot", "sub", None, None),
        P("shot", "sub", None, None),
        P("shot", "sub", None, None),
        P("shot", "sub", None, None),
        P("shot", None),
        P("shot"),
        P("shot", None),
        P("shot", None, None),
        P(),
    )
    out_specs = P(None, "shot", None, "sub", None)
    return jax.shard_map(
        per_device, mesh=mesh, in_specs=in_specs, out_specs=out_specs, check_vma=False
    )
```

```python
import functools

import jax
import jax.numpy as jnp
import ml_dtypes
import numpy as np
from jax import lax
from jax.experimental import pallas as pl
from jax.experimental.pallas import tpu as pltpu
from jax.sharding import PartitionSpec as P

STEPS = 4
STENCIL = (-205.0 / 72.0, 8.0 / 5.0, -1.0 / 5.0, 8.0 / 315.0, -1.0 / 560.0)
F32 = jnp.float32
BF16 = jnp.bfloat16
SMEM = pl.BlockSpec(memory_space=pltpu.SMEM)
VMEM = pl.BlockSpec(memory_space=pltpu.VMEM)
ANY = pl.BlockSpec(memory_space=pltpu.HBM)
NX, NYL, NZ = 64, 32, 128
GROUP = 8
PAD = 4
ROWS = 64
OWN0, OWN1 = 16, 48
WIDE0, WIDE1 = 8, 56
WIDE = WIDE1 - WIDE0
OWN_X, OWN_Y = slice(PAD, PAD + NX), slice(OWN0, OWN1)
CHUNK = 8
OWN, WITH_HALO = range(4), range(-1, 5)


def depth_operator():
    band = np.zeros((NZ, NZ), np.float32)
    for i in range(NZ):
        band[i, i] = np.float32(3.0 * STENCIL[0])
        for k in range(1, 5):
            for j in (i - k, i + k):
                if 0 <= j < NZ:
                    band[j, i] = np.float32(STENCIL[k])
    high = band.astype(ml_dtypes.bfloat16)
    low = (band - high.astype(np.float32)).astype(ml_dtypes.bfloat16)
    zero = np.zeros_like(high)
    return np.block([[high, low], [high, zero]])


def clear_ends(ext):
    zeros = jnp.zeros((PAD, ROWS, NZ), F32)
    ext[0:PAD] = zeros
    ext[PAD + NX : 2 * PAD + NX] = zeros


def planes(body):
    def step(x, carry):
        body(x)
        return carry

    lax.fori_loop(0, NX, step, 0, unroll=16)


def fill_edges(ext, spots, halo_lo, halo_hi):
    has_lo, has_hi = spots[5] == 1, spots[6] == 1

    def body(t, carry):
        lo = jnp.where(has_lo, halo_lo[t], 0.0)
        hi = jnp.where(has_hi, halo_hi[t], 0.0)
        for half in range(2):
            x = PAD + 2 * t + half
            ext[x, OWN0 - 4 : OWN0, :] = lo[4 * half : 4 * half + 4]
            ext[x, OWN1 : OWN1 + 4, :] = hi[4 * half : 4 * half + 4]
        return carry

    lax.fori_loop(0, NX // 2, body, 0, unroll=8)


def fill_tiles(ext, spots, lo, hi):
    has_lo, has_hi = spots[5] == 1, spots[6] == 1

    def body(x):
        ext[PAD + x, WIDE0:OWN0, :] = jnp.where(has_lo, lo(x), 0.0)
        ext[PAD + x, OWN1:WIDE1, :] = jnp.where(has_hi, hi(x), 0.0)

    planes(body)


def fill_ring(ext, edge):
    def body(x):
        ext[PAD + x, OWN0 - 4 : OWN0, :] = edge[x, 0:4, :]
        ext[PAD + x, OWN1 : OWN1 + 4, :] = edge[x, 4:8, :]

    planes(body)


def no_edges(ext):
    zeros = jnp.zeros((4, NZ), F32)

    def body(x):
        ext[PAD + x, OWN0 - 4 : OWN0, :] = zeros
        ext[PAD + x, OWN1 : OWN1 + 4, :] = zeros

    planes(body)


def halo_taps(strip, x, j):
    way = -1 if j == 0 else 1
    acc = None
    for k in range(1, 5):
        term = STENCIL[k] * strip[x, 8 + way * k : 16 + way * k, :]
        acc = term if acc is None else acc + term
    return acc


def fill_strip(strip, spots, halo_lo, halo_hi):
    has_lo, has_hi = spots[5] == 1, spots[6] == 1
    zeros = jnp.zeros((8, NZ), F32)

    def body(t, carry):
        lo = jnp.where(has_lo, halo_lo[t], 0.0)
        hi = jnp.where(has_hi, halo_hi[t], 0.0)
        for half in range(2):
            strip[2 * t + half, 4:8, :] = lo[4 * half : 4 * half + 4]
            strip[2 * t + half, 8:16, :] = zeros
            strip[2 * t + half, 16:20, :] = hi[4 * half : 4 * half + 4]
        return carry

    lax.fori_loop(0, NX // 2, body, 0, unroll=8)


def apply_depth(ext, oper, depth, wide=False, span=None):
    r0, r1 = span or ((WIDE0, WIDE1) if wide else (OWN0, OWN1))
    n = CHUNK
    for at in range(0, NX, n):
        rows = ext[PAD + at : PAD + at + n, r0:r1, :].reshape(n * (r1 - r0), NZ)
        high = rows.astype(BF16)
        low = (rows - high.astype(F32)).astype(BF16)
        prod = jnp.dot(jnp.concatenate([high, low], axis=1), oper[...], preferred_element_type=F32)
        depth[at : at + n, r0 - WIDE0 : r1 - WIDE0, :] = (prod[:, :NZ] + prod[:, NZ:]).reshape(n, r1 - r0, NZ)


def laplace(ext, depth, tiles, emit):
    def body(g, carry):
        base = PAD + g * GROUP
        for j in tiles:
            r0 = OWN0 + 8 * j
            col = [ext[base - PAD + i, r0 : r0 + 8, :] for i in range(GROUP + 2 * PAD)]
            for xi in range(GROUP):
                acc = depth[g * GROUP + xi, r0 - WIDE0 : r0 - WIDE0 + 8, :]
                for k in range(1, 5):
                    beside = (
                        col[xi + PAD + k]
                        + col[xi + PAD - k]
                        + (
                            ext[base + xi, r0 + k : r0 + k + 8, :]
                            + ext[base + xi, r0 - k : r0 - k + 8, :]
                        )
                    )
                    acc = acc + STENCIL[k] * beside
                emit(g * GROUP + xi, g, xi, j, acc)
        return carry

    lax.fori_loop(0, NX // GROUP, body, 0, unroll=2)


def tile(j):
    return slice(8 * j, 8 * j + 8)


def ext_tile(j):
    return slice(OWN0 + 8 * j, OWN0 + 8 * j + 8)


def send_rows(send_lo, send_hi, read):
    def body(t, carry):
        for half in range(2):
            send_lo[t, 4 * half : 4 * half + 4, :] = read(2 * t + half, slice(0, 4))
            send_hi[t, 4 * half : 4 * half + 4, :] = read(2 * t + half, slice(NYL - 4, NYL))
        return carry

    lax.fori_loop(0, NX // 2, body, 0, unroll=8)


def send_tiles(send_lo, send_hi, field):
    def body(x):
        send_lo[x] = field[x, 0:8, :]
        send_hi[x] = field[x, NYL - 8 : NYL, :]

    planes(body)


def add_source(spots, amount, ref, x0, y0, wide=False):
    @pl.when(spots[7 if wide else 1] == 1)
    def _():
        x, y, z = x0 + spots[2], y0 + spots[3], spots[4]
        lanes = lax.broadcasted_iota(jnp.int32, (1, NZ), 1)
        row = ref[x, pl.ds(y, 1), :]
        ref[x, pl.ds(y, 1), :] = row + jnp.where(lanes == z, amount, 0.0)


NOW, PREV, EDGES, HALF, TURNED = 0, 32, 64, 72, 144


def unpack(turned, base, sems, now, edge, prev):
    copies = []
    for n, (off, rows, dst) in enumerate(((NOW, NYL, now), (EDGES, 8, edge), (PREV, NYL, prev))):
        copies.append(pltpu.make_async_copy(turned.at[:, base + off : base + off + rows, :], dst, sems.at[n]))
        copies[n].start()
    return copies


def first_kernel(spots, wavelet, turned, r2, oper, lap, new, send_lo, send_hi, now, edge, ext, depth, prev, sems):
    copies = unpack(turned, 0, sems, now, edge, prev)
    clear_ends(ext)
    copies[0].wait()
    ext[OWN_X, OWN_Y, :] = now[...]
    apply_depth(ext, oper, depth)
    for c in copies[1:]:
        c.wait()
    fill_ring(ext, edge)

    def emit(x, g, xi, j, value):
        lap[x, tile(j), :] = value
        new[x, tile(j), :] = 2.0 * ext[PAD + x, ext_tile(j), :] - prev[x, tile(j), :] + r2[x, tile(j), :] * value

    laplace(ext, depth, OWN, emit)
    add_source(spots, wavelet[0], new, 0, 0)
    send_tiles(send_lo, send_hi, new)


def spread_edges(edge, lo, hi):
    def body(x):
        lo[x, 4:8, :] = edge[x, 0:4, :]
        hi[x, 0:4, :] = edge[x, 4:8, :]

    planes(body)


def spread_halos(halo_lo, halo_hi, lo, hi):
    def body(t, carry):
        for half in range(2):
            lo[2 * t + half, 4:8, :] = halo_lo[t, 4 * half : 4 * half + 4, :]
            hi[2 * t + half, 0:4, :] = halo_hi[t, 4 * half : 4 * half + 4, :]
        return carry

    lax.fori_loop(0, NX // 2, body, 0, unroll=8)


def middle_kernel(now, prev, r2, oper, lap, new, ext, depth):
    clear_ends(ext)
    no_edges(ext)
    ext[OWN_X, OWN_Y, :] = now[...]
    apply_depth(ext, oper, depth)

    def emit(x, g, xi, j, value):
        lap[x, tile(j), :] = value
        new[x, tile(j), :] = 2.0 * ext[PAD + x, ext_tile(j), :] - prev[x, tile(j), :] + r2[x, tile(j), :] * value

    laplace(ext, depth, OWN, emit)


def middle_end_kernel(
    spots, wavelet, now, now_lo, now_hi, edge, r2, r2_lo, r2_hi, oper, lap_in, new_in,
    lap_a, new_a, lap_b, new_b, send_lo, send_hi, ext, ext2, depth, old_lo, old_hi, strip,
):
    has = (spots[5] == 1, spots[6] == 1)
    clear_ends(ext)
    clear_ends(ext2)
    ext[OWN_X, OWN_Y, :] = now[...]
    fill_tiles(ext, spots, lambda x: now_lo[x], lambda x: now_hi[x])
    spread_edges(edge, old_lo, old_hi)
    zeros = jnp.zeros((8, NZ), F32)

    def near(x):
        strip[x, 4:8, :] = ext[PAD + x, OWN0 - 4 : OWN0, :]
        strip[x, 8:16, :] = zeros
        strip[x, 16:20, :] = ext[PAD + x, OWN1 : OWN1 + 4, :]

    planes(near)
    apply_depth(ext, oper, depth, span=(WIDE0, OWN0))
    apply_depth(ext, oper, depth, span=(OWN1, WIDE1))

    def own(x):
        for j in OWN:
            value, u = lap_in[x, tile(j), :], new_in[x, tile(j), :]
            if j in (0, 3):
                more = halo_taps(strip, x, j)
                value = value + more
                u = u + r2[x, tile(j), :] * more
            lap_a[x, tile(j), :] = value
            new_a[x, tile(j), :] = u
            ext2[PAD + x, ext_tile(j), :] = u

    planes(own)

    def emit(x, g, xi, j, value):
        old, weight, there = (old_lo, r2_lo, has[0]) if j < 0 else (old_hi, r2_hi, has[1])
        u = 2.0 * ext[PAD + x, ext_tile(j), :] - old[x] + weight[x] * value
        ext2[PAD + x, ext_tile(j), :] = jnp.where(there, u, 0.0)

    laplace(ext, depth, (-1, 4), emit)
    add_source(spots, wavelet[1], new_a, 0, 0)
    add_source(spots, wavelet[1], ext2, PAD, OWN0, True)
    apply_depth(ext2, oper, depth)

    def emit_b(x, g, xi, j, value):
        lap_b[x, tile(j), :] = value
        new_b[x, tile(j), :] = 2.0 * ext2[PAD + x, ext_tile(j), :] - now[x, tile(j), :] + r2[x, tile(j), :] * value

    laplace(ext2, depth, OWN, emit_b)
    add_source(spots, wavelet[2], new_b, 0, 0)
    send_rows(send_lo, send_hi, lambda x, rows: new_b[x, rows, :])


def late_kernel(spots, turned, r2, r2_lo, r2_hi, oper, mu, late, edge, ext, depth, later, sems):
    copies = unpack(turned, HALF, sems, late, edge, later)
    clear_ends(ext)
    for c in copies[:2]:
        c.wait()

    def weigh(x):
        ext[PAD + x, OWN_Y, :] = late[x] * r2[x]
        ext[PAD + x, OWN0 - 4 : OWN0, :] = edge[x, 0:4, :] * r2_lo[x, 4:8, :]
        ext[PAD + x, OWN1 : OWN1 + 4, :] = edge[x, 4:8, :] * r2_hi[x, 0:4, :]

    planes(weigh)
    apply_depth(ext, oper, depth)
    copies[2].wait()

    def emit(x, g, xi, j, value):
        mu[x, tile(j), :] = 2.0 * late[x, tile(j), :] + value - later[x, tile(j), :]

    laplace(ext, depth, OWN, emit)


def turn_kernel(spots, wavelet, now, prev, r2, oper, part, count, data, lap, mu, ext, depth, new):
    clear_ends(ext)
    no_edges(ext)
    ext[OWN_X, OWN_Y, :] = now[...]
    apply_depth(ext, oper, depth)

    def emit(x, g, xi, j, value):
        new[x, tile(j), :] = 2.0 * ext[PAD + x, ext_tile(j), :] - prev[x, tile(j), :] + r2[x, tile(j), :] * value
        lap[x, tile(j), :] = value

    laplace(ext, depth, OWN, emit)
    add_source(spots, wavelet[3], new, 0, 0)

    def finish(x):
        mu[x] = part[x] + (count[x, 8 : 8 + NYL, :] * new[x] - data[x])

    planes(finish)


def turn_end_kernel(spots, halo_lo, halo_hi, r2, count, lap, mu_in, total, mu, send_lo, send_hi, strip):
    fill_strip(strip, spots, halo_lo, halo_hi)

    def body(x):
        for j in OWN:
            m, value = mu_in[x, tile(j), :], lap[x, tile(j), :]
            if j in (0, 3):
                more = halo_taps(strip, x, j)
                value = value + more
                m = m + count[x, 8 + 8 * j : 16 + 8 * j, :] * (r2[x, tile(j), :] * more)
                (send_hi if j else send_lo)[x] = m
            mu[x, tile(j), :] = m
            total[x, tile(j), :] = m * value

    planes(body)


def back_kernel(spots, late, later, r2, oper, count, data, wave, lap, total_in, total, mu, ext, depth):
    clear_ends(ext)
    no_edges(ext)
    ext[OWN_X, OWN_Y, :] = late[...] * r2[...]
    apply_depth(ext, oper, depth)

    def emit(x, g, xi, j, value):
        wide = slice(8 + 8 * j, 16 + 8 * j)
        m = 2.0 * late[x, tile(j), :] + value - later[x, tile(j), :]
        m = m + (count[x, wide, :] * wave[x, tile(j), :] - data[x, wide, :])
        mu[x, tile(j), :] = m
        total[x, tile(j), :] = total_in[x, tile(j), :] + m * lap[x, tile(j), :]

    laplace(ext, depth, OWN, emit)


def back_end_kernel(
    spots, late, late_lo, late_hi, edge, r2, r2_lo, r2_hi, oper, count, data_a, data_b,
    wave_lo, wave_hi, wave_b, lap_a, lap_b, mu_in, total_in,
    total, mu_a, mu_b, send_lo, send_hi, ext, ext2, depth, old_lo, old_hi, u_lo, u_hi, strip,
):
    has = (spots[5] == 1, spots[6] == 1)
    clear_ends(ext)
    clear_ends(ext2)
    ext[OWN_X, OWN_Y, :] = late[...] * r2[...]
    fill_tiles(ext, spots, lambda x: late_lo[x] * r2_lo[x], lambda x: late_hi[x] * r2_hi[x])
    spread_edges(edge, old_lo, old_hi)
    spread_halos(wave_lo, wave_hi, u_lo, u_hi)
    zeros = jnp.zeros((8, NZ), F32)

    def near(x):
        strip[x, 4:8, :] = ext[PAD + x, OWN0 - 4 : OWN0, :]
        strip[x, 8:16, :] = zeros
        strip[x, 16:20, :] = ext[PAD + x, OWN1 : OWN1 + 4, :]

    planes(near)
    apply_depth(ext, oper, depth, span=(WIDE0, OWN0))
    apply_depth(ext, oper, depth, span=(OWN1, WIDE1))

    def own(x):
        for j in OWN:
            mu, sofar = mu_in[x, tile(j), :], total_in[x, tile(j), :]
            if j in (0, 3):
                more = halo_taps(strip, x, j)
                mu = mu + more
                sofar = sofar + more * lap_a[x, tile(j), :]
            mu_a[x, tile(j), :] = mu
            total[x, tile(j), :] = sofar
            ext2[PAD + x, ext_tile(j), :] = mu * r2[x, tile(j), :]

    planes(own)

    def emit(x, g, xi, j, value):
        wide = slice(8 + 8 * j, 16 + 8 * j)
        close, old, u, weight, there = (
            (late_lo, old_lo, u_lo, r2_lo, has[0]) if j < 0 else (late_hi, old_hi, u_hi, r2_hi, has[1])
        )
        mu = 2.0 * close[x] + value - old[x] + (count[x, wide, :] * u[x] - data_a[x, wide, :])
        ext2[PAD + x, ext_tile(j), :] = jnp.where(there, mu * weight[x], 0.0)

    laplace(ext, depth, (-1, 4), emit)
    apply_depth(ext2, oper, depth)

    def emit_b(x, g, xi, j, value):
        mu = 2.0 * mu_a[x, tile(j), :] + value - late[x, tile(j), :]
        mu = mu + (count[x, 8 + 8 * j : 16 + 8 * j, :] * wave_b[x, tile(j), :] - data_b[x, tile(j), :])
        mu_b[x, tile(j), :] = mu
        total[x, tile(j), :] = total[x, tile(j), :] + mu * lap_b[x, tile(j), :]

    laplace(ext2, depth, OWN, emit_b)
    send_rows(send_lo, send_hi, lambda x, rows: mu_b[x, rows, :] * r2[x, rows, :])


def last_kernel(
    spots, late, later, r2, oper, count, data, wave, lap, total_in, total, ext, depth
):
    clear_ends(ext)
    ext[OWN_X, OWN_Y, :] = late[...] * r2[...]
    no_edges(ext)
    apply_depth(ext, oper, depth)

    def emit(x, g, xi, j, value):
        mu = 2.0 * late[x, tile(j), :] + value - later[x, tile(j), :]
        mu = mu + (count[x, 8 + 8 * j : 16 + 8 * j, :] * wave[x, tile(j), :] - data[x, tile(j), :])
        total[x, tile(j), :] = total_in[x, tile(j), :] + mu * lap[x, tile(j), :]

    laplace(ext, depth, OWN, emit)


def last_end_kernel(ids, spots, halo_lo, halo_hi, lap, total, *rest):
    outs, others, strip = rest[:4], rest[4], rest[5]
    fill_strip(strip, spots, halo_lo, halo_hi)
    _, y, core = split_shot(ids[0])
    for k in range(4):
        for side in range(2):
            cls = 2 * lax.rem(y + k, 4) + (core if side == 0 else 1 - core)
            g = lax.rem(cls - spots[0] + GROUP, GROUP)
            out = outs[k] if side == 0 else others.at[k]
            for xi in range(GROUP):
                x = g * GROUP + xi
                for j in OWN:
                    value = total[x, tile(j), :]
                    if j in (0, 3):
                        value = value + lap[x, tile(j), :] * halo_taps(strip, x, j)
                    out[xi, tile(j), :] = value


def pack_kernel(now, prev, late, later, out, near, edge, sems):
    order = ((0, now, NOW), (2, late, HALF + NOW), (1, prev, PREV), (3, later, HALF + PREV))
    bring = {f: pltpu.make_async_copy(field, near.at[f], sems.at[f]) for f, field, _ in order}
    for f, _, _ in order:
        bring[f].start()
    none = jnp.zeros((4, NZ), F32)
    sent = []
    for f, _, off in order:
        bring[f].wait()
        for p in range(8):
            sent.append(
                pltpu.make_async_copy(
                    near.at[f, :, NYL * p : NYL * p + NYL, :], out.at[p, :, off : off + NYL, :], sems.at[4 + 8 * f + p]
                )
            )
            sent[-1].start()
        if f % 2 == 0:

            def body(xi, carry):
                for p in range(8):
                    lo = NYL * p
                    edge[f // 2, p, xi, 0:4, :] = near[f, xi, lo - 4 : lo, :] if p > 0 else none
                    edge[f // 2, p, xi, 4:8, :] = near[f, xi, lo + NYL : lo + NYL + 4, :] if p < 7 else none
                return carry

            lax.fori_loop(0, GROUP, body, 0)
            at = f // 2 * HALF + EDGES
            sent.append(pltpu.make_async_copy(edge.at[f // 2], out.at[:, :, at : at + 8, :], sems.at[36 + f // 2]))
            sent[-1].start()
    for c in sent:
        c.wait()


def copy_block(dst, src):
    def body(x, carry):
        dst[x] = src[x]
        return carry

    lax.fori_loop(0, GROUP, body, 0, unroll=4)


def split_shot(me):
    return me // 8, lax.rem(me // 2, 4), lax.rem(me, 2)


def slot_of(start, which):
    return (start + lax.rem(which - start + 32, 8)) // 8


def select_kernel(ids, apertures, piece, other, piece_c, other_c, *outs):
    half, y, core = split_shot(ids[0])
    for k in range(4):
        start = apertures[8 * half + 2 * lax.rem(y + k, 4) + core, 0]
        for j in range(2):
            m = slot_of(start, 2 * y + j)
            row = m // 2
            own_half = lax.rem(m, 2) == half
            own_core = core == j
            for src, same_half, same_core in (
                (piece, True, True),
                (other, False, True),
                (piece_c, True, False),
                (other_c, False, False),
            ):

                @pl.when(jnp.logical_and(own_half == same_half, own_core == same_core))
                def _():
                    copy_block(outs[k].at[j], src.at[row])


def assemble_kernel(ids, apertures, r0, r1, r2, r3, out, send_lo, send_hi):
    _, y, _ = split_shot(ids[0])
    first = apertures[ids[0], 0]
    for k, src in enumerate((r0, r1, r2, r3)):
        for j in range(2):
            at = lax.rem(2 * lax.rem(y - k + 4, 4) + j - first + 32, 8)
            copy_block(out.at[pl.ds(at * GROUP, GROUP)], src.at[j])
    send_tiles(send_lo, send_hi, out)


def receivers_kernel(cells, lines, observed, count, data3, data1, data2, data4):
    zeros = jnp.zeros((NYL, NZ), F32)
    zeros_wide = jnp.zeros((WIDE, NZ), F32)

    def clear(x):
        for d in (count, data3):
            d[x] = zeros_wide
        for d in (data1, data2, data4):
            d[x] = zeros

    planes(clear)
    lanes = lax.broadcasted_iota(jnp.int32, (1, NZ), 1)

    def body(r, carry):
        y = lines[r]

        @pl.when(jnp.logical_and(y >= -8, y < NYL + 8))
        def _():
            cell = cells[r]
            x = cell // (256 * NZ)
            hit = lanes == lax.rem(cell, NZ)
            row = pl.ds(y + 8, 1)
            count[x, row, :] = count[x, row, :] + jnp.where(hit, 1.0, 0.0)
            data3[x, row, :] = data3[x, row, :] + jnp.where(hit, observed[2, r], 0.0)

            @pl.when(jnp.logical_and(y >= 0, y < NYL))
            def _():
                own = pl.ds(y, 1)
                for n, d in ((0, data1), (1, data2), (3, data4)):
                    d[x, own, :] = d[x, own, :] + jnp.where(hit, observed[n, r], 0.0)

        return carry

    lax.fori_loop(0, cells.shape[0], body, 0)


def bins_kernel(give, ids, apertures, *rest):
    recv, out = rest[:8], rest[8]
    mine, y, core = split_shot(ids[0])
    which = lax.rem(ids[0], 8)
    out[...] = jnp.zeros((2, GROUP, NYL, NZ), F32)
    for t in range(8):
        shot = 8 * mine + 2 * lax.rem(y - t % 4 + 4, 4) + (core if t < 4 else 1 - core)
        m = slot_of(apertures[shot, 0], which)
        i = m // 2
        block = recv[t].at[0] if t == 4 else recv[t]

        @pl.when((lax.rem(m, 2) != mine) if give else (lax.rem(m, 2) == mine))
        def _():
            out[i] = out[i] + block[...]


FIELD = jax.ShapeDtypeStruct((NX, NYL, NZ), F32)
WIDE_FIELD = jax.ShapeDtypeStruct((NX, WIDE, NZ), F32)
EDGE = jax.ShapeDtypeStruct((NX // 2, 8, NZ), F32)
TILE = jax.ShapeDtypeStruct((NX, 8, NZ), F32)
BLOCKS = jax.ShapeDtypeStruct((4, GROUP, NYL, NZ), F32)
BLOCK = jax.ShapeDtypeStruct((GROUP, NYL, NZ), F32)
PAIR = jax.ShapeDtypeStruct((2, GROUP, NYL, NZ), F32)
EXT = pltpu.VMEM((NX + 2 * PAD, ROWS, NZ), F32)
DEPTH = pltpu.VMEM((NX, WIDE, NZ), F32)
FIELD_VMEM = pltpu.VMEM((NX, NYL, NZ), F32)
STRIP = pltpu.VMEM((NX, 24, NZ), F32)
MAIN = 10 << 20
TILE_VMEM = pltpu.VMEM((NX, 8, NZ), F32)


def call(kernel, specs, outs, scratch=(), flops=0, moved=0, out_spec=VMEM, limit=12):
    return pl.pallas_call(
        kernel,
        in_specs=specs,
        out_specs=[out_spec] * len(outs),
        out_shape=outs,
        scratch_shapes=list(scratch),
        compiler_params=pltpu.CompilerParams(vmem_limit_bytes=limit << 20),
        cost_estimate=pl.CostEstimate(flops=flops, bytes_accessed=moved, transcendentals=0),
    )


def per_device(
    courant_squared,
    wave_now,
    wave_prev,
    adj_late,
    adj_later,
    wavelet,
    sources,
    receivers,
    observed,
    apertures,
):
    me = lax.axis_index("shot")
    part = lax.axis_index("sub")
    ids = jnp.stack([me, part]).astype(jnp.int32)
    first = apertures[me, 0]
    oper = jnp.asarray(depth_operator())
    up = [(i, (i + 1) % 8) for i in range(8)]
    down = [((i + 1) % 8, i) for i in range(8)]
    across = [(i, (i + 8) % 16) for i in range(16)]
    chip = [(i, i ^ 1) for i in range(16)]

    def along(k):
        return [(8 * h + 2 * y + c, 8 * h + 2 * ((y + k) % 4) + c) for h in range(2) for y in range(4) for c in range(2)]

    def edges(lo, hi):
        return lax.ppermute(hi, "sub", up), lax.ppermute(lo, "sub", down)

    piece = courant_squared[:, 0]
    other = lax.ppermute(piece, "shot", across)
    piece_c = lax.ppermute(piece, "shot", chip)
    other_c = lax.ppermute(other, "shot", chip)
    blocks = call(select_kernel, [SMEM] * 2 + [VMEM] * 4, [PAIR] * 4, moved=2 << 20)(
        ids, apertures, piece, other, piece_c, other_c
    )
    come = [blocks[0]] + [lax.ppermute(blocks[k], "shot", along(k)) for k in (1, 2, 3)]

    (packed,) = call(
        pack_kernel,
        [ANY] * 4,
        [jax.ShapeDtypeStruct((8, GROUP, TURNED, NZ), F32)],
        [
            pltpu.VMEM((4, GROUP, 256, NZ), F32),
            pltpu.VMEM((2, 8, GROUP, 8, NZ), F32),
            pltpu.SemaphoreType.DMA((38,)),
        ],
        moved=9 << 20,
        out_spec=ANY,
        limit=58,
    )(wave_now[0], wave_prev[0], adj_late[0], adj_later[0])
    turned = lax.all_to_all(packed, "sub", 0, 0, tiled=True).reshape(NX, TURNED, NZ)
    r2, *r2_send = call(assemble_kernel, [SMEM] * 2 + [VMEM] * 4, [FIELD, TILE, TILE], moved=2 << 20)(
        ids, apertures, *come
    )
    r2_halo = edges(*r2_send)

    cell = sources[0]
    line = (cell // NZ) % 256 - NYL * part
    spots = jnp.stack(
        [
            first % 8,
            ((line >= 0) & (line < NYL)).astype(jnp.int32),
            cell // (256 * NZ),
            line,
            cell % NZ,
            (part > 0).astype(jnp.int32),
            (part < 7).astype(jnp.int32),
            ((line >= -8) & (line < NYL + 8)).astype(jnp.int32),
        ]
    )
    amounts = wavelet[0]
    cells = receivers[0]
    lines = (cells // NZ) % 256 - NYL * part

    count, data3, data1, data2, data4 = call(
        receivers_kernel, [SMEM] * 3, [WIDE_FIELD, WIDE_FIELD] + [FIELD] * 3, flops=1 << 40, moved=6 << 20
    )(cells, lines, observed[0])
    r2, count = lax.optimization_barrier((r2, count))

    lap0, u1, lo, hi, u0, u0_edge = call(
        first_kernel,
        [SMEM, SMEM, ANY, VMEM, VMEM],
        [FIELD, FIELD, TILE, TILE, FIELD, TILE],
        [EXT, DEPTH, FIELD_VMEM, pltpu.SemaphoreType.DMA((3,))],
        flops=10 << 20,
        moved=8 << 20,
    )(spots, amounts, turned, r2, oper)
    u1_halo = edges(lo, hi)
    part4, mu5, mu5_edge = call(
        late_kernel,
        [SMEM, ANY] + [VMEM] * 4,
        [FIELD, FIELD, TILE],
        [EXT, DEPTH, FIELD_VMEM, pltpu.SemaphoreType.DMA((3,))],
        flops=10 << 20,
        moved=6 << 20,
    )(spots, turned, r2, *r2_halo, oper)
    lap1, u2 = call(middle_kernel, [VMEM] * 4, [FIELD, FIELD], [EXT, DEPTH], flops=MAIN, moved=6 << 20)(u1, u0, r2, oper)
    u2, part4 = lax.optimization_barrier((u2, part4))
    lap1, u2, lap2, u3, lo, hi = call(
        middle_end_kernel,
        [SMEM, SMEM] + [VMEM] * 10,
        [FIELD] * 4 + [EDGE] * 2,
        [EXT, EXT, DEPTH, TILE_VMEM, TILE_VMEM, STRIP],
        flops=20 << 20,
        moved=12 << 20,
    )(spots, amounts, u1, *u1_halo, u0_edge, r2, *r2_halo, oper, lap1, u2)
    u3_halo = edges(lo, hi)
    lap3, mu4 = call(
        turn_kernel,
        [SMEM, SMEM] + [VMEM] * 7,
        [FIELD, FIELD],
        [EXT, DEPTH, FIELD_VMEM],
        flops=MAIN,
        moved=8 << 20,
    )(spots, amounts, u3, u2, r2, oper, part4, count, data4)
    total, mu4, lo, hi = call(
        turn_end_kernel, [SMEM] + [VMEM] * 6, [FIELD, FIELD, TILE, TILE], [STRIP], flops=1 << 20, moved=4 << 20
    )(spots, *u3_halo, r2, count, lap3, mu4)
    mu4_halo = edges(lo, hi)
    total, mu3 = call(
        back_kernel, [SMEM] + [VMEM] * 9, [FIELD, FIELD], [EXT, DEPTH], flops=MAIN, moved=8 << 20
    )(spots, mu4, mu5, r2, oper, count, data3, u3, lap2, total)
    total, mu3, mu2, lo, hi = call(
        back_end_kernel,
        [SMEM] + [VMEM] * 18,
        [FIELD] * 3 + [EDGE] * 2,
        [EXT, EXT, DEPTH] + [TILE_VMEM] * 4 + [STRIP],
        flops=20 << 20,
        moved=16 << 20,
    )(
        spots, mu4, *mu4_halo, mu5_edge, r2, *r2_halo, oper, count, data3, data2,
        *u3_halo, u2, lap2, lap1, mu3, total,
    )
    mu2_halo = edges(lo, hi)
    (total,) = call(last_kernel, [SMEM] + [VMEM] * 9, [FIELD], [EXT, DEPTH], flops=MAIN, moved=8 << 20)(
        spots, mu2, mu3, r2, oper, count, data1, u1, lap0, total
    )
    *sent, others = call(
        last_end_kernel, [SMEM] * 2 + [VMEM] * 4, [BLOCK] * 4 + [BLOCKS], [STRIP], flops=1 << 20, moved=3 << 20
    )(ids, spots, *mu2_halo, lap0, total)

    own = [sent[0]] + [lax.ppermute(sent[k], "shot", along(k)) for k in (1, 2, 3)]
    others = lax.ppermute(others, "shot", chip)
    recv = own + [others] + [lax.ppermute(others[k], "shot", along(k)) for k in (1, 2, 3)]
    give, keep = (
        call(functools.partial(bins_kernel, side), [SMEM] * 2 + [VMEM] * 8, [PAIR], moved=1 << 20)(ids, apertures, *recv)[0]
        for side in (True, False)
    )
    result = keep + lax.ppermute(give, "shot", across)
    return result[:, None]


def solution(mesh):
    in_specs = (
        P(None, "shot", None, "sub", None),
        P("shot", "sub", None, None),
        P("shot", "sub", None, None),
        P("shot", "sub", None, None),
        P("shot", "sub", None, None),
        P("shot", None),
        P("shot"),
        P("shot", None),
        P("shot", None, None),
        P(),
    )
    out_specs = P(None, "shot", None, "sub", None)
    return jax.shard_map(
        per_device, mesh=mesh, in_specs=in_specs, out_specs=out_specs, check_vma=False
    )
```
